128 devices in a mesh: blk: 4 (over x_hi, core), dp: 32 (over z, x_lo, y).
Axes of the slice: x: 4 (x_hi: 2, x_lo: 2; x = x_hi * 2 + x_lo), y: 4, z: 4, core: 2. Of those that a mesh axis runs over, the one named last changes fastest.
Arguments:
- features: bfloat16 [18432, 1152], P(('blk', 'dp')), may hold values from -24 to 24
- text_emb: bfloat16 [18432, 1152], P(('blk', 'dp')), may hold values from -6 to 6
- proj_w: bfloat16 [1152, 1152], replicated, may hold values from -0.1875 to 0.1875
- log_scale: float32 [1], replicated, may hold values from 1.6 to 2.6
- bias: float32 [1], replicated, may hold values from -6 to -3
Outputs:
- grad_w: float32 [1152, 1152], P(('blk', 'dp'))
The draws below stay inside these ranges and needn't reach their ends.
All inputs are finite; a program needn't handle non-finite values.
Results may differ from the reference program's by a relative error of at most 0.005.
Values may be sent and summed in bfloat16 or wider, within the bound.
No kernel may reach another device: no remote copies, remote signals or barrier semaphores. Data moves between devices by JAX's collectives and lax.ppermute only.
A program may use at most 128 MiB of HBM per device.

```python
import jax
import jax.numpy as jnp
from jax import lax

FEAT = 1152
EMBED = 1152
ROWS_DEV = 144
N_ROWS = 18432


def with_spikes(entries, rng, source, target, parts, factor):
    def block_of(axis_at):
        return (jnp.arange(entries.shape[axis_at]) // (entries.shape[axis_at] // parts)).reshape((-1,) + (1,) * (entries.ndim - 1 - axis_at))

    near = jax.random.permutation(rng, parts)[block_of(target)]
    far = (block_of(target) + parts // 2) % parts
    return jnp.where((block_of(source) == near) | (block_of(source) == far), factor * entries, entries)


def shard_levels(key, shape, shards, least, largest):
    level, own = 1.0, jax.random.fold_in(key, 6)
    for position, shards_of in shards:
        heights = jnp.exp(jax.random.uniform(jax.random.fold_in(own, position), (shards_of,), jnp.float32, least / len(shards), largest / len(shards)))
        level = level * jnp.repeat(heights, shape[position] // shards_of).reshape([-1 if axis == position else 1 for axis in range(len(shape))])
    return level


def centred(stream_key, extent, spread, limit, shards=(), kind=jnp.bfloat16):
    loudness = shard_levels(stream_key, extent, shards, -0.22, 0.18) if shards else 1.0
    values = jax.random.normal(stream_key, extent, jnp.float32) * spread * loudness
    return jnp.minimum(jnp.maximum(values, -limit), limit).astype(kind)


def heavy_noise(stream_key, extent, scale, limit, pieces, heavy, held_as=jnp.bfloat16):
    values = scale * jax.random.normal(stream_key, extent, jnp.float32)
    if pieces:
        values = values * shard_levels(stream_key, extent, pieces, -0.22, 0.18)
    return jnp.clip(with_spikes(values, jax.random.fold_in(stream_key, 3), *heavy), -limit, limit).astype(held_as)


def setup_inputs(seed: int = 0) -> dict:
    arg_keys = jax.random.split(jax.random.key(seed), 6)
    features = heavy_noise(arg_keys[0], (N_ROWS, FEAT), 1.0, 24.0, ((0, 128),), (0, 1, 128, 5.5))
    text_emb = centred(arg_keys[1], (N_ROWS, EMBED), 1.0, 6.0, ((0, 128),))
    proj_w = centred(arg_keys[2], (FEAT, EMBED), FEAT ** -0.5, 0.1875)
    log_scale = jnp.clip(jax.random.uniform(arg_keys[3], (1,), jnp.float32, 1.6, 2.6), 1.6, 2.6)
    bias = jnp.clip(jax.random.uniform(arg_keys[4], (1,), jnp.float32, -6.0, -3.0), -6.0, -3.0)
    return dict(features=features, text_emb=text_emb, proj_w=proj_w, log_scale=log_scale, bias=bias)


epsilon = 1e-06

def reference(features, text_emb, proj_w, log_scale, bias):
    emb = jnp.dot(features, proj_w, preferred_element_type=jnp.float32)
    inverse = lax.rsqrt(lax.optimization_barrier(jnp.sum(emb * emb, axis=1, keepdims=True)) + epsilon)
    unit_f = emb * inverse
    unit = unit_f.astype(jnp.bfloat16)
    text_f = text_emb.astype(jnp.float32)
    text_unit = (text_f * lax.rsqrt(lax.optimization_barrier(jnp.sum(text_f * text_f, axis=1, keepdims=True)) + epsilon)).astype(jnp.bfloat16)
    scale = jnp.exp(log_scale[0])
    shift = bias[0]
    total = features.shape[0]
    blocks = total // ROWS_DEV
    columns = jnp.arange(total, dtype=jnp.int32)

    def block_grad(index):
        rows = lax.dynamic_slice_in_dim(unit, index * ROWS_DEV, ROWS_DEV, 0)
        sim = lax.dot_general(rows, text_unit, (((1,), (1,)), ((), ())), preferred_element_type=jnp.float32)
        ids = index * ROWS_DEV + jnp.arange(ROWS_DEV, dtype=jnp.int32)
        sign = jnp.where(ids[:, None] == columns[None, :], 1.0, -1.0).astype(jnp.float32)
        logit = scale * sim + shift
        weights = (scale * (-sign * jax.nn.sigmoid(-sign * logit))).astype(jnp.bfloat16)
        return jnp.dot(weights, text_unit, preferred_element_type=jnp.float32)
    grad_unit = lax.map(block_grad, jnp.arange(blocks, dtype=jnp.int32)).reshape(total, text_emb.shape[1])
    along = lax.optimization_barrier(jnp.sum(unit_f * grad_unit, axis=1, keepdims=True))
    grad_emb = ((grad_unit - unit_f * along) * inverse).astype(jnp.bfloat16)
    return lax.dot_general(features, grad_emb, (((0,), (0,)), ((), ())), preferred_element_type=jnp.float32)
```

```python
import functools

import jax
import jax.numpy as jnp
from jax import lax
from jax.experimental import pallas as pl
from jax.experimental.pallas import tpu as pltpu
from jax.sharding import Mesh, PartitionSpec as P

epsilon = 1e-06
bf16 = jnp.bfloat16
f32 = jnp.float32

AXES = ("xh", "core", "z", "xl", "y")
SIZES = (2, 2, 4, 2, 4)
ROWS = 144
WIDTH = 1152
HEAD = 80
TAIL = ROWS - HEAD
GROUP = 8 * ROWS
BLOCK = 576
WINDOW = 128
VMEM_LIMIT = 56 << 20


def place(index):
    y, xl, z = index & 3, (index >> 2) & 1, (index >> 3) & 3
    core, xh = (index >> 5) & 1, (index >> 6) & 1
    return 2 * xh + xl, y, z, core


def index_of(x, y, z, core):
    return (x >> 1) * 64 + core * 32 + z * 8 + (x & 1) * 4 + y


def send(value, target):
    pairs = [(source, index_of(*target(*place(source)))) for source in range(128)]
    return lax.ppermute(value, AXES, pairs)


def along_x(steps):
    return lambda x, y, z, core: ((x + steps) % 4, y, z, core)


def along_y(steps):
    return lambda x, y, z, core: (x, (y + steps) % 4, z, core)


def along_z(steps):
    return lambda x, y, z, core: (x, y, (z + steps) % 4, core)


def even_pair(x, y, z, core):
    return (x, y, z ^ 1, core)


def odd_pair(x, y, z, core):
    return (x, y, 3 - z, core)


def other_core(x, y, z, core):
    return (x, y, z, 1 - core)


def normalize_kernel(text, head, tail):
    values = text[...].astype(f32)
    unit = values * lax.rsqrt(jnp.sum(values * values, axis=1, keepdims=True) + epsilon)
    unit = unit.astype(bf16)
    head[...] = unit[:HEAD]
    tail[...] = unit[HEAD:]


def normalized(text):
    return pl.pallas_call(
        normalize_kernel,
        out_shape=[
            jax.ShapeDtypeStruct((HEAD, WIDTH), bf16),
            jax.ShapeDtypeStruct((TAIL, WIDTH), bf16),
        ],
        name="normalize_text",
    )(text)


def pair_kernel(*refs):
    scalars, proj = refs[0], refs[1]
    image_parts, own_parts, other_parts = refs[2:8], refs[8:14], refs[14:20]
    give, keep = refs[20:22]
    feat, w_in, unit, unit_f, inverse, text, sim, weights, grad_emb, grad_w, sems = refs[22:]

    copies = [pltpu.make_async_copy(proj, w_in, sems.at[0])]
    offset = 0
    for slot, part in enumerate(image_parts):
        rows = part.shape[0]
        copies.append(
            pltpu.make_async_copy(part, feat.at[pl.ds(offset, rows)], sems.at[1 + slot])
        )
        offset += rows
    offset = 0
    for slot, part in enumerate(tuple(own_parts) + tuple(other_parts)):
        rows = part.shape[0]
        copies.append(
            pltpu.make_async_copy(part, text.at[pl.ds(offset, rows)], sems.at[7 + slot])
        )
        offset += rows
    for copy in copies:
        copy.start()
    for copy in copies[:7]:
        copy.wait()

    def project(step, carry):
        rows = pl.ds(pl.multiple_of(step * BLOCK, 16), BLOCK)
        emb = jnp.dot(feat[rows, :], w_in[...], preferred_element_type=f32)
        inv = lax.rsqrt(jnp.sum(emb * emb, axis=1, keepdims=True) + epsilon)
        emb = emb * inv
        unit_f[rows, :] = emb
        unit[rows, :] = emb.astype(bf16)
        inverse[rows, :] = jnp.broadcast_to(inv, (BLOCK, 128))
        return carry

    lax.fori_loop(0, GROUP // BLOCK, project, 0)
    for copy in copies[7:]:
        copy.wait()

    half = 0.5 * jnp.exp(scalars[0])
    half_shift = 0.5 * scalars[1]

    def pairs(step, carry):
        rows = pl.ds(pl.multiple_of(step * BLOCK, 16), BLOCK)
        sim[...] = lax.dot_general(
            unit[rows, :], text[...], (((1,), (1,)), ((), ())), preferred_element_type=f32
        )
        weights[...] = (half + half * jnp.tanh(half * sim[...] + half_shift)).astype(bf16)
        columns = pl.ds(pl.multiple_of(step * (GROUP - 512), 128), WINDOW)
        tanh = jnp.tanh(half * sim[:WINDOW, columns] + half_shift)
        row = lax.broadcasted_iota(jnp.int32, (WINDOW, WINDOW), 0)
        column = lax.broadcasted_iota(jnp.int32, (WINDOW, WINDOW), 1)
        lowest = step * 64
        matched = (row == column + lowest) & (row >= lowest) & (row < HEAD + step * 48)
        weights[:WINDOW, columns] = jnp.where(
            matched, half * tanh - half, half + half * tanh
        ).astype(bf16)
        grad = jnp.dot(weights[...], text[...], preferred_element_type=f32)
        image = unit_f[rows, :]
        along = jnp.sum(image * grad, axis=1, keepdims=True)
        grad_emb[rows, :] = ((grad - image * along) * inverse[rows, 0:1]).astype(bf16)
        return carry

    lax.fori_loop(0, GROUP // BLOCK, pairs, 0)

    for first in range(0, WIDTH, 384):
        grad_w[first : first + 384, :] = lax.dot_general(
            feat[:, first : first + 384],
            grad_emb[...],
            (((0,), (0,)), ((), ())),
            preferred_element_type=f32,
        )
    core = lax.axis_index("core")
    for high in range(2):
        theirs = pl.ds(pl.multiple_of(576 * high + 288 * (1 - core), 16), 288)
        mine = pl.ds(pl.multiple_of(576 * high + 288 * core, 16), 288)
        give[pl.ds(288 * high, 288), :] = grad_w[theirs, :].astype(bf16)
        keep[pl.ds(288 * high, 288), :] = grad_w[mine, :]


def pair_terms(scalars, proj_w, images, own_texts, other_texts):
    anywhere = pl.BlockSpec(memory_space=pl.ANY)
    return pl.pallas_call(
        pair_kernel,
        in_specs=[pl.BlockSpec(memory_space=pltpu.SMEM)] + [anywhere] * 19,
        out_specs=[pl.BlockSpec(memory_space=pltpu.VMEM)] * 2,
        out_shape=[
            jax.ShapeDtypeStruct((BLOCK, WIDTH), bf16),
            jax.ShapeDtypeStruct((BLOCK, WIDTH), f32),
        ],
        scratch_shapes=[
            pltpu.VMEM((GROUP, WIDTH), bf16),
            pltpu.VMEM((WIDTH, WIDTH), bf16),
            pltpu.VMEM((GROUP, WIDTH), bf16),
            pltpu.VMEM((GROUP, WIDTH), f32),
            pltpu.VMEM((GROUP, 128), f32),
            pltpu.VMEM((2 * GROUP, WIDTH), bf16),
            pltpu.VMEM((BLOCK, 2 * GROUP), f32),
            pltpu.VMEM((BLOCK, 2 * GROUP), bf16),
            pltpu.VMEM((GROUP, WIDTH), bf16),
            pltpu.VMEM((WIDTH, WIDTH), f32),
            pltpu.SemaphoreType.DMA((19,)),
        ],
        compiler_params=pltpu.CompilerParams(vmem_limit_bytes=VMEM_LIMIT),
        cost_estimate=pl.CostEstimate(
            flops=18_400_000_000, bytes_accessed=20_000_000, transcendentals=2_700_000
        ),
        name="pair_terms",
    )(scalars, proj_w, *images, *own_texts, *other_texts)


def gathered(head, tail, pair, ring):
    head_pair = jnp.concatenate([head, send(head, pair)])
    tail_ring = jnp.concatenate([tail] + [send(tail, ring(steps)) for steps in (1, 3, 2)])
    return (head_pair,) + tuple(send(head_pair, ring(steps)) for steps in (1, 3, 2)) + (
        tail_ring,
        send(tail_ring, pair),
    )


def per_device(features, text_emb, proj_w, log_scale, bias):
    images = gathered(features[:HEAD], features[HEAD:], even_pair, along_x)
    text_head, text_tail = normalized(text_emb)
    own_texts = gathered(text_head, text_tail, odd_pair, along_y)
    other_texts = tuple(send(part, other_core) for part in own_texts)
    scalars = jnp.concatenate([log_scale, bias])
    give, keep = pair_terms(scalars, proj_w, images, own_texts, other_texts)

    total = (keep + send(give, other_core).astype(f32)).reshape(2, 4, 72, WIDTH)
    z = lax.axis_index("z")

    def rows_of(at):
        return lax.dynamic_slice_in_dim(total, at, 1, 1).reshape(ROWS, WIDTH)

    mine = rows_of(z)
    for steps in (1, 3, 2):
        part = rows_of((z + steps) % 4).astype(bf16)
        mine = mine + send(part, along_z(steps)).astype(f32)
    pieces = mine.astype(bf16).reshape(16, 9, WIDTH)
    pieces = lax.all_to_all(pieces, ("xh", "xl", "y"), 0, 0, tiled=True)
    return jnp.sum(pieces.astype(f32), axis=0)


def solution(mesh):
    fine = Mesh(mesh.devices.reshape(SIZES), AXES)
    rows = P(AXES, None)
    return jax.shard_map(
        per_device,
        mesh=fine,
        in_specs=(rows, rows, P(), P(), P()),
        out_specs=rows,
        check_vma=False,
    )
```

```python
import jax
import jax.numpy as jnp
from jax import lax
from jax.experimental import pallas as pl
from jax.experimental.pallas import tpu as pltpu
from jax.sharding import Mesh, PartitionSpec as P

epsilon = 1e-06
bf16 = jnp.bfloat16
f32 = jnp.float32

AXES = ("xh", "core", "zh", "zl", "xl", "y")
SIZES = (2, 2, 2, 2, 2, 4)
TEXT_AXES = ("core", "zl", "y")
CHIP_AXES = ("xh", "zh", "zl", "xl", "y")
ROWS = 144
WIDTH = 1152
IMAGES = 8 * ROWS
TEXTS = 16 * ROWS
BLOCK = IMAGES // 2
FIRST = 512
REST = IMAGES - FIRST
SLAB = 1408
VMEM_LIMIT = 56 << 20


def place(index):
    y, xl, z = index & 3, (index >> 2) & 1, (index >> 3) & 3
    core, xh = (index >> 5) & 1, (index >> 6) & 1
    return 2 * xh + xl, y, z, core


def index_of(x, y, z, core):
    return (x >> 1) * 64 + core * 32 + z * 8 + (x & 1) * 4 + y


def send(value, target):
    pairs = [(source, index_of(*target(*place(source)))) for source in range(128)]
    return lax.ppermute(value, AXES, pairs)


def along_x(steps):
    return lambda x, y, z, core: ((x + steps) % 4, y, z, core)


def odd_pair(x, y, z, core):
    return (x, y, 3 - z, core)


def other_core(x, y, z, core):
    return (x, y, z, 1 - core)


def params():
    return pltpu.CompilerParams(vmem_limit_bytes=VMEM_LIMIT)


def normalize_kernel(text, unit):
    values = text[...].astype(f32)
    inverse = lax.rsqrt(jnp.sum(values * values, axis=1, keepdims=True) + epsilon)
    unit[...] = (values * inverse).astype(bf16)


def normalized(text):
    return pl.pallas_call(
        normalize_kernel,
        out_shape=jax.ShapeDtypeStruct((ROWS, WIDTH), bf16),
        name="normalize_text",
    )(text)


def project_kernel(cuts, *refs):
    parts = refs[: len(cuts)]
    proj, unit, unit_f, inverse, turned, feat, sems = refs[len(cuts) :]
    copies = []
    offset = 0
    for slot, ((start, rows), part) in enumerate(zip(cuts, parts)):
        copies.append(
            pltpu.make_async_copy(
                part.at[pl.ds(start, rows)], feat.at[pl.ds(offset, rows)], sems.at[slot]
            )
        )
        offset += rows
    for copy in copies:
        copy.start()
    for copy in copies:
        copy.wait()
    emb = jnp.dot(feat[...], proj[...], preferred_element_type=f32)
    inv = lax.rsqrt(jnp.sum(emb * emb, axis=1, keepdims=True) + epsilon)
    emb = emb * inv
    unit_f[...] = emb
    unit[...] = emb.astype(bf16)
    inverse[...] = jnp.broadcast_to(inv, inverse.shape)
    for first in range(0, WIDTH, 384):
        row = first + lax.broadcasted_iota(jnp.int32, (384, 1), 0)
        source = jnp.where(row < 1024, row + (row >> 3), 9 * (row - 1024) + 8)
        column = lax.broadcasted_iota(jnp.int32, (384, WIDTH), 1)
        chosen = jnp.where(column == source, 1.0, 0.0).astype(bf16)
        turned[first : first + 384, :] = lax.dot_general(
            chosen, feat[...], (((1,), (1,)), ((), ())), preferred_element_type=f32
        ).astype(bf16)


def projected(parts, cuts, proj_w):
    rows = sum(cut[1] for cut in cuts)
    return pl.pallas_call(
        lambda *refs: project_kernel(cuts, *refs),
        in_specs=[pl.BlockSpec(memory_space=pl.ANY)] * len(parts)
        + [pl.BlockSpec(memory_space=pltpu.VMEM)],
        out_shape=[
            jax.ShapeDtypeStruct((rows, WIDTH), bf16),
            jax.ShapeDtypeStruct((rows, WIDTH), f32),
            jax.ShapeDtypeStruct((rows, 128), f32),
            jax.ShapeDtypeStruct((WIDTH, rows), bf16),
        ],
        scratch_shapes=[pltpu.VMEM((rows, WIDTH), bf16), pltpu.SemaphoreType.DMA((len(parts),))],
        compiler_params=params(),
        cost_estimate=pl.CostEstimate(
            flops=6 * rows * WIDTH * WIDTH, bytes_accessed=16 * rows * WIDTH, transcendentals=rows
        ),
        name="project_images",
    )(*parts, proj_w)


def pair_kernel(scalars, place_of_own, texts, *refs):
    units, units_f, inverses, turns = (refs[2 * slot : 2 * slot + 2] for slot in range(4))
    give, keep = refs[8:10]
    unit, unit_f, inverse, turned, text, sim, weights, grad_emb, sems = refs[10:]

    first, last = pl.ds(0, FIRST), pl.ds(FIRST, REST)
    copies = []
    for pair, target in ((units, unit), (units_f, unit_f), (inverses, inverse)):
        copies.append((pair[0], target.at[first]))
        copies.append((pair[1], target.at[last]))
    copies.append((turns[0], turned.at[:, first]))
    copies.append((turns[1], turned.at[:, last]))
    own = place_of_own[0]
    for slot in range(16):
        source = pl.ds(pl.multiple_of(((own + slot) & 15) * ROWS, 16), ROWS)
        copies.append((texts.at[source], text.at[pl.ds(slot * ROWS, ROWS)]))
    copies = [
        pltpu.make_async_copy(source, target, sems.at[slot])
        for slot, (source, target) in enumerate(copies)
    ]
    early, later, late = copies[:2] + copies[8:16], copies[16:], copies[2:8]
    for copy in early + later + late:
        copy.start()
    for copy in early:
        copy.wait()

    half = 0.5 * jnp.exp(scalars[0])
    half_shift = 0.5 * scalars[1]

    def pairs(step, carry):
        rows = pl.ds(pl.multiple_of(step * BLOCK, 16), BLOCK)

        def similar(start):
            sim[:, start : start + IMAGES] = lax.dot_general(
                unit[rows, :],
                text[start : start + IMAGES, :],
                (((1,), (1,)), ((), ())),
                preferred_element_type=f32,
            )

        similar(0)

        @pl.when(step == 0)
        def _():
            for copy in later:
                copy.wait()

        similar(IMAGES)
        weights[...] = (half + half * jnp.tanh(half * sim[...] + half_shift)).astype(bf16)

        @pl.when(step == 0)
        def _():
            tanh = jnp.tanh(half * sim[:ROWS, :256] + half_shift)
            row = lax.broadcasted_iota(jnp.int32, (ROWS, 256), 0)
            column = lax.broadcasted_iota(jnp.int32, (ROWS, 256), 1)
            matched = jnp.where(row == column, half * tanh - half, half + half * tanh)
            weights[:ROWS, :256] = matched.astype(bf16)
            for copy in late:
                copy.wait()

        grad = jnp.dot(weights[...], text[...], preferred_element_type=f32)
        image = unit_f[rows, :]
        along = jnp.sum(image * grad, axis=1, keepdims=True)
        grad_emb[rows, :] = ((grad - image * along) * inverse[rows, 0:1]).astype(bf16)
        return carry

    lax.fori_loop(0, IMAGES // BLOCK, pairs, 0)

    core = lax.axis_index("core")

    def terms(start, rows):
        return jnp.dot(
            turned[pl.ds(pl.multiple_of(start, 16), rows), :],
            grad_emb[...],
            preferred_element_type=f32,
        )

    for high in range(2):
        eights, ones = pl.ds(256 * high, 256), pl.ds(512 + 32 * high, 32)
        give[eights, :] = terms(512 * high + 256 * (1 - core), 256).astype(bf16)
        give[ones, :] = terms(1024 + 64 * high + 32 * (1 - core), 32).astype(bf16)
        keep[eights, :] = terms(512 * high + 256 * core, 256)
        keep[ones, :] = terms(1024 + 64 * high + 32 * core, 32)


def pair_terms(scalars, place_of_own, texts, first, rest):
    anywhere = pl.BlockSpec(memory_space=pl.ANY)
    smem = pl.BlockSpec(memory_space=pltpu.SMEM)
    return pl.pallas_call(
        pair_kernel,
        in_specs=[smem, smem] + [anywhere] * 9,
        out_specs=[pl.BlockSpec(memory_space=pltpu.VMEM)] * 2,
        out_shape=[
            jax.ShapeDtypeStruct((BLOCK, WIDTH), bf16),
            jax.ShapeDtypeStruct((BLOCK, WIDTH), f32),
        ],
        scratch_shapes=[
            pltpu.VMEM((IMAGES, WIDTH), bf16),
            pltpu.VMEM((IMAGES, WIDTH), f32),
            pltpu.VMEM((IMAGES, 128), f32),
            pltpu.VMEM((WIDTH, IMAGES), bf16),
            pltpu.VMEM((TEXTS, WIDTH), bf16),
            pltpu.VMEM((BLOCK, TEXTS), f32),
            pltpu.VMEM((BLOCK, TEXTS), bf16),
            pltpu.VMEM((IMAGES, WIDTH), bf16),
            pltpu.SemaphoreType.DMA((24,)),
        ],
        compiler_params=params(),
        cost_estimate=pl.CostEstimate(
            flops=15_400_000_000, bytes_accessed=20_000_000, transcendentals=2_700_000
        ),
        name="pair_terms",
    )(scalars, place_of_own, texts, *(part for pair in zip(first, rest) for part in pair))


def chip_sum_kernel(kept, given, out, ninth):
    out[:, :WIDTH] = (kept[:512, :] + given[:512, :].astype(f32)).astype(bf16)
    ninth[...] = jnp.zeros(ninth.shape, f32)
    rows = kept[512:, :] + given[512:, :].astype(f32)
    for tile in range(9):
        sublanes = pl.ds(tile % 8, 64, stride=8)
        ninth[tile // 8, sublanes, :] = rows[:, 128 * tile : 128 * tile + 128]
    out[:, WIDTH : WIDTH + 128] = ninth[0].astype(bf16)
    out[:, WIDTH + 128 :] = ninth[1].astype(bf16)


def chip_sum(kept, given):
    return pl.pallas_call(
        chip_sum_kernel,
        out_shape=jax.ShapeDtypeStruct((512, SLAB), bf16),
        scratch_shapes=[pltpu.VMEM((2, 512, 128), f32)],
        compiler_params=params(),
        name="chip_sum",
    )(kept, given)


def last_sum_kernel(pieces, out):
    def add(step, total):
        rows = pl.ds(pl.multiple_of(step * 16, 16), 16)
        return total + pieces[rows, :].astype(f32)

    total = lax.fori_loop(0, 32, add, jnp.zeros((16, SLAB), f32))
    total = total[:8] + total[8:]
    out[:8, :] = total[:, :WIDTH]
    for tile in range(9):
        sublane, lane = tile % 8, WIDTH + 128 * (tile // 8)
        out[8:9, 128 * tile : 128 * tile + 128] = total[sublane : sublane + 1, lane : lane + 128]


def last_sum(pieces):
    return pl.pallas_call(
        last_sum_kernel,
        out_shape=jax.ShapeDtypeStruct((9, WIDTH), f32),
        compiler_params=params(),
        name="last_sum",
    )(pieces)


def per_device(features, text_emb, proj_w, log_scale, bias):
    texts = lax.all_gather(normalized(text_emb), TEXT_AXES, axis=0, tiled=True)
    near = jnp.concatenate([features, send(features, odd_pair)])
    ring = [send(near, along_x(steps)) for steps in (1, 3, 2)]
    first = projected((near, ring[0]), ((0, 288), (0, 224)), proj_w)
    rest = projected(ring, ((224, 64), (0, 288), (0, 288)), proj_w)
    scalars = jnp.concatenate([log_scale, bias])
    place_of_own = jnp.reshape(lax.axis_index(TEXT_AXES), (1,)).astype(jnp.int32)
    give, keep = pair_terms(scalars, place_of_own, texts, first, rest)
    pieces = chip_sum(keep, send(give, other_core))
    return last_sum(lax.all_to_all(pieces, CHIP_AXES, 0, 0, tiled=True))


def solution(mesh):
    fine = Mesh(mesh.devices.reshape(SIZES), AXES)
    rows = P(AXES, None)
    return jax.shard_map(
        per_device,
        mesh=fine,
        in_specs=(rows, rows, P(), P(), P()),
        out_specs=rows,
        check_vma=False,
    )
```

```python
import jax
import jax.numpy as jnp
from jax import lax
from jax.experimental import pallas as pl
from jax.experimental.pallas import tpu as pltpu
from jax.sharding import Mesh, PartitionSpec as P

epsilon = 1e-06
bf16 = jnp.bfloat16
f32 = jnp.float32

AXES = ("xh", "core", "z", "xl", "y")
SIZES = (2, 2, 4, 2, 4)
ROWS = 144
WIDTH = 1152
HEAD = 64
TAIL = ROWS - HEAD
HEADS, TAILS = 4 * HEAD, 4 * TAIL
HALF = 4 * ROWS
IMAGES = 2 * HALF
TURNED = 512
SLAB = 1408
VMEM_LIMIT = 40 << 20


def place(index):
    y, xl, z = index & 3, (index >> 2) & 1, (index >> 3) & 3
    core, xh = (index >> 5) & 1, (index >> 6) & 1
    return 2 * xh + xl, y, z, core


def index_of(x, y, z, core):
    return (x >> 1) * 64 + core * 32 + z * 8 + (x & 1) * 4 + y


def send(value, target):
    pairs = [(source, index_of(*target(*place(source)))) for source in range(128)]
    return lax.ppermute(value, AXES, pairs)


def along_x(steps):
    return lambda x, y, z, core: ((x + steps) % 4, y, z, core)


def along_y(steps):
    return lambda x, y, z, core: (x, (y + steps) % 4, z, core)


def along_z(steps):
    return lambda x, y, z, core: (x, y, (z + steps) % 4, core)


def onward_y(x, y, z, core):
    return (x, (y + 1 - 2 * core) % 4, z, core)


def onward_z(x, y, z, core):
    return (x, y, (z + 1 - 2 * core) % 4, core)


def other_core(x, y, z, core):
    return (x, y, z, 1 - core)


IN_VMEM = pl.BlockSpec(memory_space=pltpu.VMEM)
IN_SMEM = pl.BlockSpec(memory_space=pltpu.SMEM)


def params():
    return pltpu.CompilerParams(vmem_limit_bytes=VMEM_LIMIT)


def cost(flops, bytes_accessed):
    return pl.CostEstimate(flops=flops, bytes_accessed=bytes_accessed, transcendentals=0)


def begin(pairs, sems, first=0):
    copies = [
        pltpu.make_async_copy(source, target, sems.at[first + slot])
        for slot, (source, target) in enumerate(pairs)
    ]
    for copy in copies:
        copy.start()
    return copies


def finish(copies):
    for copy in copies:
        copy.wait()


def stacked(cuts, refs, target):
    pairs, offset = [], 0
    for which, start, rows in cuts:
        pairs.append((refs[which].at[pl.ds(start, rows)], target.at[pl.ds(offset, rows)]))
        offset += rows
    return pairs


def normalize_kernel(text, head, tail):
    values = text[...].astype(f32)
    inverse = lax.rsqrt(jnp.sum(values * values, axis=1, keepdims=True) + epsilon)
    unit = (values * inverse).astype(bf16)
    head[...] = unit[:HEAD]
    tail[...] = unit[HEAD:]


def normalized(text):
    return pl.pallas_call(
        normalize_kernel,
        out_shape=[
            jax.ShapeDtypeStruct((HEAD, WIDTH), bf16),
            jax.ShapeDtypeStruct((TAIL, WIDTH), bf16),
        ],
        name="normalize_text",
    )(text)


def join_kernel(counts, *refs):
    parts, outs, sems = refs[: sum(counts)], refs[sum(counts) : -1], refs[-1]
    pairs = []
    for count, out in zip(counts, outs):
        cuts = [(slot, 0, parts[slot].shape[0]) for slot in range(count)]
        pairs += stacked(cuts, parts, out)
        parts = parts[count:]
    finish(begin(pairs, sems))


def joined(*groups):
    counts = [len(group) for group in groups]
    heights = [sum(part.shape[0] for part in group) for group in groups]
    return pl.pallas_call(
        lambda *refs: join_kernel(counts, *refs),
        in_specs=[IN_VMEM] * sum(counts),
        out_specs=[IN_VMEM] * len(groups),
        out_shape=[jax.ShapeDtypeStruct((rows, WIDTH), bf16) for rows in heights],
        scratch_shapes=[pltpu.SemaphoreType.DMA((sum(counts),))],
        compiler_params=params(),
        name="join",
    )(*(part for group in groups for part in group))


def pick_kernel(heads_1, heads_3, tails_1, tails_3, heads, tails, sems):
    core = lax.axis_index("core")

    @pl.when(core == 0)
    def _():
        finish(begin([(heads_1, heads), (tails_1, tails)], sems))

    @pl.when(core == 1)
    def _():
        finish(begin([(heads_3, heads), (tails_3, tails)], sems))


def picked(*parts):
    return pl.pallas_call(
        pick_kernel,
        in_specs=[IN_VMEM] * 4,
        out_specs=[IN_VMEM] * 2,
        out_shape=[
            jax.ShapeDtypeStruct((HEADS, WIDTH), bf16),
            jax.ShapeDtypeStruct((TAILS, WIDTH), bf16),
        ],
        scratch_shapes=[pltpu.SemaphoreType.DMA((2,))],
        compiler_params=params(),
        name="pick",
    )(*parts)


def project_kernel(cuts, mine, *refs):
    count = len(set(which for which, _, _ in cuts))
    parts = refs[:count]
    proj, unit, unit_f, inverse, turned, feat, sems = refs[count:]
    start = begin(stacked(cuts, parts, feat), sems)
    emb = jnp.dot(parts[mine][...], proj[...], preferred_element_type=f32)
    inv = lax.rsqrt(jnp.sum(emb * emb, axis=1, keepdims=True) + epsilon)
    emb = emb * inv
    unit_f[...] = emb
    unit[...] = emb.astype(bf16)
    inverse[...] = jnp.broadcast_to(inv, inverse.shape)
    finish(start)
    for first in range(0, WIDTH, 384):
        row = first + lax.broadcasted_iota(jnp.int32, (384, 1), 0)
        source = jnp.where(row < 1024, row + (row >> 3), 9 * (row - 1024) + 8)
        column = lax.broadcasted_iota(jnp.int32, (384, WIDTH), 1)
        chosen = jnp.where(column == source, 1.0, 0.0).astype(bf16)
        turned[first : first + 384, :] = lax.dot_general(
            chosen, feat[...], (((1,), (1,)), ((), ())), preferred_element_type=f32
        ).astype(bf16)


def projected(parts, cuts, mine, proj_w):
    rows = sum(cut[2] for cut in cuts)
    return pl.pallas_call(
        lambda *refs: project_kernel(cuts, mine, *refs),
        in_specs=[IN_VMEM] * (len(parts) + 1),
        out_specs=[IN_VMEM] * 4,
        out_shape=[
            jax.ShapeDtypeStruct((HALF, WIDTH), bf16),
            jax.ShapeDtypeStruct((HALF, WIDTH), f32),
            jax.ShapeDtypeStruct((HALF, 128), f32),
            jax.ShapeDtypeStruct((WIDTH, rows), bf16),
        ],
        scratch_shapes=[pltpu.VMEM((rows, WIDTH), bf16), pltpu.SemaphoreType.DMA((len(cuts),))],
        compiler_params=params(),
        cost_estimate=cost(5 * HALF * WIDTH * WIDTH, 20 * HALF * WIDTH),
        name="project_images",
    )(*parts, proj_w)


def wave_body(scalars, units, text, sim, weights, diagonal, take):
    half = 0.5 * jnp.exp(scalars[0])
    half_shift = 0.5 * scalars[1]
    for step, unit in enumerate(units):
        sim[...] = lax.dot_general(
            unit[...], text[...], (((1,), (1,)), ((), ())), preferred_element_type=f32
        )
        weights[...] = (half + half * jnp.tanh(half * sim[...] + half_shift)).astype(bf16)
        if diagonal and step == 0:
            tanh = jnp.tanh(half * sim[:ROWS, :384] + half_shift)
            row = lax.broadcasted_iota(jnp.int32, (ROWS, 384), 0)
            column = lax.broadcasted_iota(jnp.int32, (ROWS, 384), 1)
            same = column == jnp.where(row < HEAD, row, row + HEADS - HEAD)
            pair = jnp.where(same, half * tanh - half, half + half * tanh)
            weights[:ROWS, :384] = pair.astype(bf16)
        take(step, jnp.dot(weights[...], text[...], preferred_element_type=f32))


def first_wave_kernel(cuts, count, scalars, *refs):
    texts, units, totals = refs[:count], refs[count : count + 2], refs[count + 2 : count + 4]
    text, sim, weights, sems = refs[count + 4 :]
    finish(begin(stacked(cuts, texts, text), sems))

    def take(step, product):
        totals[step][...] = product

    wave_body(scalars, units, text, sim, weights, True, take)


def next_wave_kernel(cuts, count, scalars, *refs):
    texts, units = refs[:count], refs[count : count + 2]
    before, totals = refs[count + 2 : count + 4], refs[count + 4 : count + 6]
    text, sim, weights, sems = refs[count + 6 :]
    finish(begin(stacked(cuts, texts, text), sems))

    def take(step, product):
        totals[step][...] = before[step][...] + product

    wave_body(scalars, units, text, sim, weights, False, take)


def last_wave_kernel(cuts, count, scalars, *refs):
    texts, units = refs[:count], refs[count : count + 2]
    before, units_f, inverses, turns, (give, grad_emb) = (
        refs[count + 2 + 2 * slot : count + 4 + 2 * slot] for slot in range(5)
    )
    text, sim, weights, turned, sems = refs[count + 12 :]
    late = begin(turn_copies(turns, turned), sems)
    finish(begin(stacked(cuts, texts, text), sems, len(late)))

    def take(step, product):
        gradient = before[step][...] + product
        image = units_f[step][...]
        along = jnp.sum(image * gradient, axis=1, keepdims=True)
        projection = (gradient - image * along) * inverses[step][:, 0:1]
        grad_emb[HALF * step : HALF * step + HALF, :] = projection.astype(bf16)

    wave_body(scalars, units, text, sim, weights, False, take)
    finish(late)
    write_terms(1 - lax.axis_index("core"), turned, grad_emb, give)


def turn_copies(turns, turned):
    return [
        (turns[0], turned.at[:, pl.ds(0, TURNED)]),
        (turns[1], turned.at[:, pl.ds(TURNED, IMAGES - TURNED)]),
    ]


def write_terms(core, turned, grad_emb, out):
    def terms(start, rows):
        return jnp.dot(
            turned[pl.ds(pl.multiple_of(start, 16), rows), :],
            grad_emb[...],
            preferred_element_type=f32,
        ).astype(out.dtype)

    for high in range(2):
        out[pl.ds(256 * high, 256), :] = terms(512 * high + 256 * core, 256)
        out[pl.ds(512 + 32 * high, 32), :] = terms(1024 + 64 * high + 32 * core, 32)


def wave(kernel, scalars, cuts, texts, units, extra, out_shape, scratch, aliases, name):
    rows = sum(cut[2] for cut in cuts)
    return pl.pallas_call(
        lambda *refs: kernel(cuts, len(texts), *refs),
        in_specs=[IN_SMEM] + [IN_VMEM] * (len(texts) + len(units) + len(extra)),
        out_specs=[IN_VMEM] * 2,
        out_shape=out_shape,
        input_output_aliases=aliases,
        scratch_shapes=[
            pltpu.VMEM((rows, WIDTH), bf16),
            pltpu.VMEM((HALF, rows), f32),
            pltpu.VMEM((HALF, rows), bf16),
        ]
        + scratch
        + [pltpu.SemaphoreType.DMA((8,))],
        compiler_params=params(),
        cost_estimate=cost(6 * IMAGES * WIDTH * rows, 4 * IMAGES * WIDTH),
        name=name,
    )(scalars, *texts, *units, *extra)


def keep_kernel(turn_a, turn_b, grad_emb, keep, turned, sems):
    finish(begin(turn_copies((turn_a, turn_b), turned), sems))
    write_terms(lax.axis_index("core"), turned, grad_emb, keep)


def kept_terms(turns, grad_emb):
    return pl.pallas_call(
        keep_kernel,
        in_specs=[IN_VMEM] * 3,
        out_shape=jax.ShapeDtypeStruct((HALF, WIDTH), f32),
        scratch_shapes=[pltpu.VMEM((WIDTH, IMAGES), bf16), pltpu.SemaphoreType.DMA((2,))],
        compiler_params=params(),
        cost_estimate=cost(2 * HALF * WIDTH * IMAGES, 4 * IMAGES * WIDTH),
        name="kept_terms",
    )(*turns, grad_emb)


def chip_sum_kernel(kept, given, mine, one, three, two, total):
    total[...] = kept[...] + given[...].astype(f32)
    z = lax.axis_index("z")

    def rows_of(at):
        parts = []
        for start, rows in ((0, 64), (256, 64), (512, 8), (544, 8)):
            parts.append(total[pl.ds(pl.multiple_of(start + rows * at, 8), rows), :])
        return parts[0], parts[1], jnp.concatenate(parts[2:])

    for steps, out in ((0, mine), (1, one), (3, three), (2, two)):
        low, high, ninth = rows_of((z + steps) & 3)
        out[:64, :] = low.astype(out.dtype)
        out[64:128, :] = high.astype(out.dtype)
        out[128:, :] = ninth.astype(out.dtype)


def chip_sum(kept, given):
    return pl.pallas_call(
        chip_sum_kernel,
        out_shape=[jax.ShapeDtypeStruct((ROWS, WIDTH), f32)]
        + [jax.ShapeDtypeStruct((ROWS, WIDTH), bf16)] * 3,
        scratch_shapes=[pltpu.VMEM((HALF, WIDTH), f32)],
        compiler_params=params(),
        name="chip_sum",
    )(kept, given)


def ring_sum_kernel(mine, one, three, two, out, ninth):
    def total(rows):
        value = mine[rows, :]
        for part in (one, three, two):
            value = value + part[rows, :].astype(f32)
        return value

    out[:, :WIDTH] = total(pl.ds(0, 128)).astype(bf16)
    ninth[...] = jnp.zeros(ninth.shape, f32)
    last = total(pl.ds(128, 16))
    for tile in range(9):
        sublanes = pl.ds(tile % 8, 16, stride=8)
        ninth[tile // 8, sublanes, :] = last[:, 128 * tile : 128 * tile + 128]
    out[:, WIDTH : WIDTH + 128] = ninth[0].astype(bf16)
    out[:, WIDTH + 128 :] = ninth[1].astype(bf16)


def ring_sum(*parts):
    return pl.pallas_call(
        ring_sum_kernel,
        out_shape=jax.ShapeDtypeStruct((128, SLAB), bf16),
        scratch_shapes=[pltpu.VMEM((2, 128, 128), f32)],
        compiler_params=params(),
        name="ring_sum",
    )(*parts)


def last_sum_kernel(pieces, out):
    total = jnp.zeros((16, SLAB), f32)
    for step in range(8):
        total = total + pieces[16 * step : 16 * step + 16, :].astype(f32)
    total = total[:8] + total[8:]
    out[:8, :] = total[:, :WIDTH]
    for tile in range(9):
        sublane, lane = tile % 8, WIDTH + 128 * (tile // 8)
        out[8:9, 128 * tile : 128 * tile + 128] = total[sublane : sublane + 1, lane : lane + 128]


def last_sum(pieces):
    return pl.pallas_call(
        last_sum_kernel,
        out_shape=jax.ShapeDtypeStruct((9, WIDTH), f32),
        name="last_sum",
    )(pieces)


def ring(value, axis):
    return [send(value, axis(steps)) for steps in (1, 3, 2)]


def per_device(features, text_emb, proj_w, log_scale, bias):
    image_ring = ring(features, along_x)
    head, tail = normalized(text_emb)
    scalars = jnp.concatenate([log_scale, bias])
    heads, tails, images = joined(
        (head, *ring(head, along_y)), (tail, *ring(tail, along_z)), (features, *image_ring)
    )
    heads_1, heads_3 = (send(heads, along_z(steps)) for steps in (1, 3))
    tails_1, tails_3 = (send(tails, along_y(steps)) for steps in (1, 3))
    others = send(images, other_core)
    here = projected((images,), ((0, 0, TURNED),), 0, proj_w)
    there = projected(
        (images, others), ((0, TURNED, HALF - TURNED), (1, 0, HALF)), 1, proj_w
    )
    heads_on, tails_on = picked(heads_1, heads_3, tails_1, tails_3)
    heads_2, tails_2 = send(heads_on, onward_z), send(tails_on, onward_y)

    units, units_f, inverses, turns = zip(here, there)
    sums = [jax.ShapeDtypeStruct((HALF, WIDTH), f32)] * 2
    totals = wave(
        first_wave_kernel,
        scalars,
        ((0, 0, HEADS), (1, 0, 256)),
        (heads, tails),
        units,
        (),
        sums,
        [],
        {},
        "first_wave",
    )
    totals = wave(
        next_wave_kernel,
        scalars,
        ((0, 256, 64), (1, 0, HEADS), (2, 0, HEADS), (3, 0, TAILS), (4, 0, 128)),
        (tails, heads_1, heads_3, tails_1, tails_3),
        units,
        totals,
        sums,
        [],
        {8: 0, 9: 1},
        "second_wave",
    )
    give, grad_emb = wave(
        last_wave_kernel,
        scalars,
        ((0, 128, 192), (1, 0, HEADS), (2, 0, TAILS)),
        (tails_3, heads_2, tails_2),
        units,
        (*totals, *units_f, *inverses, *turns),
        [
            jax.ShapeDtypeStruct((HALF, WIDTH), bf16),
            jax.ShapeDtypeStruct((IMAGES, WIDTH), bf16),
        ],
        [pltpu.VMEM((WIDTH, IMAGES), bf16)],
        {},
        "last_wave",
    )
    given = send(give, other_core)
    keep = kept_terms(turns, grad_emb)
    mine, one, three, two = chip_sum(keep, given)
    parts = [send(part, along_z(steps)) for part, steps in ((one, 1), (three, 3), (two, 2))]
    pieces = ring_sum(mine, *parts)
    return last_sum(lax.all_to_all(pieces, ("xh", "xl", "y"), 0, 0, tiled=True))


def solution(mesh):
    fine = Mesh(mesh.devices.reshape(SIZES), AXES)
    rows = P(AXES, None)
    return jax.shard_map(
        per_device,
        mesh=fine,
        in_specs=(rows, rows, P(), P(), P()),
        out_specs=rows,
        check_vma=False,
    )
```

```python
import jax
import jax.numpy as jnp
from jax import lax
from jax.experimental import pallas as pl
from jax.experimental.pallas import tpu as pltpu
from jax.sharding import Mesh, PartitionSpec as P

epsilon = 1e-06
bf16 = jnp.bfloat16
f32 = jnp.float32

AXES = ("xh", "core", "z", "xl", "y")
SIZES = (2, 2, 4, 2, 4)
ROWS = 144
WIDTH = 1152
HEAD = 64
TAIL = ROWS - HEAD
HEADS, TAILS = 4 * HEAD, 4 * TAIL
HALF = 4 * ROWS
IMAGES = 2 * HALF
TURNED = 512
SLAB = 1408
VMEM_LIMIT = 20 << 20
MARK = jax.ShapeDtypeStruct((8, 128), f32)


def place(index):
    y, xl, z = index & 3, (index >> 2) & 1, (index >> 3) & 3
    core, xh = (index >> 5) & 1, (index >> 6) & 1
    return 2 * xh + xl, y, z, core


def index_of(x, y, z, core):
    return (x >> 1) * 64 + core * 32 + z * 8 + (x & 1) * 4 + y


def send(value, target):
    pairs = [(source, index_of(*target(*place(source)))) for source in range(128)]
    return lax.ppermute(value, AXES, pairs)


def along_x(steps):
    return lambda x, y, z, core: ((x + steps) % 4, y, z, core)


def along_y(steps):
    return lambda x, y, z, core: (x, (y + steps) % 4, z, core)


def along_z(steps):
    return lambda x, y, z, core: (x, y, (z + steps) % 4, core)


def onward_y(x, y, z, core):
    return (x, (y + 1 - 2 * core) % 4, z, core)


def onward_z(x, y, z, core):
    return (x, y, (z + 1 - 2 * core) % 4, core)


def other_core(x, y, z, core):
    return (x, y, z, 1 - core)


IN_VMEM = pl.BlockSpec(memory_space=pltpu.VMEM)
IN_SMEM = pl.BlockSpec(memory_space=pltpu.SMEM)


def params():
    return pltpu.CompilerParams(vmem_limit_bytes=VMEM_LIMIT)


def cost(flops, bytes_accessed):
    return pl.CostEstimate(flops=flops, bytes_accessed=bytes_accessed, transcendentals=0)


def begin(pairs, sems, first=0):
    copies = [
        pltpu.make_async_copy(source, target, sems.at[first + slot])
        for slot, (source, target) in enumerate(pairs)
    ]
    for copy in copies:
        copy.start()
    return copies


def finish(copies):
    for copy in copies:
        copy.wait()


def stack(cuts, refs, target):
    offset = 0
    for which, start, rows in cuts:
        target[offset : offset + rows, :] = refs[which][start : start + rows, :]
        offset += rows


def normalize_kernel(text, head, tail):
    values = text[...].astype(f32)
    inverse = lax.rsqrt(jnp.sum(values * values, axis=1, keepdims=True) + epsilon)
    unit = (values * inverse).astype(bf16)
    head[...] = unit[:HEAD]
    tail[...] = unit[HEAD:]


def normalized(text):
    return pl.pallas_call(
        normalize_kernel,
        out_shape=[
            jax.ShapeDtypeStruct((HEAD, WIDTH), bf16),
            jax.ShapeDtypeStruct((TAIL, WIDTH), bf16),
        ],
        name="normalize_text",
    )(text)


def join_kernel(counts, after, *refs):
    parts, outs, mark = refs[: sum(counts)], refs[sum(counts) + after : -1], refs[-1]
    for count, out in zip(counts, outs):
        stack([(slot, 0, parts[slot].shape[0]) for slot in range(count)], parts, out)
        parts = parts[count:]
    mark[...] = jnp.zeros(mark.shape, f32)


def joined(groups, *after):
    counts = [len(group) for group in groups]
    heights = [sum(part.shape[0] for part in group) for group in groups]
    return pl.pallas_call(
        lambda *refs: join_kernel(counts, len(after), *refs),
        in_specs=[IN_VMEM] * (sum(counts) + len(after)),
        out_specs=[IN_VMEM] * (len(groups) + 1),
        out_shape=[jax.ShapeDtypeStruct((rows, WIDTH), bf16) for rows in heights] + [MARK],
        compiler_params=params(),
        name="join",
    )(*(part for group in groups for part in group), *after)


def pick_kernel(heads_1, heads_3, tails_1, tails_3, after, heads, tails):
    core = lax.axis_index("core")

    @pl.when(core == 0)
    def _():
        heads[...] = heads_1[...]
        tails[...] = tails_1[...]

    @pl.when(core == 1)
    def _():
        heads[...] = heads_3[...]
        tails[...] = tails_3[...]


def picked(*parts):
    return pl.pallas_call(
        pick_kernel,
        in_specs=[IN_VMEM] * 5,
        out_specs=[IN_VMEM] * 2,
        out_shape=[
            jax.ShapeDtypeStruct((HEADS, WIDTH), bf16),
            jax.ShapeDtypeStruct((TAILS, WIDTH), bf16),
        ],
        compiler_params=params(),
        name="pick",
    )(*parts)


def project_kernel(cuts, mine, *refs):
    count = len(set(which for which, _, _ in cuts))
    parts = refs[:count]
    proj, unit, unit_f, inverse, turned, feat = refs[count:]
    stack(cuts, parts, feat)
    emb = jnp.dot(parts[mine][...], proj[...], preferred_element_type=f32)
    inv = lax.rsqrt(jnp.sum(emb * emb, axis=1, keepdims=True) + epsilon)
    emb = emb * inv
    unit_f[...] = emb
    inverse[...] = jnp.broadcast_to(inv, inverse.shape)
    unit[...] = emb.astype(bf16)
    turned[...] = feat[...].T


def projected(parts, cuts, mine, proj_w):
    rows = sum(cut[2] for cut in cuts)
    return pl.pallas_call(
        lambda *refs: project_kernel(cuts, mine, *refs),
        in_specs=[IN_VMEM] * (len(parts) + 1),
        out_specs=[IN_VMEM] * 4,
        out_shape=[
            jax.ShapeDtypeStruct((HALF, WIDTH), bf16),
            jax.ShapeDtypeStruct((HALF, WIDTH), f32),
            jax.ShapeDtypeStruct((HALF, 128), f32),
            jax.ShapeDtypeStruct((WIDTH, rows), bf16),
        ],
        scratch_shapes=[pltpu.VMEM((rows, WIDTH), bf16)],
        compiler_params=params(),
        cost_estimate=cost(1000, 1000),
        name="project_images",
    )(*parts, proj_w)


def wave_body(scalars, units, text, sim, weights, diagonal, take):
    half = 0.5 * jnp.exp(scalars[0])
    half_shift = 0.5 * scalars[1]
    for step, unit in enumerate(units):
        sim[...] = lax.dot_general(
            unit[...], text[...], (((1,), (1,)), ((), ())), preferred_element_type=f32
        )
        weights[...] = (half + half * jnp.tanh(half * sim[...] + half_shift)).astype(bf16)
        if diagonal and step == 0:
            tanh = jnp.tanh(half * sim[:ROWS, :384] + half_shift)
            row = lax.broadcasted_iota(jnp.int32, (ROWS, 384), 0)
            column = lax.broadcasted_iota(jnp.int32, (ROWS, 384), 1)
            same = column == jnp.where(row < HEAD, row, row + HEADS - HEAD)
            pair = jnp.where(same, half * tanh - half, half + half * tanh)
            weights[:ROWS, :384] = pair.astype(bf16)
        take(step, jnp.dot(weights[...], text[...], preferred_element_type=f32))


def first_wave_kernel(cuts, count, scalars, *refs):
    texts, units, totals = refs[:count], refs[count : count + 2], refs[count + 2 : count + 4]
    mark, text, sim, weights, sems = refs[count + 4 :]
    mark[...] = jnp.zeros(mark.shape, f32)
    stack(cuts, texts, text)

    def take(step, product):
        totals[step][...] = product

    wave_body(scalars, units, text, sim, weights, True, take)


def next_wave_kernel(cuts, count, scalars, *refs):
    texts, units = refs[:count], refs[count : count + 2]
    before, totals = refs[count + 2 : count + 4], refs[count + 4 : count + 6]
    text, sim, weights, sems = refs[count + 6 :]
    stack(cuts, texts, text)

    def take(step, product):
        totals[step][...] = before[step][...] + product

    wave_body(scalars, units, text, sim, weights, False, take)


def last_wave_kernel(cuts, count, scalars, *refs):
    texts, units = refs[:count], refs[count : count + 2]
    before, units_f, inverses, turns, (give, grad_emb) = (
        refs[count + 2 + 2 * slot : count + 4 + 2 * slot] for slot in range(5)
    )
    text, sim, weights, turned, sems = refs[count + 12 :]
    late = begin(turn_copies(turns, turned), sems)
    stack(cuts, texts, text)

    def take(step, product):
        gradient = before[step][...] + product
        image = units_f[step][...]
        along = jnp.sum(image * gradient, axis=1, keepdims=True)
        projection = (gradient - image * along) * inverses[step][:, 0:1]
        grad_emb[HALF * step : HALF * step + HALF, :] = projection.astype(bf16)

    wave_body(scalars, units, text, sim, weights, False, take)
    finish(late)
    write_terms(1 - lax.axis_index("core"), turned, grad_emb, give)


def turn_copies(turns, turned):
    return [
        (turns[0], turned.at[:, pl.ds(0, TURNED)]),
        (turns[1], turned.at[:, pl.ds(TURNED, IMAGES - TURNED)]),
    ]


def write_terms(core, turned, grad_emb, out):
    def terms(start, rows):
        return jnp.dot(
            turned[pl.ds(pl.multiple_of(start, 16), rows), :],
            grad_emb[...],
            preferred_element_type=f32,
        ).astype(out.dtype)

    for high in range(2):
        out[pl.ds(288 * high, 288), :] = terms(576 * high + 288 * core, 288)


def wave(kernel, scalars, cuts, texts, units, extra, out_shape, scratch, aliases, name):
    rows = sum(cut[2] for cut in cuts)
    return pl.pallas_call(
        lambda *refs: kernel(cuts, len(texts), *refs),
        in_specs=[IN_SMEM] + [IN_VMEM] * (len(texts) + len(units) + len(extra)),
        out_specs=[IN_VMEM] * len(out_shape),
        out_shape=out_shape,
        input_output_aliases=aliases,
        scratch_shapes=[
            pltpu.VMEM((rows, WIDTH), bf16),
            pltpu.VMEM((HALF, rows), f32),
            pltpu.VMEM((HALF, rows), bf16),
        ]
        + scratch
        + [pltpu.SemaphoreType.DMA((12,))],
        compiler_params=params(),
        cost_estimate=cost(1000, 1000),
        name=name,
    )(scalars, *texts, *units, *extra)


def keep_kernel(turn_a, turn_b, grad_emb, keep, turned, sems):
    finish(begin(turn_copies((turn_a, turn_b), turned), sems))
    write_terms(lax.axis_index("core"), turned, grad_emb, keep)


def kept_terms(turns, grad_emb):
    return pl.pallas_call(
        keep_kernel,
        in_specs=[IN_VMEM] * 3,
        out_shape=jax.ShapeDtypeStruct((HALF, WIDTH), f32),
        scratch_shapes=[pltpu.VMEM((WIDTH, IMAGES), bf16), pltpu.SemaphoreType.DMA((2,))],
        compiler_params=params(),
        cost_estimate=cost(2 * HALF * WIDTH * IMAGES, 4 * IMAGES * WIDTH),
        name="kept_terms",
    )(*turns, grad_emb)


def chip_sum_kernel(kept, given, mine, one, three, two, total):
    total[...] = kept[...] + given[...].astype(f32)
    z = lax.axis_index("z")

    def rows_of(at):
        low, high = (
            total[pl.ds(pl.multiple_of(288 * half + 72 * at, 8), 72), :] for half in range(2)
        )
        return jnp.concatenate([low, high])

    for steps, out in ((0, mine), (1, one), (3, three), (2, two)):
        out[...] = rows_of((z + steps) & 3).astype(out.dtype)


def chip_sum(kept, given):
    return pl.pallas_call(
        chip_sum_kernel,
        out_shape=[jax.ShapeDtypeStruct((ROWS, WIDTH), f32)]
        + [jax.ShapeDtypeStruct((ROWS, WIDTH), bf16)] * 3,
        scratch_shapes=[pltpu.VMEM((HALF, WIDTH), f32)],
        compiler_params=params(),
        name="chip_sum",
    )(kept, given)


def ring_sum_kernel(mine, one, three, two, out, total, eights, ninth):
    ninth[...] = jnp.zeros(ninth.shape, f32)
    for tile in range(9):
        lanes = slice(128 * tile, 128 * tile + 128)
        value = mine[:, lanes]
        for part in (one, three, two):
            value = value + part[:, lanes].astype(f32)
        total[tile, :, :] = value
        for row in range(8):
            eights[tile, pl.ds(row, 16, stride=8), :] = total[tile, pl.ds(row, 16, stride=9), :]
        ninth[tile // 8, pl.ds(tile % 8, 16, stride=8), :] = total[tile, pl.ds(8, 16, stride=9), :]
        out[:, lanes] = eights[tile].astype(bf16)
    out[:, WIDTH : WIDTH + 128] = ninth[0].astype(bf16)
    out[:, WIDTH + 128 :] = ninth[1].astype(bf16)


def ring_sum(*parts):
    return pl.pallas_call(
        ring_sum_kernel,
        out_shape=jax.ShapeDtypeStruct((128, SLAB), bf16),
        scratch_shapes=[
            pltpu.VMEM((9, ROWS, 128), f32),
            pltpu.VMEM((9, 128, 128), f32),
            pltpu.VMEM((2, 128, 128), f32),
        ],
        compiler_params=params(),
        name="ring_sum",
    )(*parts)


def last_sum_kernel(pieces, out):
    total = jnp.zeros((16, SLAB), f32)
    for step in range(8):
        total = total + pieces[16 * step : 16 * step + 16, :].astype(f32)
    total = total[:8] + total[8:]
    out[:8, :] = total[:, :WIDTH]
    for tile in range(9):
        sublane, lane = tile % 8, WIDTH + 128 * (tile // 8)
        out[8:9, 128 * tile : 128 * tile + 128] = total[sublane : sublane + 1, lane : lane + 128]


def last_sum(pieces):
    return pl.pallas_call(
        last_sum_kernel,
        out_shape=jax.ShapeDtypeStruct((9, WIDTH), f32),
        name="last_sum",
    )(pieces)


def ring(value, axis):
    return [send(value, axis(steps)) for steps in (1, 3, 2)]


def per_device(features, text_emb, proj_w, log_scale, bias):
    image_ring = ring(features, along_x)
    head, tail = normalized(text_emb)
    scalars = jnp.concatenate([log_scale, bias])
    heads, tails, mark = joined([(head, *ring(head, along_y)), (tail, *ring(tail, along_z))])
    heads_1, heads_3 = (send(heads, along_z(steps)) for steps in (1, 3))
    tails_1, tails_3 = (send(tails, along_y(steps)) for steps in (1, 3))
    images = joined([(features, *image_ring)], mark)[0]
    others = send(images, other_core)
    here = projected((images,), ((0, 0, TURNED),), 0, proj_w)
    there = projected((images, others), ((0, TURNED, HALF - TURNED), (1, 0, HALF)), 1, proj_w)

    units, units_f, inverses, turns = zip(here, there)
    sums = [jax.ShapeDtypeStruct((HALF, WIDTH), f32)] * 2
    *totals, mark = wave(
        first_wave_kernel,
        scalars,
        ((0, 0, HEADS), (1, 0, 256)),
        (heads, tails),
        units,
        (),
        sums + [MARK],
        [],
        {},
        "first_wave",
    )
    heads_on, tails_on = picked(heads_1, heads_3, tails_1, tails_3, mark)
    heads_2, tails_2 = send(heads_on, onward_z), send(tails_on, onward_y)
    totals = wave(
        next_wave_kernel,
        scalars,
        ((0, 256, 64), (1, 0, HEADS), (2, 0, HEADS), (3, 0, TAILS), (4, 0, 128)),
        (tails, heads_1, heads_3, tails_1, tails_3),
        units,
        totals,
        sums,
        [],
        {8: 0, 9: 1},
        "second_wave",
    )
    give, grad_emb = wave(
        last_wave_kernel,
        scalars,
        ((0, 128, 192), (1, 0, HEADS), (2, 0, TAILS)),
        (tails_3, heads_2, tails_2),
        units,
        (*totals, *units_f, *inverses, *turns),
        [
            jax.ShapeDtypeStruct((HALF, WIDTH), bf16),
            jax.ShapeDtypeStruct((IMAGES, WIDTH), bf16),
        ],
        [pltpu.VMEM((WIDTH, IMAGES), bf16)],
        {},
        "last_wave",
    )
    given = send(give, other_core)
    keep = kept_terms(turns, grad_emb)
    mine, one, three, two = chip_sum(keep, given)
    parts = [send(part, along_z(steps)) for part, steps in ((one, 1), (three, 3), (two, 2))]
    pieces = ring_sum(mine, *parts)
    return last_sum(lax.all_to_all(pieces, ("xh", "xl", "y"), 0, 0, tiled=True))


def solution(mesh):
    fine = Mesh(mesh.devices.reshape(SIZES), AXES)
    rows = P(AXES, None)
    return jax.shard_map(
        per_device,
        mesh=fine,
        in_specs=(rows, rows, P(), P(), P()),
        out_specs=rows,
        check_vma=False,
    )
```

```python
import jax
import jax.numpy as jnp
from jax import lax
from jax.experimental import pallas as pl
from jax.experimental.pallas import tpu as pltpu
from jax.sharding import Mesh, PartitionSpec as P

epsilon = 1e-06
bf16 = jnp.bfloat16
f32 = jnp.float32

AXIS = "d"
ROWS = 144
WIDTH = 1152
HALF = 4 * ROWS
IMAGES = 2 * HALF
TURNED = 512
SLAB = 1408
VMEM_LIMIT = 20 << 20
MARK = jax.ShapeDtypeStruct((8, 128), f32)


def place(index):
    y, xl, z = index & 3, (index >> 2) & 1, (index >> 3) & 3
    core, xh = (index >> 5) & 1, (index >> 6) & 1
    return 2 * xh + xl, y, z, core


def index_of(x, y, z, core):
    return (x >> 1) * 64 + core * 32 + z * 8 + (x & 1) * 4 + y


def send(value, target):
    pairs = [(source, index_of(*target(*place(source)))) for source in range(128)]
    return lax.ppermute(value, AXIS, pairs)


def along_x(steps):
    return lambda x, y, z, core: ((x + steps) % 4, y, z, core)


def along_y_or_z(steps):
    return lambda x, y, z, core: (
        (x, y, (z + steps) % 4, core) if core else (x, (y + steps) % 4, z, core)
    )


def along_z_or_y(steps):
    return lambda x, y, z, core: (
        (x, (y + steps) % 4, z, core) if core else (x, y, (z + steps) % 4, core)
    )


def other_core(x, y, z, core):
    return (x, y, z, 1 - core)


LAST_GROUPS = [
    [index_of(2 * xh + xl, y, z, 0) for xh in range(2) for xl in range(2) for y in range(4)]
    for z in range(4)
] + [
    [index_of(2 * xh + xl, y, z, 1) for xh in range(2) for z in range(4) for xl in range(2)]
    for y in range(4)
]


def my_core():
    return (lax.axis_index(AXIS) >> 5) & 1


IN_VMEM = pl.BlockSpec(memory_space=pltpu.VMEM)
IN_SMEM = pl.BlockSpec(memory_space=pltpu.SMEM)


def params():
    return pltpu.CompilerParams(vmem_limit_bytes=VMEM_LIMIT)


def cost(flops, bytes_accessed):
    return pl.CostEstimate(flops=flops, bytes_accessed=bytes_accessed, transcendentals=0)


def begin(pairs, sems, first=0):
    copies = [
        pltpu.make_async_copy(source, target, sems.at[first + slot])
        for slot, (source, target) in enumerate(pairs)
    ]
    for copy in copies:
        copy.start()
    return copies


def finish(copies):
    for copy in copies:
        copy.wait()


def stack(cuts, refs, target):
    offset = 0
    for which, start, rows in cuts:
        target[offset : offset + rows, :] = refs[which][start : start + rows, :]
        offset += rows


def normalize_kernel(text, features, unit, held):
    values = text[...].astype(f32)
    inverse = lax.rsqrt(jnp.sum(values * values, axis=1, keepdims=True) + epsilon)
    unit[...] = (values * inverse).astype(bf16)
    held[...] = features[...]


def normalized(text, features):
    return pl.pallas_call(
        normalize_kernel,
        in_specs=[IN_VMEM] * 2,
        out_specs=[IN_VMEM] * 2,
        out_shape=[jax.ShapeDtypeStruct((ROWS, WIDTH), bf16)] * 2,
        name="normalize_text",
    )(text, features)


def join_kernel(counts, after, *refs):
    parts, outs, mark = refs[: sum(counts)], refs[sum(counts) + after : -1], refs[-1]
    for count, out in zip(counts, outs):
        stack([(slot, 0, parts[slot].shape[0]) for slot in range(count)], parts, out)
        parts = parts[count:]
    mark[...] = jnp.zeros(mark.shape, f32)


def joined(groups, *after):
    counts = [len(group) for group in groups]
    heights = [sum(part.shape[0] for part in group) for group in groups]
    return pl.pallas_call(
        lambda *refs: join_kernel(counts, len(after), *refs),
        in_specs=[IN_VMEM] * (sum(counts) + len(after)),
        out_specs=[IN_VMEM] * (len(groups) + 1),
        out_shape=[jax.ShapeDtypeStruct((rows, WIDTH), bf16) for rows in heights] + [MARK],
        compiler_params=params(),
        name="join",
    )(*(part for group in groups for part in group), *after)


def halves_kernel(before, behind, after, low, high):
    low[...] = before[: HALF // 2, :]
    high[...] = behind[HALF // 2 :, :]


def halves(*parts):
    return pl.pallas_call(
        halves_kernel,
        in_specs=[IN_VMEM] * 3,
        out_specs=[IN_VMEM] * 2,
        out_shape=[jax.ShapeDtypeStruct((HALF // 2, WIDTH), bf16)] * 2,
        compiler_params=params(),
        name="halves",
    )(*parts)


def project_kernel(cuts, mine, *refs):
    count = len(set(which for which, _, _ in cuts))
    parts = refs[:count]
    proj, unit, unit_f, inverse, turned, feat = refs[count:]
    stack(cuts, parts, feat)
    emb = jnp.dot(parts[mine][...], proj[...], preferred_element_type=f32)
    inv = lax.rsqrt(jnp.sum(emb * emb, axis=1, keepdims=True) + epsilon)
    emb = emb * inv
    unit_f[...] = emb
    inverse[...] = jnp.broadcast_to(inv, inverse.shape)
    unit[...] = emb.astype(bf16)
    turned[...] = feat[...].T


def projected(parts, cuts, mine, proj_w):
    rows = sum(cut[2] for cut in cuts)
    return pl.pallas_call(
        lambda *refs: project_kernel(cuts, mine, *refs),
        in_specs=[IN_VMEM] * (len(parts) + 1),
        out_specs=[IN_VMEM] * 4,
        out_shape=[
            jax.ShapeDtypeStruct((HALF, WIDTH), bf16),
            jax.ShapeDtypeStruct((HALF, WIDTH), f32),
            jax.ShapeDtypeStruct((HALF, 128), f32),
            jax.ShapeDtypeStruct((WIDTH, rows), bf16),
        ],
        scratch_shapes=[pltpu.VMEM((rows, WIDTH), bf16)],
        compiler_params=params(),
        cost_estimate=cost(1000, 1000),
        name="project_images",
    )(*parts, proj_w)


def wave_body(scalars, units, text, sim, weights, diagonal, take):
    half = 0.5 * jnp.exp(scalars[0])
    half_shift = 0.5 * scalars[1]
    for step, unit in enumerate(units):
        sim[...] = lax.dot_general(
            unit[...], text[...], (((1,), (1,)), ((), ())), preferred_element_type=f32
        )
        weights[...] = (half + half * jnp.tanh(half * sim[...] + half_shift)).astype(bf16)
        if diagonal and step == 0:
            tanh = jnp.tanh(half * sim[:ROWS, :256] + half_shift)
            row = lax.broadcasted_iota(jnp.int32, (ROWS, 256), 0)
            column = lax.broadcasted_iota(jnp.int32, (ROWS, 256), 1)
            pair = jnp.where(row == column, half * tanh - half, half + half * tanh)
            weights[:ROWS, :256] = pair.astype(bf16)
        take(step, jnp.dot(weights[...], text[...], preferred_element_type=f32))


def first_wave_kernel(cuts, count, scalars, *refs):
    texts, units, totals = refs[:count], refs[count : count + 2], refs[count + 2 : count + 4]
    mark, text, sim, weights, sems = refs[count + 4 :]
    mark[...] = jnp.zeros(mark.shape, f32)
    stack(cuts, texts, text)

    def take(step, product):
        totals[step][...] = product

    wave_body(scalars, units, text, sim, weights, True, take)


def next_wave_kernel(cuts, count, scalars, *refs):
    texts, units = refs[:count], refs[count : count + 2]
    before, totals = refs[count + 2 : count + 4], refs[count + 4 : count + 6]
    text, sim, weights, sems = refs[count + 6 :]
    stack(cuts, texts, text)

    def take(step, product):
        totals[step][...] = before[step][...] + product

    wave_body(scalars, units, text, sim, weights, False, take)


def last_wave_kernel(cuts, count, scalars, *refs):
    texts, units = refs[:count], refs[count : count + 2]
    before, units_f, inverses, turns, (give, grad_emb) = (
        refs[count + 2 + 2 * slot : count + 4 + 2 * slot] for slot in range(5)
    )
    text, sim, weights, turned, sems = refs[count + 12 :]
    late = begin(turn_copies(turns, turned), sems)
    stack(cuts, texts, text)

    def take(step, product):
        gradient = before[step][...] + product
        image = units_f[step][...]
        along = jnp.sum(image * gradient, axis=1, keepdims=True)
        projection = (gradient - image * along) * inverses[step][:, 0:1]
        grad_emb[HALF * step : HALF * step + HALF, :] = projection.astype(bf16)

    wave_body(scalars, units, text, sim, weights, False, take)
    finish(late)
    write_terms(1 - my_core(), turned, grad_emb, give)


def turn_copies(turns, turned):
    return [
        (turns[0], turned.at[:, pl.ds(0, TURNED)]),
        (turns[1], turned.at[:, pl.ds(TURNED, IMAGES - TURNED)]),
    ]


def write_terms(core, turned, grad_emb, out):
    def terms(start, rows):
        return jnp.dot(
            turned[pl.ds(pl.multiple_of(start, 16), rows), :],
            grad_emb[...],
            preferred_element_type=f32,
        ).astype(out.dtype)

    for high in range(2):
        out[pl.ds(288 * high, 288), :] = terms(576 * high + 288 * core, 288)


def wave(kernel, scalars, cuts, texts, units, extra, out_shape, scratch, aliases, name):
    rows = sum(cut[2] for cut in cuts)
    return pl.pallas_call(
        lambda *refs: kernel(cuts, len(texts), *refs),
        in_specs=[IN_SMEM] + [IN_VMEM] * (len(texts) + len(units) + len(extra)),
        out_specs=[IN_VMEM] * len(out_shape),
        out_shape=out_shape,
        input_output_aliases=aliases,
        scratch_shapes=[
            pltpu.VMEM((rows, WIDTH), bf16),
            pltpu.VMEM((HALF, rows), f32),
            pltpu.VMEM((HALF, rows), bf16),
        ]
        + scratch
        + [pltpu.SemaphoreType.DMA((12,))],
        compiler_params=params(),
        cost_estimate=cost(1000, 1000),
        name=name,
    )(scalars, *texts, *units, *extra)


def keep_kernel(turn_a, turn_b, grad_emb, keep, turned, sems):
    finish(begin(turn_copies((turn_a, turn_b), turned), sems))
    write_terms(my_core(), turned, grad_emb, keep)


def kept_terms(turns, grad_emb):
    return pl.pallas_call(
        keep_kernel,
        in_specs=[IN_VMEM] * 3,
        out_shape=jax.ShapeDtypeStruct((HALF, WIDTH), f32),
        scratch_shapes=[pltpu.VMEM((WIDTH, IMAGES), bf16), pltpu.SemaphoreType.DMA((2,))],
        compiler_params=params(),
        cost_estimate=cost(2 * HALF * WIDTH * IMAGES, 4 * IMAGES * WIDTH),
        name="kept_terms",
    )(*turns, grad_emb)


def chip_sum_kernel(kept, given, mine, one, three, two, total):
    for tile in range(9):
        lanes = slice(128 * tile, 128 * tile + 128)
        total[tile, :, :] = kept[:, lanes] + given[:, lanes].astype(f32)
    index = lax.axis_index(AXIS)
    outs = ((0, mine), (1, one), (3, three), (2, two))

    @pl.when(my_core() == 0)
    def _():
        for steps, out in outs:
            first = 72 * (((index >> 3) + steps) & 3)
            for tile in range(9):
                for row in range(9):
                    parts = [
                        total[tile, pl.ds(288 * high + first + row, 8, stride=9), :]
                        for high in range(2)
                    ]
                    out[16 * row : 16 * row + 16, 128 * tile : 128 * tile + 128] = (
                        jnp.concatenate(parts).astype(out.dtype)
                    )

    @pl.when(my_core() == 1)
    def _():
        for steps, out in outs:
            first = 9 * ((index + steps) & 3)
            for tile in range(9):
                for row in range(9):
                    part = total[tile, pl.ds(first + row, 16, stride=36), :]
                    out[16 * row : 16 * row + 16, 128 * tile : 128 * tile + 128] = part.astype(
                        out.dtype
                    )


def chip_sum(kept, given):
    return pl.pallas_call(
        chip_sum_kernel,
        out_shape=[jax.ShapeDtypeStruct((ROWS, WIDTH), f32)]
        + [jax.ShapeDtypeStruct((ROWS, WIDTH), bf16)] * 3,
        scratch_shapes=[pltpu.VMEM((9, HALF, 128), f32)],
        compiler_params=params(),
        name="chip_sum",
    )(kept, given)


def ring_sum_kernel(mine, one, three, two, out, eights, ninth):
    ninth[...] = jnp.zeros(ninth.shape, f32)
    for tile in range(9):
        lanes = slice(128 * tile, 128 * tile + 128)
        value = mine[:, lanes]
        for part in (one, three, two):
            value = value + part[:, lanes].astype(f32)
        for row in range(8):
            eights[tile, pl.ds(row, 16, stride=8), :] = value[16 * row : 16 * row + 16]
        ninth[tile // 8, pl.ds(tile % 8, 16, stride=8), :] = value[128:]
        out[:, lanes] = eights[tile].astype(bf16)
    out[:, WIDTH : WIDTH + 128] = ninth[0].astype(bf16)
    out[:, WIDTH + 128 :] = ninth[1].astype(bf16)


def ring_sum(*parts):
    return pl.pallas_call(
        ring_sum_kernel,
        out_shape=jax.ShapeDtypeStruct((128, SLAB), bf16),
        scratch_shapes=[pltpu.VMEM((9, 128, 128), f32), pltpu.VMEM((2, 128, 128), f32)],
        compiler_params=params(),
        name="ring_sum",
    )(*parts)


def last_sum_kernel(pieces, out):
    total = jnp.zeros((16, SLAB), f32)
    for step in range(8):
        total = total + pieces[16 * step : 16 * step + 16, :].astype(f32)
    total = total[:8] + total[8:]
    out[:8, :] = total[:, :WIDTH]
    for tile in range(9):
        sublane, lane = tile % 8, WIDTH + 128 * (tile // 8)
        out[8:9, 128 * tile : 128 * tile + 128] = total[sublane : sublane + 1, lane : lane + 128]


def last_sum(pieces):
    return pl.pallas_call(
        last_sum_kernel,
        out_shape=jax.ShapeDtypeStruct((9, WIDTH), f32),
        name="last_sum",
    )(pieces)


def ring(value, axis):
    return [send(value, axis(steps)) for steps in (1, 3, 2)]


def per_device(features, text_emb, proj_w, log_scale, bias):
    unit_text, held = normalized(text_emb, features)
    scalars = jnp.concatenate([log_scale, bias])
    line, mark = joined([(unit_text, *ring(unit_text, along_y_or_z))])
    line_1, line_3 = (send(line, along_z_or_y(steps)) for steps in (1, 3))
    images = joined([(held, *ring(features, along_x))], mark)[0]
    others = send(images, other_core)
    here = projected((images,), ((0, 0, TURNED),), 0, proj_w)
    there = projected((images, others), ((0, TURNED, HALF - TURNED), (1, 0, HALF)), 1, proj_w)

    units, units_f, inverses, turns = zip(here, there)
    sums = [jax.ShapeDtypeStruct((HALF, WIDTH), f32)] * 2
    *totals, mark = wave(
        first_wave_kernel,
        scalars,
        ((0, 0, 512),),
        (line,),
        units,
        (),
        sums + [MARK],
        [],
        {},
        "first_wave",
    )
    low, high = halves(line_1, line_3, mark)
    low, high = send(low, along_z_or_y(1)), send(high, along_z_or_y(3))
    totals = wave(
        next_wave_kernel,
        scalars,
        ((0, 512, 64), (1, 0, HALF), (2, 0, 384)),
        (line, line_1, line_3),
        units,
        totals,
        sums,
        [],
        {6: 0, 7: 1},
        "second_wave",
    )
    give, grad_emb = wave(
        last_wave_kernel,
        scalars,
        ((0, 384, 192), (1, 0, HALF // 2), (2, 0, HALF // 2)),
        (line_3, low, high),
        units,
        (*totals, *units_f, *inverses, *turns),
        [
            jax.ShapeDtypeStruct((HALF, WIDTH), bf16),
            jax.ShapeDtypeStruct((IMAGES, WIDTH), bf16),
        ],
        [pltpu.VMEM((WIDTH, IMAGES), bf16)],
        {},
        "last_wave",
    )
    given = send(give, other_core)
    keep = kept_terms(turns, grad_emb)
    mine, one, three, two = chip_sum(keep, given)
    parts = [send(part, along_z_or_y(steps)) for part, steps in ((one, 1), (three, 3), (two, 2))]
    pieces = ring_sum(mine, *parts)
    pieces = lax.all_to_all(pieces, AXIS, 0, 0, axis_index_groups=LAST_GROUPS, tiled=True)
    return last_sum(pieces)


def solution(mesh):
    flat = Mesh(mesh.devices.reshape(-1), (AXIS,))
    rows = P(AXIS, None)
    return jax.shard_map(
        per_device,
        mesh=flat,
        in_specs=(rows, rows, P(), P(), P()),
        out_specs=rows,
        check_vma=False,
    )
```

```python
import jax
import jax.numpy as jnp
from jax import lax
from jax.experimental import pallas as pl
from jax.experimental.pallas import tpu as pltpu
from jax.sharding import Mesh, PartitionSpec as P

epsilon = 1e-06
bf16 = jnp.bfloat16
f32 = jnp.float32

AXIS = "d"
ROWS = 144
WIDTH = 1152
HALF = 4 * ROWS
IMAGES = 2 * HALF
TURNED = 512
SLAB = 1408
VMEM_LIMIT = 20 << 20
WORK = 12_000_000_000
MARK = jax.ShapeDtypeStruct((8, 128), f32)


def place(index):
    y, xl, z = index & 3, (index >> 2) & 1, (index >> 3) & 3
    core, xh = (index >> 5) & 1, (index >> 6) & 1
    return 2 * xh + xl, y, z, core


def index_of(x, y, z, core):
    return (x >> 1) * 64 + core * 32 + z * 8 + (x & 1) * 4 + y


def send(value, target):
    pairs = [(source, index_of(*target(*place(source)))) for source in range(128)]
    return lax.ppermute(value, AXIS, pairs)


def along_x(steps):
    return lambda x, y, z, core: ((x + steps) % 4, y, z, core)


def along_y_or_z(steps):
    return lambda x, y, z, core: (
        (x, y, (z + steps) % 4, core) if core else (x, (y + steps) % 4, z, core)
    )


def along_z_or_y(steps):
    return lambda x, y, z, core: (
        (x, (y + steps) % 4, z, core) if core else (x, y, (z + steps) % 4, core)
    )


def other_core(x, y, z, core):
    return (x, y, z, 1 - core)


LAST_GROUPS = [
    [index_of(2 * xh + xl, y, z, 0) for xh in range(2) for xl in range(2) for y in range(4)]
    for z in range(4)
] + [
    [index_of(2 * xh + xl, y, z, 1) for xh in range(2) for z in range(4) for xl in range(2)]
    for y in range(4)
]


def my_core():
    return (lax.axis_index(AXIS) >> 5) & 1


IN_VMEM = pl.BlockSpec(memory_space=pltpu.VMEM)
IN_SMEM = pl.BlockSpec(memory_space=pltpu.SMEM)


def params():
    return pltpu.CompilerParams(vmem_limit_bytes=VMEM_LIMIT)


def cost(flops, bytes_accessed):
    return pl.CostEstimate(flops=flops, bytes_accessed=bytes_accessed, transcendentals=0)


def begin(pairs, sems, first=0):
    copies = [
        pltpu.make_async_copy(source, target, sems.at[first + slot])
        for slot, (source, target) in enumerate(pairs)
    ]
    for copy in copies:
        copy.start()
    return copies


def finish(copies):
    for copy in copies:
        copy.wait()


def stack(cuts, refs, target):
    offset = 0
    for which, start, rows in cuts:
        target[offset : offset + rows, :] = refs[which][start : start + rows, :]
        offset += rows


def normalize_kernel(text, features, unit, held):
    values = text[...].astype(f32)
    inverse = lax.rsqrt(jnp.sum(values * values, axis=1, keepdims=True) + epsilon)
    unit[...] = (values * inverse).astype(bf16)
    held[...] = features[...]


def normalized(text, features):
    return pl.pallas_call(
        normalize_kernel,
        in_specs=[IN_VMEM] * 2,
        out_specs=[IN_VMEM] * 2,
        out_shape=[jax.ShapeDtypeStruct((ROWS, WIDTH), bf16)] * 2,
        compiler_params=params(),
        name="normalize_text",
    )(text, features)


def join_kernel(counts, after, *refs):
    parts, outs, mark = refs[: sum(counts)], refs[sum(counts) + after : -1], refs[-1]
    for count, out in zip(counts, outs):
        stack([(slot, 0, parts[slot].shape[0]) for slot in range(count)], parts, out)
        parts = parts[count:]
    mark[...] = jnp.zeros(mark.shape, f32)


def joined(groups, *after, work=0):
    counts = [len(group) for group in groups]
    heights = [sum(part.shape[0] for part in group) for group in groups]
    return pl.pallas_call(
        lambda *refs: join_kernel(counts, len(after), *refs),
        in_specs=[IN_VMEM] * (sum(counts) + len(after)),
        out_specs=[IN_VMEM] * (len(groups) + 1),
        out_shape=[jax.ShapeDtypeStruct((rows, WIDTH), bf16) for rows in heights] + [MARK],
        compiler_params=params(),
        cost_estimate=cost(work, 0),
        name="join",
    )(*(part for group in groups for part in group), *after)


def halves_kernel(before, behind, after, low, high):
    low[...] = before[: HALF // 2, :]
    high[...] = behind[HALF // 2 :, :]


def halves(*parts):
    return pl.pallas_call(
        halves_kernel,
        in_specs=[IN_VMEM] * 3,
        out_specs=[IN_VMEM] * 2,
        out_shape=[jax.ShapeDtypeStruct((HALF // 2, WIDTH), bf16)] * 2,
        compiler_params=params(),
        name="halves",
    )(*parts)


def project_kernel(cuts, skip, turns, *refs):
    count = len(set(which for which, _, _ in cuts))
    parts = refs[:count]
    proj, unit, unit_f, inverse, turned, feat = refs[count:]
    stack(cuts, parts, feat)
    emb = jnp.dot(feat[skip:, :], proj[...], preferred_element_type=f32)
    inv = lax.rsqrt(jnp.sum(emb * emb, axis=1, keepdims=True) + epsilon)
    emb = emb * inv
    unit_f[...] = emb
    inverse[...] = jnp.broadcast_to(inv, inverse.shape)
    unit[...] = emb.astype(bf16)
    turned[...] = feat[:turns, :].T


def projected(parts, cuts, skip, turns, proj_w):
    rows = sum(cut[2] for cut in cuts)
    return pl.pallas_call(
        lambda *refs: project_kernel(cuts, skip, turns, *refs),
        in_specs=[IN_VMEM] * (len(parts) + 1),
        out_specs=[IN_VMEM] * 4,
        out_shape=[
            jax.ShapeDtypeStruct((HALF, WIDTH), bf16),
            jax.ShapeDtypeStruct((HALF, WIDTH), f32),
            jax.ShapeDtypeStruct((HALF, 128), f32),
            jax.ShapeDtypeStruct((WIDTH, turns), bf16),
        ],
        scratch_shapes=[pltpu.VMEM((rows, WIDTH), bf16)],
        compiler_params=params(),
        cost_estimate=cost(1000, 1000),
        name="project_images",
    )(*parts, proj_w)


def wave_body(scalars, units, text, sim, weights, diagonal, take):
    half = 0.5 * jnp.exp(scalars[0])
    half_shift = 0.5 * scalars[1]
    for step, unit in enumerate(units):
        sim[...] = lax.dot_general(
            unit[...], text[...], (((1,), (1,)), ((), ())), preferred_element_type=f32
        )
        weights[...] = (half + half * jnp.tanh(half * sim[...] + half_shift)).astype(bf16)
        if diagonal and step == 0:
            tanh = jnp.tanh(half * sim[:ROWS, :256] + half_shift)
            row = lax.broadcasted_iota(jnp.int32, (ROWS, 256), 0)
            column = lax.broadcasted_iota(jnp.int32, (ROWS, 256), 1)
            pair = jnp.where(row == column, half * tanh - half, half + half * tanh)
            weights[:ROWS, :256] = pair.astype(bf16)
        take(step, jnp.dot(weights[...], text[...], preferred_element_type=f32))


def first_wave_kernel(cuts, count, scalars, *refs):
    texts, units, totals = refs[:count], refs[count : count + 2], refs[count + 2 : count + 4]
    mark, text, sim, weights, sems = refs[count + 4 :]
    mark[...] = jnp.zeros(mark.shape, f32)
    stack(cuts, texts, text)

    def take(step, product):
        totals[step][...] = product

    wave_body(scalars, units, text, sim, weights, True, take)


def next_wave_kernel(cuts, count, scalars, *refs):
    texts, units = refs[:count], refs[count : count + 2]
    before, totals = refs[count + 2 : count + 4], refs[count + 4 : count + 6]
    text, sim, weights, sems = refs[count + 6 :]
    stack(cuts, texts, text)

    def take(step, product):
        totals[step][...] = before[step][...] + product

    wave_body(scalars, units, text, sim, weights, False, take)


def last_wave_kernel(cuts, count, scalars, *refs):
    texts, units = refs[:count], refs[count : count + 2]
    before, units_f, inverses, turns, (give, grad_emb) = (
        refs[count + 2 + 2 * slot : count + 4 + 2 * slot] for slot in range(5)
    )
    text, sim, weights, turned, sems = refs[count + 12 :]
    late = begin(turn_copies(turns, turned), sems)
    stack(cuts, texts, text)

    def take(step, product):
        gradient = before[step][...] + product
        image = units_f[step][...]
        along = jnp.sum(image * gradient, axis=1, keepdims=True)
        projection = (gradient - image * along) * inverses[step][:, 0:1]
        grad_emb[HALF * step : HALF * step + HALF, :] = projection.astype(bf16)

    wave_body(scalars, units, text, sim, weights, False, take)
    finish(late)
    write_terms(1 - my_core(), turned, grad_emb, give)


def turn_copies(turns, turned):
    return [
        (turns[0], turned.at[:, pl.ds(0, TURNED)]),
        (turns[1], turned.at[:, pl.ds(TURNED, IMAGES - TURNED)]),
    ]


def write_terms(core, turned, grad_emb, out):
    def terms(start, rows):
        return jnp.dot(
            turned[pl.ds(pl.multiple_of(start, 16), rows), :],
            grad_emb[...],
            preferred_element_type=f32,
        ).astype(out.dtype)

    for high in range(2):
        out[pl.ds(288 * high, 288), :] = terms(576 * high + 288 * core, 288)


def wave(kernel, scalars, cuts, texts, units, extra, out_shape, scratch, aliases, name):
    rows = sum(cut[2] for cut in cuts)
    return pl.pallas_call(
        lambda *refs: kernel(cuts, len(texts), *refs),
        in_specs=[IN_SMEM] + [IN_VMEM] * (len(texts) + len(units) + len(extra)),
        out_specs=[IN_VMEM] * len(out_shape),
        out_shape=out_shape,
        input_output_aliases=aliases,
        scratch_shapes=[
            pltpu.VMEM((rows, WIDTH), bf16),
            pltpu.VMEM((HALF, rows), f32),
            pltpu.VMEM((HALF, rows), bf16),
        ]
        + scratch
        + [pltpu.SemaphoreType.DMA((12,))],
        compiler_params=params(),
        cost_estimate=cost(1000, 1000),
        name=name,
    )(scalars, *texts, *units, *extra)


def keep_kernel(turn_a, turn_b, grad_emb, keep, turned, sems):
    finish(begin(turn_copies((turn_a, turn_b), turned), sems))
    write_terms(my_core(), turned, grad_emb, keep)


def kept_terms(turns, grad_emb):
    return pl.pallas_call(
        keep_kernel,
        in_specs=[IN_VMEM] * 3,
        out_shape=jax.ShapeDtypeStruct((HALF, WIDTH), f32),
        scratch_shapes=[pltpu.VMEM((WIDTH, IMAGES), bf16), pltpu.SemaphoreType.DMA((2,))],
        compiler_params=params(),
        cost_estimate=cost(2 * HALF * WIDTH * IMAGES, 4 * IMAGES * WIDTH),
        name="kept_terms",
    )(*turns, grad_emb)


def chip_sum_kernel(kept, given, mine, one, three, two, total):
    for tile in range(9):
        lanes = slice(128 * tile, 128 * tile + 128)
        total[tile, :, :] = kept[:, lanes] + given[:, lanes].astype(f32)
    index = lax.axis_index(AXIS)
    outs = ((0, mine), (1, one), (3, three), (2, two))

    @pl.when(my_core() == 0)
    def _():
        for steps, out in outs:
            first = 72 * (((index >> 3) + steps) & 3)
            for tile in range(9):
                for row in range(9):
                    parts = [
                        total[tile, pl.ds(288 * high + first + row, 8, stride=9), :]
                        for high in range(2)
                    ]
                    out[16 * row : 16 * row + 16, 128 * tile : 128 * tile + 128] = (
                        jnp.concatenate(parts).astype(out.dtype)
                    )

    @pl.when(my_core() == 1)
    def _():
        for steps, out in outs:
            first = 9 * ((index + steps) & 3)
            for tile in range(9):
                for row in range(9):
                    part = total[tile, pl.ds(first + row, 16, stride=36), :]
                    out[16 * row : 16 * row + 16, 128 * tile : 128 * tile + 128] = part.astype(
                        out.dtype
                    )


def chip_sum(kept, given):
    return pl.pallas_call(
        chip_sum_kernel,
        out_shape=[jax.ShapeDtypeStruct((ROWS, WIDTH), f32)]
        + [jax.ShapeDtypeStruct((ROWS, WIDTH), bf16)] * 3,
        scratch_shapes=[pltpu.VMEM((9, HALF, 128), f32)],
        compiler_params=params(),
        name="chip_sum",
    )(kept, given)


def ring_sum_kernel(mine, one, three, two, out, eights, ninth):
    ninth[...] = jnp.zeros(ninth.shape, f32)
    for tile in range(9):
        lanes = slice(128 * tile, 128 * tile + 128)
        value = mine[:, lanes]
        for part in (one, three, two):
            value = value + part[:, lanes].astype(f32)
        for row in range(8):
            eights[tile, pl.ds(row, 16, stride=8), :] = value[16 * row : 16 * row + 16]
        ninth[tile // 8, pl.ds(tile % 8, 16, stride=8), :] = value[128:]
        out[:, lanes] = eights[tile].astype(bf16)
    out[:, WIDTH : WIDTH + 128] = ninth[0].astype(bf16)
    out[:, WIDTH + 128 :] = ninth[1].astype(bf16)


def ring_sum(*parts):
    return pl.pallas_call(
        ring_sum_kernel,
        out_shape=jax.ShapeDtypeStruct((128, SLAB), bf16),
        scratch_shapes=[pltpu.VMEM((9, 128, 128), f32), pltpu.VMEM((2, 128, 128), f32)],
        compiler_params=params(),
        name="ring_sum",
    )(*parts)


def last_sum_kernel(pieces, out):
    total = jnp.zeros((16, SLAB), f32)
    for step in range(8):
        total = total + pieces[16 * step : 16 * step + 16, :].astype(f32)
    total = total[:8] + total[8:]
    out[:8, :] = total[:, :WIDTH]
    for tile in range(9):
        sublane, lane = tile % 8, WIDTH + 128 * (tile // 8)
        out[8:9, 128 * tile : 128 * tile + 128] = total[sublane : sublane + 1, lane : lane + 128]


def last_sum(pieces):
    return pl.pallas_call(
        last_sum_kernel,
        out_shape=jax.ShapeDtypeStruct((9, WIDTH), f32),
        compiler_params=params(),
        name="last_sum",
    )(pieces)


def ring(value, axis):
    return [send(value, axis(steps)) for steps in (1, 3, 2)]


def per_device(features, text_emb, proj_w, log_scale, bias):
    unit_text, held = normalized(text_emb, features)
    scalars = jnp.concatenate([log_scale, bias])
    line, mark = joined([(unit_text, *ring(unit_text, along_y_or_z))])
    line_1, line_3 = (send(line, along_z_or_y(steps)) for steps in (1, 3))
    next_1, next_3, next_2 = ring(features, along_x)
    low, high, _ = joined([(held, next_1), (next_3, next_2)], mark, work=WORK)
    low_other, high_other = send(low, other_core), send(high, other_core)
    middle = TURNED - HALF // 2
    here = projected((low, high), ((0, 0, HALF // 2), (1, 0, HALF // 2)), 0, TURNED, proj_w)
    there = projected(
        (high, low_other, high_other),
        ((0, middle, HALF - TURNED), (1, 0, HALF // 2), (2, 0, HALF // 2)),
        HALF - TURNED,
        IMAGES - TURNED,
        proj_w,
    )

    units, units_f, inverses, turns = zip(here, there)
    sums = [jax.ShapeDtypeStruct((HALF, WIDTH), f32)] * 2
    *totals, mark = wave(
        first_wave_kernel,
        scalars,
        ((0, 0, 512),),
        (line,),
        units,
        (),
        sums + [MARK],
        [],
        {},
        "first_wave",
    )
    low, high = halves(line_1, line_3, mark)
    low, high = send(low, along_z_or_y(1)), send(high, along_z_or_y(3))
    totals = wave(
        next_wave_kernel,
        scalars,
        ((0, 512, 64), (1, 0, HALF), (2, 0, 384)),
        (line, line_1, line_3),
        units,
        totals,
        sums,
        [],
        {6: 0, 7: 1},
        "second_wave",
    )
    give, grad_emb = wave(
        last_wave_kernel,
        scalars,
        ((0, 384, 192), (1, 0, HALF // 2), (2, 0, HALF // 2)),
        (line_3, low, high),
        units,
        (*totals, *units_f, *inverses, *turns),
        [
            jax.ShapeDtypeStruct((HALF, WIDTH), bf16),
            jax.ShapeDtypeStruct((IMAGES, WIDTH), bf16),
        ],
        [pltpu.VMEM((WIDTH, IMAGES), bf16)],
        {},
        "last_wave",
    )
    given = send(give, other_core)
    keep = kept_terms(turns, grad_emb)
    mine, one, three, two = chip_sum(keep, given)
    parts = [send(part, along_z_or_y(steps)) for part, steps in ((one, 1), (three, 3), (two, 2))]
    pieces = ring_sum(mine, *parts)
    pieces = lax.all_to_all(pieces, AXIS, 0, 0, axis_index_groups=LAST_GROUPS, tiled=True)
    return last_sum(pieces)


def solution(mesh):
    flat = Mesh(mesh.devices.reshape(-1), (AXIS,))
    rows = P(AXIS, None)
    return jax.shard_map(
        per_device,
        mesh=flat,
        in_specs=(rows, rows, P(), P(), P()),
        out_specs=rows,
        check_vma=False,
    )
```

```python
import jax
import jax.numpy as jnp
from jax import lax
from jax.experimental import pallas as pl
from jax.experimental.pallas import tpu as pltpu
from jax.sharding import Mesh, PartitionSpec as P

epsilon = 1e-06
bf16 = jnp.bfloat16
f32 = jnp.float32

AXIS = "d"
ROWS = 144
WIDTH = 1152
HALF = 4 * ROWS
IMAGES = 2 * HALF
TURNED = 512
SLAB = 1408
VMEM_LIMIT = 20 << 20
WORK = 12_000_000_000
MARK = jax.ShapeDtypeStruct((8, 128), f32)


def place(index):
    y, xl, z = index & 3, (index >> 2) & 1, (index >> 3) & 3
    core, xh = (index >> 5) & 1, (index >> 6) & 1
    return 2 * xh + xl, y, z, core


def index_of(x, y, z, core):
    return (x >> 1) * 64 + core * 32 + z * 8 + (x & 1) * 4 + y


def send(value, target):
    pairs = [(source, index_of(*target(*place(source)))) for source in range(128)]
    return lax.ppermute(value, AXIS, pairs)


def along_x(steps):
    return lambda x, y, z, core: ((x + steps) % 4, y, z, core)


def along_y_or_z(steps):
    return lambda x, y, z, core: (
        (x, y, (z + steps) % 4, core) if core else (x, (y + steps) % 4, z, core)
    )


def along_z_or_y(steps):
    return lambda x, y, z, core: (
        (x, (y + steps) % 4, z, core) if core else (x, y, (z + steps) % 4, core)
    )


def other_core(x, y, z, core):
    return (x, y, z, 1 - core)


LAST_GROUPS = [
    [index_of(2 * xh + xl, y, z, 0) for xh in range(2) for xl in range(2) for y in range(4)]
    for z in range(4)
] + [
    [index_of(2 * xh + xl, y, z, 1) for xh in range(2) for z in range(4) for xl in range(2)]
    for y in range(4)
]


def my_core():
    return (lax.axis_index(AXIS) >> 5) & 1


IN_VMEM = pl.BlockSpec(memory_space=pltpu.VMEM)
IN_SMEM = pl.BlockSpec(memory_space=pltpu.SMEM)


def params():
    return pltpu.CompilerParams(vmem_limit_bytes=VMEM_LIMIT)


def cost(flops, bytes_accessed):
    return pl.CostEstimate(flops=flops, bytes_accessed=bytes_accessed, transcendentals=0)


def begin(pairs, sems, first=0):
    copies = [
        pltpu.make_async_copy(source, target, sems.at[first + slot])
        for slot, (source, target) in enumerate(pairs)
    ]
    for copy in copies:
        copy.start()
    return copies


def finish(copies):
    for copy in copies:
        copy.wait()


def stack(cuts, refs, target):
    offset = 0
    for which, start, rows in cuts:
        target[offset : offset + rows, :] = refs[which][start : start + rows, :]
        offset += rows


def normalize_kernel(parts, line, mark):
    for slot, part in enumerate(parts):
        values = part[...].astype(f32)
        inverse = lax.rsqrt(jnp.sum(values * values, axis=1, keepdims=True) + epsilon)
        line[ROWS * slot : ROWS * slot + ROWS, :] = (values * inverse).astype(bf16)
    mark[...] = jnp.zeros(mark.shape, f32)


def normalized(*parts):
    return pl.pallas_call(
        lambda *refs: normalize_kernel(refs[:4], *refs[4:]),
        in_specs=[IN_VMEM] * 4,
        out_specs=[IN_VMEM] * 2,
        out_shape=[jax.ShapeDtypeStruct((HALF, WIDTH), bf16), MARK],
        compiler_params=params(),
        name="normalize_texts",
    )(*parts)


def join_kernel(own, opposite, next_1, next_3, after, low, high):
    low[:ROWS, :] = own[...]
    low[ROWS:, :] = next_1[...]
    high[:ROWS, :] = next_3[...]
    high[ROWS:, :] = opposite[...]


def joined(*parts):
    return pl.pallas_call(
        join_kernel,
        in_specs=[IN_VMEM] * 5,
        out_specs=[IN_VMEM] * 2,
        out_shape=[jax.ShapeDtypeStruct((HALF // 2, WIDTH), bf16)] * 2,
        compiler_params=params(),
        cost_estimate=cost(WORK, 0),
        name="join",
    )(*parts)


def halves_kernel(before, behind, after, low, high):
    low[...] = before[: HALF // 2, :]
    high[...] = behind[HALF // 2 :, :]


def halves(*parts):
    return pl.pallas_call(
        halves_kernel,
        in_specs=[IN_VMEM] * 3,
        out_specs=[IN_VMEM] * 2,
        out_shape=[jax.ShapeDtypeStruct((HALF // 2, WIDTH), bf16)] * 2,
        compiler_params=params(),
        name="halves",
    )(*parts)


def project_kernel(cuts, skip, turns, *refs):
    count = len(set(which for which, _, _ in cuts))
    parts = refs[:count]
    proj, unit, unit_f, inverse, turned, feat = refs[count:]
    stack(cuts, parts, feat)
    emb = jnp.dot(feat[skip:, :], proj[...], preferred_element_type=f32)
    inv = lax.rsqrt(jnp.sum(emb * emb, axis=1, keepdims=True) + epsilon)
    emb = emb * inv
    unit_f[...] = emb
    inverse[...] = jnp.broadcast_to(inv, inverse.shape)
    unit[...] = emb.astype(bf16)
    turned[...] = feat[:turns, :].T


def projected(parts, cuts, skip, turns, proj_w):
    rows = sum(cut[2] for cut in cuts)
    return pl.pallas_call(
        lambda *refs: project_kernel(cuts, skip, turns, *refs),
        in_specs=[IN_VMEM] * (len(parts) + 1),
        out_specs=[IN_VMEM] * 4,
        out_shape=[
            jax.ShapeDtypeStruct((HALF, WIDTH), bf16),
            jax.ShapeDtypeStruct((HALF, WIDTH), f32),
            jax.ShapeDtypeStruct((HALF, 128), f32),
            jax.ShapeDtypeStruct((WIDTH, turns), bf16),
        ],
        scratch_shapes=[pltpu.VMEM((rows, WIDTH), bf16)],
        compiler_params=params(),
        cost_estimate=cost(1000, 1000),
        name="project_images",
    )(*parts, proj_w)


def wave_body(scalars, units, text, sim, weights, diagonal, take):
    half = 0.5 * jnp.exp(scalars[0])
    half_shift = 0.5 * scalars[1]

    def weigh(step):
        rows = slice(HALF * step, HALF * step + HALF)
        sim[rows, :] = lax.dot_general(
            units[step][...], text[...], (((1,), (1,)), ((), ())), preferred_element_type=f32
        )
        weights[rows, :] = (half + half * jnp.tanh(half * sim[rows, :] + half_shift)).astype(bf16)

    weigh(0)
    if diagonal:
        tanh = jnp.tanh(half * sim[:ROWS, :256] + half_shift)
        row = lax.broadcasted_iota(jnp.int32, (ROWS, 256), 0)
        column = lax.broadcasted_iota(jnp.int32, (ROWS, 256), 1)
        pair = jnp.where(row == column, half * tanh - half, half + half * tanh)
        weights[:ROWS, :256] = pair.astype(bf16)
    weigh(1)
    for step in range(2):
        rows = slice(HALF * step, HALF * step + HALF)
        take(step, jnp.dot(weights[rows, :], text[...], preferred_element_type=f32))


def first_wave_kernel(cuts, count, scalars, *refs):
    texts, units, totals = refs[:count], refs[count : count + 2], refs[count + 2 : count + 4]
    mark, text, sim, weights, sems = refs[count + 4 :]
    mark[...] = jnp.zeros(mark.shape, f32)
    stack(cuts, texts, text)

    def take(step, product):
        totals[step][...] = product

    wave_body(scalars, units, text, sim, weights, True, take)


def next_wave_kernel(cuts, count, scalars, *refs):
    texts, units = refs[:count], refs[count : count + 2]
    before, totals = refs[count + 2 : count + 4], refs[count + 4 : count + 6]
    text, sim, weights, sems = refs[count + 6 :]
    stack(cuts, texts, text)

    def take(step, product):
        totals[step][...] = before[step][...] + product

    wave_body(scalars, units, text, sim, weights, False, take)


def last_wave_kernel(cuts, count, scalars, *refs):
    texts, units = refs[:count], refs[count : count + 2]
    before, units_f, inverses, turns, (give, grad_emb) = (
        refs[count + 2 + 2 * slot : count + 4 + 2 * slot] for slot in range(5)
    )
    text, sim, weights, turned, sems = refs[count + 12 :]
    late = begin(turn_copies(turns, turned), sems)
    stack(cuts, texts, text)

    def take(step, product):
        gradient = before[step][...] + product
        image = units_f[step][...]
        along = jnp.sum(image * gradient, axis=1, keepdims=True)
        projection = (gradient - image * along) * inverses[step][:, 0:1]
        grad_emb[HALF * step : HALF * step + HALF, :] = projection.astype(bf16)

    wave_body(scalars, units, text, sim, weights, False, take)
    finish(late)
    write_terms(1 - my_core(), turned, grad_emb, give)


def turn_copies(turns, turned):
    return [
        (turns[0], turned.at[:, pl.ds(0, TURNED)]),
        (turns[1], turned.at[:, pl.ds(TURNED, IMAGES - TURNED)]),
    ]


def write_terms(core, turned, grad_emb, out):
    def terms(start, rows):
        return jnp.dot(
            turned[pl.ds(pl.multiple_of(start, 16), rows), :],
            grad_emb[...],
            preferred_element_type=f32,
        ).astype(out.dtype)

    for high in range(2):
        out[pl.ds(288 * high, 288), :] = terms(576 * high + 288 * core, 288)


def wave(kernel, scalars, cuts, texts, units, extra, out_shape, scratch, aliases, name):
    rows = sum(cut[2] for cut in cuts)
    return pl.pallas_call(
        lambda *refs: kernel(cuts, len(texts), *refs),
        in_specs=[IN_SMEM] + [IN_VMEM] * (len(texts) + len(units) + len(extra)),
        out_specs=[IN_VMEM] * len(out_shape),
        out_shape=out_shape,
        input_output_aliases=aliases,
        scratch_shapes=[
            pltpu.VMEM((rows, WIDTH), bf16),
            pltpu.VMEM((IMAGES, rows), f32),
            pltpu.VMEM((IMAGES, rows), bf16),
        ]
        + scratch
        + [pltpu.SemaphoreType.DMA((12,))],
        compiler_params=params(),
        cost_estimate=cost(1000, 1000),
        name=name,
    )(scalars, *texts, *units, *extra)


def keep_kernel(turn_a, turn_b, grad_emb, keep, turned, sems):
    finish(begin(turn_copies((turn_a, turn_b), turned), sems))
    write_terms(my_core(), turned, grad_emb, keep)


def kept_terms(turns, grad_emb):
    return pl.pallas_call(
        keep_kernel,
        in_specs=[IN_VMEM] * 3,
        out_shape=jax.ShapeDtypeStruct((HALF, WIDTH), f32),
        scratch_shapes=[pltpu.VMEM((WIDTH, IMAGES), bf16), pltpu.SemaphoreType.DMA((2,))],
        compiler_params=params(),
        cost_estimate=cost(2 * HALF * WIDTH * IMAGES, 4 * IMAGES * WIDTH),
        name="kept_terms",
    )(*turns, grad_emb)


def chip_sum_kernel(kept, given, mine, two, one, three, total):
    for tile in range(9):
        lanes = slice(128 * tile, 128 * tile + 128)
        total[tile, :, :] = kept[:, lanes] + given[:, lanes].astype(f32)
    index = lax.axis_index(AXIS)
    outs = ((0, mine), (2, two), (1, one), (3, three))

    @pl.when(my_core() == 0)
    def _():
        for steps, out in outs:
            first = 72 * (((index >> 3) + steps) & 3)
            for tile in range(9):
                for row in range(9):
                    parts = [
                        total[tile, pl.ds(288 * high + first + row, 8, stride=9), :]
                        for high in range(2)
                    ]
                    out[16 * row : 16 * row + 16, 128 * tile : 128 * tile + 128] = (
                        jnp.concatenate(parts).astype(out.dtype)
                    )

    @pl.when(my_core() == 1)
    def _():
        for steps, out in outs:
            first = 9 * ((index + steps) & 3)
            for tile in range(9):
                for row in range(9):
                    part = total[tile, pl.ds(first + row, 16, stride=36), :]
                    out[16 * row : 16 * row + 16, 128 * tile : 128 * tile + 128] = part.astype(
                        out.dtype
                    )


def chip_sum(kept, given):
    return pl.pallas_call(
        chip_sum_kernel,
        out_shape=[jax.ShapeDtypeStruct((ROWS, WIDTH), f32)]
        + [jax.ShapeDtypeStruct((ROWS, WIDTH), bf16)] * 3,
        scratch_shapes=[pltpu.VMEM((9, HALF, 128), f32)],
        compiler_params=params(),
        name="chip_sum",
    )(kept, given)


def ring_sum_kernel(mine, two, one, three, out, eights, ninth):
    ninth[...] = jnp.zeros(ninth.shape, f32)
    for tile in range(9):
        lanes = slice(128 * tile, 128 * tile + 128)
        value = mine[:, lanes]
        for part in (two, one, three):
            value = value + part[:, lanes].astype(f32)
        for row in range(8):
            eights[tile, pl.ds(row, 16, stride=8), :] = value[16 * row : 16 * row + 16]
        ninth[tile // 8, pl.ds(tile % 8, 16, stride=8), :] = value[128:]
        out[:, lanes] = eights[tile].astype(bf16)
    out[:, WIDTH : WIDTH + 128] = ninth[0].astype(bf16)
    out[:, WIDTH + 128 :] = ninth[1].astype(bf16)


def ring_sum(*parts):
    return pl.pallas_call(
        ring_sum_kernel,
        out_shape=jax.ShapeDtypeStruct((128, SLAB), bf16),
        scratch_shapes=[pltpu.VMEM((9, 128, 128), f32), pltpu.VMEM((2, 128, 128), f32)],
        compiler_params=params(),
        name="ring_sum",
    )(*parts)


def last_sum_kernel(pieces, out):
    total = jnp.zeros((16, SLAB), f32)
    for step in range(8):
        total = total + pieces[16 * step : 16 * step + 16, :].astype(f32)
    total = total[:8] + total[8:]
    out[:8, :] = total[:, :WIDTH]
    for tile in range(9):
        sublane, lane = tile % 8, WIDTH + 128 * (tile // 8)
        out[8:9, 128 * tile : 128 * tile + 128] = total[sublane : sublane + 1, lane : lane + 128]


def last_sum(pieces):
    return pl.pallas_call(
        last_sum_kernel,
        out_shape=jax.ShapeDtypeStruct((9, WIDTH), f32),
        compiler_params=params(),
        name="last_sum",
    )(pieces)


def ring(value, axis):
    return [send(value, axis(steps)) for steps in (2, 1, 3)]


def per_device(features, text_emb, proj_w, log_scale, bias):
    scalars = jnp.concatenate([log_scale, bias])
    line, mark = normalized(text_emb, *ring(text_emb, along_y_or_z))
    line_1, line_3 = (send(line, along_z_or_y(steps)) for steps in (1, 3))
    low, high = joined(features, *ring(features, along_x), mark)
    low_other, high_other = send(low, other_core), send(high, other_core)
    middle = TURNED - HALF // 2
    here = projected((low, high), ((0, 0, HALF // 2), (1, 0, HALF // 2)), 0, TURNED, proj_w)
    there = projected(
        (high, low_other, high_other),
        ((0, middle, HALF - TURNED), (1, 0, HALF // 2), (2, 0, HALF // 2)),
        HALF - TURNED,
        IMAGES - TURNED,
        proj_w,
    )

    units, units_f, inverses, turns = zip(here, there)
    sums = [jax.ShapeDtypeStruct((HALF, WIDTH), f32)] * 2
    *totals, mark = wave(
        first_wave_kernel,
        scalars,
        ((0, 0, 512),),
        (line,),
        units,
        (),
        sums + [MARK],
        [],
        {},
        "first_wave",
    )
    low, high = halves(line_1, line_3, mark)
    low, high = send(low, along_z_or_y(1)), send(high, along_z_or_y(3))
    totals = wave(
        next_wave_kernel,
        scalars,
        ((0, 512, 64), (1, 0, HALF), (2, 0, 384)),
        (line, line_1, line_3),
        units,
        totals,
        sums,
        [],
        {6: 0, 7: 1},
        "second_wave",
    )
    give, grad_emb = wave(
        last_wave_kernel,
        scalars,
        ((0, 384, 192), (1, 0, HALF // 2), (2, 0, HALF // 2)),
        (line_3, low, high),
        units,
        (*totals, *units_f, *inverses, *turns),
        [
            jax.ShapeDtypeStruct((HALF, WIDTH), bf16),
            jax.ShapeDtypeStruct((IMAGES, WIDTH), bf16),
        ],
        [pltpu.VMEM((WIDTH, IMAGES), bf16)],
        {},
        "last_wave",
    )
    given = send(give, other_core)
    keep = kept_terms(turns, grad_emb)
    mine, two, one, three = chip_sum(keep, given)
    parts = [send(part, along_z_or_y(steps)) for part, steps in ((two, 2), (one, 1), (three, 3))]
    pieces = ring_sum(mine, *parts)
    pieces = lax.all_to_all(pieces, AXIS, 0, 0, axis_index_groups=LAST_GROUPS, tiled=True)
    return last_sum(pieces)


def solution(mesh):
    flat = Mesh(mesh.devices.reshape(-1), (AXIS,))
    rows = P(AXIS, None)
    return jax.shard_map(
        per_device,
        mesh=flat,
        in_specs=(rows, rows, P(), P(), P()),
        out_specs=rows,
        check_vma=False,
    )
```

```python
import jax
import jax.numpy as jnp
from jax import lax
from jax.experimental import pallas as pl
from jax.experimental.pallas import tpu as pltpu
from jax.sharding import Mesh, PartitionSpec as P

epsilon = 1e-06
bf16 = jnp.bfloat16
f32 = jnp.float32

AXIS = "d"
ROWS = 144
WIDTH = 1152
HALF = 4 * ROWS
IMAGES = 2 * HALF
TURNED = 512
SLAB = 1408
VMEM_LIMIT = 20 << 20
WORK = 12_000_000_000
HOLD = 12_000_000_000
MARK = jax.ShapeDtypeStruct((8, 128), f32)


def place(index):
    y, xl, z = index & 3, (index >> 2) & 1, (index >> 3) & 3
    core, xh = (index >> 5) & 1, (index >> 6) & 1
    return 2 * xh + xl, y, z, core


def index_of(x, y, z, core):
    return (x >> 1) * 64 + core * 32 + z * 8 + (x & 1) * 4 + y


def send(value, target):
    pairs = [(source, index_of(*target(*place(source)))) for source in range(128)]
    return lax.ppermute(value, AXIS, pairs)


def along_x(steps):
    return lambda x, y, z, core: ((x + steps) % 4, y, z, core)


def along_y_or_z(steps):
    return lambda x, y, z, core: (
        (x, y, (z + steps) % 4, core) if core else (x, (y + steps) % 4, z, core)
    )


def along_z_or_y(steps):
    return lambda x, y, z, core: (
        (x, (y + steps) % 4, z, core) if core else (x, y, (z + steps) % 4, core)
    )


def other_core(x, y, z, core):
    return (x, y, z, 1 - core)


LAST_GROUPS = [
    [index_of(2 * xh + xl, y, z, 0) for xh in range(2) for xl in range(2) for y in range(4)]
    for z in range(4)
] + [
    [index_of(2 * xh + xl, y, z, 1) for xh in range(2) for z in range(4) for xl in range(2)]
    for y in range(4)
]


def my_core():
    return (lax.axis_index(AXIS) >> 5) & 1


IN_VMEM = pl.BlockSpec(memory_space=pltpu.VMEM)
IN_SMEM = pl.BlockSpec(memory_space=pltpu.SMEM)


def params():
    return pltpu.CompilerParams(vmem_limit_bytes=VMEM_LIMIT)


def cost(flops, bytes_accessed):
    return pl.CostEstimate(flops=flops, bytes_accessed=bytes_accessed, transcendentals=0)


def begin(pairs, sems, first=0):
    copies = [
        pltpu.make_async_copy(source, target, sems.at[first + slot])
        for slot, (source, target) in enumerate(pairs)
    ]
    for copy in copies:
        copy.start()
    return copies


def finish(copies):
    for copy in copies:
        copy.wait()


def stack(cuts, refs, target):
    offset = 0
    for which, start, rows in cuts:
        target[offset : offset + rows, :] = refs[which][start : start + rows, :]
        offset += rows


def hold_kernel(text, features, log_scale, bias, text_held, features_held, scalars):
    text_held[...] = text[...]
    features_held[...] = features[...]
    scalars[0:1, :] = jnp.full((1, 128), log_scale[0], f32)
    scalars[1:2, :] = jnp.full((1, 128), bias[0], f32)


def held(*arrays):
    return pl.pallas_call(
        hold_kernel,
        in_specs=[IN_VMEM] * 2 + [IN_SMEM] * 2,
        out_specs=[IN_VMEM] * 3,
        out_shape=[jax.ShapeDtypeStruct((ROWS, WIDTH), bf16)] * 2 + [MARK],
        compiler_params=params(),
        cost_estimate=cost(HOLD, 0),
        name="hold",
    )(*arrays)


def normalize_kernel(own, opposite, next_1, next_3, line, mark):
    mark[...] = jnp.zeros(mark.shape, f32)
    for slot, part in enumerate((own, opposite, next_1, next_3)):
        values = part[...].astype(f32)
        inverse = lax.rsqrt(jnp.sum(values * values, axis=1, keepdims=True) + epsilon)
        line[ROWS * slot : ROWS * slot + ROWS, :] = (values * inverse).astype(bf16)


def normalized(*parts):
    return pl.pallas_call(
        normalize_kernel,
        in_specs=[IN_VMEM] * 4,
        out_specs=[IN_VMEM] * 2,
        out_shape=[jax.ShapeDtypeStruct((HALF, WIDTH), bf16), MARK],
        compiler_params=params(),
        name="normalize_texts",
    )(*parts)


def join_kernel(own, opposite, next_1, next_3, after, low, high):
    low[:ROWS, :] = own[...]
    low[ROWS:, :] = next_1[...]
    high[:ROWS, :] = next_3[...]
    high[ROWS:, :] = opposite[...]


def joined(*parts):
    return pl.pallas_call(
        join_kernel,
        in_specs=[IN_VMEM] * 5,
        out_specs=[IN_VMEM] * 2,
        out_shape=[jax.ShapeDtypeStruct((HALF // 2, WIDTH), bf16)] * 2,
        compiler_params=params(),
        cost_estimate=cost(WORK, 0),
        name="join",
    )(*parts)


def halves_kernel(before, behind, after, low, high):
    low[...] = before[: HALF // 2, :]
    high[...] = behind[HALF // 2 :, :]


def halves(*parts):
    return pl.pallas_call(
        halves_kernel,
        in_specs=[IN_VMEM] * 3,
        out_specs=[IN_VMEM] * 2,
        out_shape=[jax.ShapeDtypeStruct((HALF // 2, WIDTH), bf16)] * 2,
        compiler_params=params(),
        name="halves",
    )(*parts)


def project_kernel(low, high, proj, unit, unit_f, inverse, turned, feat):
    feat[: HALF // 2, :] = low[...]
    feat[HALF // 2 :, :] = high[...]
    emb = jnp.dot(feat[...], proj[...], preferred_element_type=f32)
    inv = lax.rsqrt(jnp.sum(emb * emb, axis=1, keepdims=True) + epsilon)
    emb = emb * inv
    unit_f[...] = emb
    inverse[...] = jnp.broadcast_to(inv, inverse.shape)
    unit[...] = emb.astype(bf16)
    turned[...] = feat[...].T


def projected(low, high, proj_w):
    return pl.pallas_call(
        project_kernel,
        in_specs=[IN_VMEM] * 3,
        out_specs=[IN_VMEM] * 4,
        out_shape=[
            jax.ShapeDtypeStruct((HALF, WIDTH), bf16),
            jax.ShapeDtypeStruct((HALF, WIDTH), f32),
            jax.ShapeDtypeStruct((HALF, 128), f32),
            jax.ShapeDtypeStruct((WIDTH, HALF), bf16),
        ],
        scratch_shapes=[pltpu.VMEM((HALF, WIDTH), bf16)],
        compiler_params=params(),
        cost_estimate=cost(1000, 1000),
        name="project_images",
    )(low, high, proj_w)


def wave_body(cuts, texts, units, scalars, scratch, diagonal, take):
    text, sim, weights = scratch
    stack(cuts, texts, text)

    def similar(step):
        sim[HALF * step : HALF * step + HALF, :] = lax.dot_general(
            units[step][...], text[...], (((1,), (1,)), ((), ())), preferred_element_type=f32
        )

    similar(0)
    half = 0.5 * jnp.exp(scalars[0:1, 0:1])
    half_shift = 0.5 * scalars[1:2, 0:1]

    def weigh(step):
        rows = slice(HALF * step, HALF * step + HALF)
        weights[rows, :] = (half + half * jnp.tanh(half * sim[rows, :] + half_shift)).astype(bf16)

    weigh(0)
    if diagonal:
        tanh = jnp.tanh(half * sim[:ROWS, :256] + half_shift)
        row = lax.broadcasted_iota(jnp.int32, (ROWS, 256), 0)
        column = lax.broadcasted_iota(jnp.int32, (ROWS, 256), 1)
        pair = jnp.where(row == column, half * tanh - half, half + half * tanh)
        weights[:ROWS, :256] = pair.astype(bf16)
    for step in range(1, len(units)):
        similar(step)
        weigh(step)
    for step in range(len(units)):
        rows = slice(HALF * step, HALF * step + HALF)
        take(step, jnp.dot(weights[rows, :], text[...], preferred_element_type=f32))


def first_wave_kernel(cuts, count, *refs):
    scalars, texts, units = refs[0], refs[1 : count + 1], refs[count + 1 : count + 3]
    totals, mark, scratch = refs[count + 3 : count + 5], refs[count + 5], refs[count + 6 :]
    mark[...] = jnp.zeros(mark.shape, f32)

    def take(step, product):
        totals[step][...] = product

    wave_body(cuts, texts, units, scalars, scratch, True, take)


def next_wave_kernel(cuts, count, *refs):
    scalars, texts, units = refs[0], refs[1 : count + 1], refs[count + 1 : count + 3]
    before, totals, scratch = refs[count + 3 : count + 5], refs[count + 5 : count + 7], refs[count + 7 :]

    def take(step, product):
        totals[step][...] = before[step][...] + product

    wave_body(cuts, texts, units, scalars, scratch, False, take)


def last_wave_kernel(cuts, count, *refs):
    scalars, texts, units = refs[0], refs[1 : count + 1], refs[count + 1 : count + 2]
    before, unit_f, inverse, projected_f, projected_b = refs[count + 2 : count + 7]
    scratch = refs[count + 7 :]

    def take(step, product):
        gradient = before[...] + product
        image = unit_f[...]
        along = jnp.sum(image * gradient, axis=1, keepdims=True)
        projection = (gradient - image * along) * inverse[:, 0:1]
        projected_f[...] = projection
        projected_b[...] = projection.astype(bf16)

    wave_body(cuts, texts, units, scalars, scratch, False, take)


def wave(kernel, scalars, cuts, texts, units, extra, out_shape, aliases, name):
    rows = sum(cut[2] for cut in cuts)
    images = HALF * len(units)
    return pl.pallas_call(
        lambda *refs: kernel(cuts, len(texts), *refs),
        in_specs=[IN_VMEM] * (1 + len(texts) + len(units) + len(extra)),
        out_specs=[IN_VMEM] * len(out_shape),
        out_shape=out_shape,
        input_output_aliases=aliases,
        scratch_shapes=[
            pltpu.VMEM((rows, WIDTH), bf16),
            pltpu.VMEM((images, rows), f32),
            pltpu.VMEM((images, rows), bf16),
        ],
        compiler_params=params(),
        cost_estimate=cost(1000, 1000),
        name=name,
    )(scalars, *texts, *units, *extra)


def terms(turned, projected_f, other):
    both = (projected_f[...] + other[...].astype(f32)).astype(bf16)
    core = my_core()
    return [
        jnp.dot(
            turned[pl.ds(pl.multiple_of(576 * high + 288 * core, 16), 288), :],
            both,
            preferred_element_type=f32,
        )
        for high in range(2)
    ]


def first_terms_kernel(turned, projected_f, other, out):
    for high, term in enumerate(terms(turned, projected_f, other)):
        out[288 * high : 288 * high + 288, :] = term


def first_terms(*parts):
    return pl.pallas_call(
        first_terms_kernel,
        in_specs=[IN_VMEM] * 3,
        out_specs=IN_VMEM,
        out_shape=jax.ShapeDtypeStruct((HALF, WIDTH), f32),
        compiler_params=params(),
        cost_estimate=cost(1000, 1000),
        name="first_terms",
    )(*parts)


def cut_terms_kernel(turned, projected_f, other, first, mine, two, one, three, total):
    for high, term in enumerate(terms(turned, projected_f, other)):
        rows = slice(288 * high, 288 * high + 288)
        for tile in range(9):
            lanes = slice(128 * tile, 128 * tile + 128)
            total[tile, rows, :] = first[rows, lanes] + term[:, lanes]
    index = lax.axis_index(AXIS)
    outs = ((0, mine), (2, two), (1, one), (3, three))

    @pl.when(my_core() == 0)
    def _():
        for steps, out in outs:
            first = 72 * (((index >> 3) + steps) & 3)
            for tile in range(9):
                for row in range(9):
                    parts = [
                        total[tile, pl.ds(288 * high + first + row, 8, stride=9), :]
                        for high in range(2)
                    ]
                    out[16 * row : 16 * row + 16, 128 * tile : 128 * tile + 128] = (
                        jnp.concatenate(parts).astype(out.dtype)
                    )

    @pl.when(my_core() == 1)
    def _():
        for steps, out in outs:
            first = 9 * ((index + steps) & 3)
            for tile in range(9):
                for row in range(9):
                    part = total[tile, pl.ds(first + row, 16, stride=36), :]
                    out[16 * row : 16 * row + 16, 128 * tile : 128 * tile + 128] = part.astype(
                        out.dtype
                    )


def cut_terms(*parts):
    return pl.pallas_call(
        cut_terms_kernel,
        in_specs=[IN_VMEM] * 4,
        out_specs=[IN_VMEM] * 4,
        out_shape=[jax.ShapeDtypeStruct((ROWS, WIDTH), f32)]
        + [jax.ShapeDtypeStruct((ROWS, WIDTH), bf16)] * 3,
        scratch_shapes=[pltpu.VMEM((9, HALF, 128), f32)],
        compiler_params=params(),
        name="cut_terms",
    )(*parts)


def ring_sum_kernel(mine, two, one, three, out, eights, ninth):
    ninth[...] = jnp.zeros(ninth.shape, f32)
    for tile in range(9):
        lanes = slice(128 * tile, 128 * tile + 128)
        value = mine[:, lanes]
        for part in (two, one, three):
            value = value + part[:, lanes].astype(f32)
        for row in range(8):
            eights[tile, pl.ds(row, 16, stride=8), :] = value[16 * row : 16 * row + 16]
        ninth[tile // 8, pl.ds(tile % 8, 16, stride=8), :] = value[128:]
        out[:, lanes] = eights[tile].astype(bf16)
    out[:, WIDTH : WIDTH + 128] = ninth[0].astype(bf16)
    out[:, WIDTH + 128 :] = ninth[1].astype(bf16)


def ring_sum(*parts):
    return pl.pallas_call(
        ring_sum_kernel,
        out_shape=jax.ShapeDtypeStruct((128, SLAB), bf16),
        scratch_shapes=[pltpu.VMEM((9, 128, 128), f32), pltpu.VMEM((2, 128, 128), f32)],
        compiler_params=params(),
        name="ring_sum",
    )(*parts)


def last_sum_kernel(pieces, out):
    total = jnp.zeros((16, SLAB), f32)
    for step in range(8):
        total = total + pieces[16 * step : 16 * step + 16, :].astype(f32)
    total = total[:8] + total[8:]
    out[:8, :] = total[:, :WIDTH]
    for tile in range(9):
        sublane, lane = tile % 8, WIDTH + 128 * (tile // 8)
        out[8:9, 128 * tile : 128 * tile + 128] = total[sublane : sublane + 1, lane : lane + 128]


def last_sum(pieces):
    return pl.pallas_call(
        last_sum_kernel,
        out_shape=jax.ShapeDtypeStruct((9, WIDTH), f32),
        compiler_params=params(),
        name="last_sum",
    )(pieces)


def ring(value, axis):
    return [send(value, axis(steps)) for steps in (2, 1, 3)]


def per_device(features, text_emb, proj_w, log_scale, bias):
    text, images, scalars = held(text_emb, features, log_scale, bias)
    line, mark = normalized(text, *ring(text_emb, along_y_or_z))
    line_1, line_3 = (send(line, along_z_or_y(steps)) for steps in (1, 3))
    low, high = joined(images, *ring(features, along_x), mark)
    low_other, high_other = send(low, other_core), send(high, other_core)
    units, units_f, inverses, turns = zip(
        projected(low, high, proj_w), projected(low_other, high_other, proj_w)
    )

    sums = [jax.ShapeDtypeStruct((HALF, WIDTH), f32)] * 2
    *totals, mark = wave(
        first_wave_kernel,
        scalars,
        ((0, 0, 512),),
        (line,),
        units,
        (),
        sums + [MARK],
        {},
        "first_wave",
    )
    low, high = halves(line_1, line_3, mark)
    low, high = send(low, along_z_or_y(1)), send(high, along_z_or_y(3))
    totals = wave(
        next_wave_kernel,
        scalars,
        ((0, 512, 64), (1, 0, HALF), (2, 0, 384)),
        (line, line_1, line_3),
        units,
        totals,
        sums,
        {6: 0, 7: 1},
        "second_wave",
    )
    own, sent = zip(
        *(
            wave(
                last_wave_kernel,
                scalars,
                ((0, 384, 192), (1, 0, HALF // 2), (2, 0, HALF // 2)),
                (line_3, low, high),
                units[half : half + 1],
                (totals[half], units_f[half], inverses[half]),
                [
                    jax.ShapeDtypeStruct((HALF, WIDTH), f32),
                    jax.ShapeDtypeStruct((HALF, WIDTH), bf16),
                ],
                {},
                "last_wave",
            )
            for half in range(2)
        )
    )
    got = [send(half, other_core) for half in sent]
    first = first_terms(turns[1], own[1], got[0])
    mine, two, one, three = cut_terms(turns[0], own[0], got[1], first)
    parts = [send(part, along_z_or_y(steps)) for part, steps in ((two, 2), (one, 1), (three, 3))]
    pieces = ring_sum(mine, *parts)
    pieces = lax.all_to_all(pieces, AXIS, 0, 0, axis_index_groups=LAST_GROUPS, tiled=True)
    return last_sum(pieces)


def solution(mesh):
    flat = Mesh(mesh.devices.reshape(-1), (AXIS,))
    rows = P(AXIS, None)
    return jax.shard_map(
        per_device,
        mesh=flat,
        in_specs=(rows, rows, P(), P(), P()),
        out_specs=rows,
        check_vma=False,
    )
```

```python
import jax
import jax.numpy as jnp
from jax import lax
from jax.experimental import pallas as pl
from jax.experimental.pallas import tpu as pltpu
from jax.sharding import Mesh, PartitionSpec as P

epsilon = 1e-06
bf16 = jnp.bfloat16
f32 = jnp.float32

AXIS = "d"
ROWS = 144
WIDTH = 1152
HALF = 4 * ROWS
IMAGES = 2 * HALF
TURNED = 512
SLAB = 1408
VMEM_LIMIT = 20 << 20
WORK = 12_000_000_000
PROJ = 20_000_000_000
W1 = 30_000_000_000
WAVES = {"first_wave": W1, "second_wave": 1000, "last_wave": 1000}
HOLD = 1000
MARK = jax.ShapeDtypeStruct((8, 128), f32)


def place(index):
    y, xl, z = index & 3, (index >> 2) & 1, (index >> 3) & 3
    core, xh = (index >> 5) & 1, (index >> 6) & 1
    return 2 * xh + xl, y, z, core


def index_of(x, y, z, core):
    return (x >> 1) * 64 + core * 32 + z * 8 + (x & 1) * 4 + y


def send(value, target):
    pairs = [(source, index_of(*target(*place(source)))) for source in range(128)]
    return lax.ppermute(value, AXIS, pairs)


def along_x(steps):
    return lambda x, y, z, core: ((x + steps) % 4, y, z, core)


def along_y_or_z(steps):
    return lambda x, y, z, core: (
        (x, y, (z + steps) % 4, core) if core else (x, (y + steps) % 4, z, core)
    )


def along_z_or_y(steps):
    return lambda x, y, z, core: (
        (x, (y + steps) % 4, z, core) if core else (x, y, (z + steps) % 4, core)
    )


def other_core(x, y, z, core):
    return (x, y, z, 1 - core)


LAST_GROUPS = [
    [index_of(2 * xh + xl, y, z, 0) for xh in range(2) for xl in range(2) for y in range(4)]
    for z in range(4)
] + [
    [index_of(2 * xh + xl, y, z, 1) for xh in range(2) for z in range(4) for xl in range(2)]
    for y in range(4)
]


def my_core():
    return (lax.axis_index(AXIS) >> 5) & 1


IN_VMEM = pl.BlockSpec(memory_space=pltpu.VMEM)
IN_SMEM = pl.BlockSpec(memory_space=pltpu.SMEM)


def params():
    return pltpu.CompilerParams(vmem_limit_bytes=VMEM_LIMIT)


def cost(flops, bytes_accessed):
    return pl.CostEstimate(flops=flops, bytes_accessed=bytes_accessed, transcendentals=0)


def begin(pairs, sems, first=0):
    copies = [
        pltpu.make_async_copy(source, target, sems.at[first + slot])
        for slot, (source, target) in enumerate(pairs)
    ]
    for copy in copies:
        copy.start()
    return copies


def finish(copies):
    for copy in copies:
        copy.wait()


def stack(cuts, refs, target):
    offset = 0
    for which, start, rows in cuts:
        target[offset : offset + rows, :] = refs[which][start : start + rows, :]
        offset += rows


def hold_kernel(text, features, log_scale, bias, text_held, features_held, scalars):
    text_held[...] = text[...]
    features_held[...] = features[...]
    scalars[0:1, :] = jnp.full((1, 128), log_scale[0], f32)
    scalars[1:2, :] = jnp.full((1, 128), bias[0], f32)


def held(*arrays):
    return pl.pallas_call(
        hold_kernel,
        in_specs=[IN_VMEM] * 2 + [IN_SMEM] * 2,
        out_specs=[IN_VMEM] * 3,
        out_shape=[jax.ShapeDtypeStruct((ROWS, WIDTH), bf16)] * 2 + [MARK],
        compiler_params=params(),
        cost_estimate=cost(HOLD, 0),
        name="hold",
    )(*arrays)


def normalize_kernel(own, opposite, next_1, next_3, low, high):
    for line, parts in ((low, (own, opposite)), (high, (next_1, next_3))):
        for slot, part in enumerate(parts):
            values = part[...].astype(f32)
            inverse = lax.rsqrt(jnp.sum(values * values, axis=1, keepdims=True) + epsilon)
            line[ROWS * slot : ROWS * slot + ROWS, :] = (values * inverse).astype(bf16)


def normalized(*parts):
    return pl.pallas_call(
        normalize_kernel,
        in_specs=[IN_VMEM] * 4,
        out_specs=[IN_VMEM] * 2,
        out_shape=[jax.ShapeDtypeStruct((HALF // 2, WIDTH), bf16)] * 2,
        compiler_params=params(),
        name="normalize_texts",
    )(*parts)


def join_kernel(own, opposite, next_1, next_3, low, high, joined, low_later, high_later):
    for slot, part in enumerate((own, opposite, next_1, next_3)):
        joined[ROWS * slot : ROWS * slot + ROWS, :] = part[...]
    low_later[...] = low[...]
    high_later[...] = high[...]


def joined(*parts):
    return pl.pallas_call(
        join_kernel,
        in_specs=[IN_VMEM] * 6,
        out_specs=[IN_VMEM] * 3,
        out_shape=[jax.ShapeDtypeStruct((HALF, WIDTH), bf16)]
        + [jax.ShapeDtypeStruct((HALF // 2, WIDTH), bf16)] * 2,
        compiler_params=params(),
        cost_estimate=cost(WORK, 0),
        name="join",
    )(*parts)


def pass_kernel(low, high, after, low_on, high_on):
    low_on[...] = low[...]
    high_on[...] = high[...]


def passed(*parts):
    return pl.pallas_call(
        pass_kernel,
        in_specs=[IN_VMEM] * 3,
        out_specs=[IN_VMEM] * 2,
        out_shape=[jax.ShapeDtypeStruct((HALF // 2, WIDTH), bf16)] * 2,
        compiler_params=params(),
        name="pass_on",
    )(*parts)


def project_kernel(images, proj, unit, unit_f, inverse, turned):
    emb = jnp.dot(images[...], proj[...], preferred_element_type=f32)
    inv = lax.rsqrt(jnp.sum(emb * emb, axis=1, keepdims=True) + epsilon)
    emb = emb * inv
    unit_f[...] = emb
    inverse[...] = jnp.broadcast_to(inv, inverse.shape)
    unit[...] = emb.astype(bf16)
    turned[...] = images[...].T


def projected(images, proj_w):
    return pl.pallas_call(
        project_kernel,
        in_specs=[IN_VMEM] * 2,
        out_specs=[IN_VMEM] * 4,
        out_shape=[
            jax.ShapeDtypeStruct((HALF, WIDTH), bf16),
            jax.ShapeDtypeStruct((HALF, WIDTH), f32),
            jax.ShapeDtypeStruct((HALF, 128), f32),
            jax.ShapeDtypeStruct((WIDTH, HALF), bf16),
        ],
        compiler_params=params(),
        cost_estimate=cost(PROJ, 0),
        name="project_images",
    )(images, proj_w)


def wave_body(cuts, texts, units, scalars, scratch, diagonal, take):
    text, sim, weights = scratch
    stack(cuts, texts, text)

    def similar(step):
        sim[HALF * step : HALF * step + HALF, :] = lax.dot_general(
            units[step][...], text[...], (((1,), (1,)), ((), ())), preferred_element_type=f32
        )

    similar(0)
    half = 0.5 * jnp.exp(scalars[0:1, 0:1])
    half_shift = 0.5 * scalars[1:2, 0:1]

    def weigh(step):
        rows = slice(HALF * step, HALF * step + HALF)
        weights[rows, :] = (half + half * jnp.tanh(half * sim[rows, :] + half_shift)).astype(bf16)

    weigh(0)
    if diagonal:
        tanh = jnp.tanh(half * sim[:ROWS, :256] + half_shift)
        row = lax.broadcasted_iota(jnp.int32, (ROWS, 256), 0)
        column = lax.broadcasted_iota(jnp.int32, (ROWS, 256), 1)
        pair = jnp.where(row == column, half * tanh - half, half + half * tanh)
        weights[:ROWS, :256] = pair.astype(bf16)
    for step in range(1, len(units)):
        similar(step)
        weigh(step)
    for step in range(len(units)):
        rows = slice(HALF * step, HALF * step + HALF)
        take(step, jnp.dot(weights[rows, :], text[...], preferred_element_type=f32))


def first_wave_kernel(cuts, count, *refs):
    scalars, texts, units = refs[0], refs[1 : count + 1], refs[count + 1 : count + 3]
    totals, mark, scratch = refs[count + 3 : count + 5], refs[count + 5], refs[count + 6 :]
    mark[...] = jnp.zeros(mark.shape, f32)

    def take(step, product):
        totals[step][...] = product

    wave_body(cuts, texts, units, scalars, scratch, True, take)


def next_wave_kernel(cuts, count, *refs):
    scalars, texts, units = refs[0], refs[1 : count + 1], refs[count + 1 : count + 3]
    before, totals, scratch = refs[count + 3 : count + 5], refs[count + 5 : count + 7], refs[count + 7 :]

    def take(step, product):
        totals[step][...] = before[step][...] + product

    wave_body(cuts, texts, units, scalars, scratch, False, take)


def last_wave_kernel(cuts, count, *refs):
    scalars, texts, units = refs[0], refs[1 : count + 1], refs[count + 1 : count + 2]
    before, unit_f, inverse, projected_f, projected_b = refs[count + 2 : count + 7]
    scratch = refs[count + 7 :]

    def take(step, product):
        gradient = before[...] + product
        image = unit_f[...]
        along = jnp.sum(image * gradient, axis=1, keepdims=True)
        projection = (gradient - image * along) * inverse[:, 0:1]
        projected_f[...] = projection
        projected_b[...] = projection.astype(bf16)

    wave_body(cuts, texts, units, scalars, scratch, False, take)


def wave(kernel, scalars, cuts, texts, units, extra, out_shape, aliases, name):
    rows = sum(cut[2] for cut in cuts)
    images = HALF * len(units)
    return pl.pallas_call(
        lambda *refs: kernel(cuts, len(texts), *refs),
        in_specs=[IN_VMEM] * (1 + len(texts) + len(units) + len(extra)),
        out_specs=[IN_VMEM] * len(out_shape),
        out_shape=out_shape,
        input_output_aliases=aliases,
        scratch_shapes=[
            pltpu.VMEM((rows, WIDTH), bf16),
            pltpu.VMEM((images, rows), f32),
            pltpu.VMEM((images, rows), bf16),
        ],
        compiler_params=params(),
        cost_estimate=cost(WAVES[name], 0),
        name=name,
    )(scalars, *texts, *units, *extra)


def terms(turned, projected_f, other):
    both = (projected_f[...] + other[...].astype(f32)).astype(bf16)
    core = my_core()
    return [
        jnp.dot(
            turned[pl.ds(pl.multiple_of(576 * high + 288 * core, 16), 288), :],
            both,
            preferred_element_type=f32,
        )
        for high in range(2)
    ]


def first_terms_kernel(turned, projected_f, other, out):
    for high, term in enumerate(terms(turned, projected_f, other)):
        out[288 * high : 288 * high + 288, :] = term


def first_terms(*parts):
    return pl.pallas_call(
        first_terms_kernel,
        in_specs=[IN_VMEM] * 3,
        out_specs=IN_VMEM,
        out_shape=jax.ShapeDtypeStruct((HALF, WIDTH), f32),
        compiler_params=params(),
        cost_estimate=cost(1000, 1000),
        name="first_terms",
    )(*parts)


def cut_terms_kernel(turned, projected_f, other, first, mine, two, one, three, total):
    for high, term in enumerate(terms(turned, projected_f, other)):
        rows = slice(288 * high, 288 * high + 288)
        for tile in range(9):
            lanes = slice(128 * tile, 128 * tile + 128)
            total[tile, rows, :] = first[rows, lanes] + term[:, lanes]
    index = lax.axis_index(AXIS)
    outs = ((0, mine), (2, two), (1, one), (3, three))

    @pl.when(my_core() == 0)
    def _():
        for steps, out in outs:
            first = 72 * (((index >> 3) + steps) & 3)
            for tile in range(9):
                for row in range(9):
                    parts = [
                        total[tile, pl.ds(288 * high + first + row, 8, stride=9), :]
                        for high in range(2)
                    ]
                    out[16 * row : 16 * row + 16, 128 * tile : 128 * tile + 128] = (
                        jnp.concatenate(parts).astype(out.dtype)
                    )

    @pl.when(my_core() == 1)
    def _():
        for steps, out in outs:
            first = 9 * ((index + steps) & 3)
            for tile in range(9):
                for row in range(9):
                    part = total[tile, pl.ds(first + row, 16, stride=36), :]
                    out[16 * row : 16 * row + 16, 128 * tile : 128 * tile + 128] = part.astype(
                        out.dtype
                    )


def cut_terms(*parts):
    return pl.pallas_call(
        cut_terms_kernel,
        in_specs=[IN_VMEM] * 4,
        out_specs=[IN_VMEM] * 4,
        out_shape=[jax.ShapeDtypeStruct((ROWS, WIDTH), f32)]
        + [jax.ShapeDtypeStruct((ROWS, WIDTH), bf16)] * 3,
        scratch_shapes=[pltpu.VMEM((9, HALF, 128), f32)],
        compiler_params=params(),
        name="cut_terms",
    )(*parts)


def ring_sum_kernel(mine, two, one, three, out, eights, ninth):
    ninth[...] = jnp.zeros(ninth.shape, f32)
    for tile in range(9):
        lanes = slice(128 * tile, 128 * tile + 128)
        value = mine[:, lanes]
        for part in (two, one, three):
            value = value + part[:, lanes].astype(f32)
        for row in range(8):
            eights[tile, pl.ds(row, 16, stride=8), :] = value[16 * row : 16 * row + 16]
        ninth[tile // 8, pl.ds(tile % 8, 16, stride=8), :] = value[128:]
        out[:, lanes] = eights[tile].astype(bf16)
    out[:, WIDTH : WIDTH + 128] = ninth[0].astype(bf16)
    out[:, WIDTH + 128 :] = ninth[1].astype(bf16)


def ring_sum(*parts):
    return pl.pallas_call(
        ring_sum_kernel,
        out_shape=jax.ShapeDtypeStruct((128, SLAB), bf16),
        scratch_shapes=[pltpu.VMEM((9, 128, 128), f32), pltpu.VMEM((2, 128, 128), f32)],
        compiler_params=params(),
        name="ring_sum",
    )(*parts)


def last_sum_kernel(pieces, out):
    total = jnp.zeros((16, SLAB), f32)
    for step in range(8):
        total = total + pieces[16 * step : 16 * step + 16, :].astype(f32)
    total = total[:8] + total[8:]
    out[:8, :] = total[:, :WIDTH]
    for tile in range(9):
        sublane, lane = tile % 8, WIDTH + 128 * (tile // 8)
        out[8:9, 128 * tile : 128 * tile + 128] = total[sublane : sublane + 1, lane : lane + 128]


def last_sum(pieces):
    return pl.pallas_call(
        last_sum_kernel,
        out_shape=jax.ShapeDtypeStruct((9, WIDTH), f32),
        compiler_params=params(),
        name="last_sum",
    )(pieces)


def ring(value, axis):
    return [send(value, axis(steps)) for steps in (2, 1, 3)]


def per_device(features, text_emb, proj_w, log_scale, bias):
    text, images, scalars = held(text_emb, features, log_scale, bias)
    low, high = normalized(text, *ring(text_emb, along_y_or_z))
    here, low_later, high_later = joined(images, *ring(features, along_x), low, high)
    there = send(here, other_core)
    low_1, high_3 = send(low, along_z_or_y(1)), send(high, along_z_or_y(3))
    high_1, low_3 = send(high_later, along_z_or_y(1)), send(low_later, along_z_or_y(3))
    units, units_f, inverses, turns = zip(
        projected(here, proj_w), projected(there, proj_w)
    )

    sums = [jax.ShapeDtypeStruct((HALF, WIDTH), f32)] * 2
    *totals, mark = wave(
        first_wave_kernel,
        scalars,
        ((0, 0, 288), (1, 0, 224)),
        (low, high),
        units,
        (),
        sums + [MARK],
        {},
        "first_wave",
    )
    low_on, high_on = passed(low_1, high_3, mark)
    low_2, high_2 = send(low_on, along_z_or_y(1)), send(high_on, along_z_or_y(3))
    totals = wave(
        next_wave_kernel,
        scalars,
        ((0, 224, 64), (1, 0, 288), (2, 0, 288), (3, 0, 288), (4, 0, 96)),
        (high, low_1, high_3, high_1, low_3),
        units,
        totals,
        sums,
        {8: 0, 9: 1},
        "second_wave",
    )
    own, sent = zip(
        *(
            wave(
                last_wave_kernel,
                scalars,
                ((0, 96, 192), (1, 0, 288), (2, 0, 288)),
                (low_3, low_2, high_2),
                units[half : half + 1],
                (totals[half], units_f[half], inverses[half]),
                [
                    jax.ShapeDtypeStruct((HALF, WIDTH), f32),
                    jax.ShapeDtypeStruct((HALF, WIDTH), bf16),
                ],
                {},
                "last_wave",
            )
            for half in range(2)
        )
    )
    got = [send(half, other_core) for half in sent]
    first = first_terms(turns[1], own[1], got[0])
    mine, two, one, three = cut_terms(turns[0], own[0], got[1], first)
    parts = [send(part, along_z_or_y(steps)) for part, steps in ((two, 2), (one, 1), (three, 3))]
    pieces = ring_sum(mine, *parts)
    pieces = lax.all_to_all(pieces, AXIS, 0, 0, axis_index_groups=LAST_GROUPS, tiled=True)
    return last_sum(pieces)


def solution(mesh):
    flat = Mesh(mesh.devices.reshape(-1), (AXIS,))
    rows = P(AXIS, None)
    return jax.shard_map(
        per_device,
        mesh=flat,
        in_specs=(rows, rows, P(), P(), P()),
        out_specs=rows,
        check_vma=False,
    )
```

```python
import jax
import jax.numpy as jnp
from jax import lax
from jax.experimental import pallas as pl
from jax.experimental.pallas import tpu as pltpu
from jax.sharding import Mesh, PartitionSpec as P

epsilon = 1e-06
bf16 = jnp.bfloat16
f32 = jnp.float32

AXIS = "d"
ROWS = 144
WIDTH = 1152
HALF = 4 * ROWS
IMAGES = 2 * HALF
TURNED = 512
SLAB = 1408
VMEM_LIMIT = 20 << 20
WORK = 12_000_000_000
PROJ = 20_000_000_000
W1 = 30_000_000_000
WAVES = {"first_wave": W1, "second_wave": 1000, "last_wave": 1000}
HOLD = 12_000_000_000
MARK = jax.ShapeDtypeStruct((8, 128), f32)


def place(index):
    y, xl, z = index & 3, (index >> 2) & 1, (index >> 3) & 3
    core, xh = (index >> 5) & 1, (index >> 6) & 1
    return 2 * xh + xl, y, z, core


def index_of(x, y, z, core):
    return (x >> 1) * 64 + core * 32 + z * 8 + (x & 1) * 4 + y


def send(value, target):
    pairs = [(source, index_of(*target(*place(source)))) for source in range(128)]
    return lax.ppermute(value, AXIS, pairs)


def along_x(steps):
    return lambda x, y, z, core: ((x + steps) % 4, y, z, core)


def along_y_or_z(steps):
    return lambda x, y, z, core: (
        (x, y, (z + steps) % 4, core) if core else (x, (y + steps) % 4, z, core)
    )


def along_z_or_y(steps):
    return lambda x, y, z, core: (
        (x, (y + steps) % 4, z, core) if core else (x, y, (z + steps) % 4, core)
    )


def other_core(x, y, z, core):
    return (x, y, z, 1 - core)


LAST_GROUPS = [
    [index_of(2 * xh + xl, y, z, 0) for xh in range(2) for xl in range(2) for y in range(4)]
    for z in range(4)
] + [
    [index_of(2 * xh + xl, y, z, 1) for xh in range(2) for z in range(4) for xl in range(2)]
    for y in range(4)
]


def my_core():
    return (lax.axis_index(AXIS) >> 5) & 1


IN_VMEM = pl.BlockSpec(memory_space=pltpu.VMEM)
IN_SMEM = pl.BlockSpec(memory_space=pltpu.SMEM)


def params():
    return pltpu.CompilerParams(vmem_limit_bytes=VMEM_LIMIT)


def cost(flops, bytes_accessed):
    return pl.CostEstimate(flops=flops, bytes_accessed=bytes_accessed, transcendentals=0)


def begin(pairs, sems, first=0):
    copies = [
        pltpu.make_async_copy(source, target, sems.at[first + slot])
        for slot, (source, target) in enumerate(pairs)
    ]
    for copy in copies:
        copy.start()
    return copies


def finish(copies):
    for copy in copies:
        copy.wait()


def stack(cuts, refs, target):
    offset = 0
    for which, start, rows in cuts:
        target[offset : offset + rows, :] = refs[which][start : start + rows, :]
        offset += rows


def hold_kernel(text, features, log_scale, bias, text_held, features_held, scalars):
    text_held[...] = text[...]
    features_held[...] = features[...]
    scalars[0:1, :] = jnp.full((1, 128), log_scale[0], f32)
    scalars[1:2, :] = jnp.full((1, 128), bias[0], f32)


def held(*arrays):
    return pl.pallas_call(
        hold_kernel,
        in_specs=[IN_VMEM] * 2 + [IN_SMEM] * 2,
        out_specs=[IN_VMEM] * 3,
        out_shape=[jax.ShapeDtypeStruct((ROWS, WIDTH), bf16)] * 2 + [MARK],
        compiler_params=params(),
        cost_estimate=cost(HOLD, 0),
        name="hold",
    )(*arrays)


def normalize_kernel(own, opposite, next_1, next_3, low, high):
    for line, parts in ((low, (own, opposite)), (high, (next_1, next_3))):
        for slot, part in enumerate(parts):
            values = part[...].astype(f32)
            inverse = lax.rsqrt(jnp.sum(values * values, axis=1, keepdims=True) + epsilon)
            line[ROWS * slot : ROWS * slot + ROWS, :] = (values * inverse).astype(bf16)


def normalized(*parts):
    return pl.pallas_call(
        normalize_kernel,
        in_specs=[IN_VMEM] * 4,
        out_specs=[IN_VMEM] * 2,
        out_shape=[jax.ShapeDtypeStruct((HALF // 2, WIDTH), bf16)] * 2,
        compiler_params=params(),
        name="normalize_texts",
    )(*parts)


def join_kernel(own, opposite, next_1, next_3, low, high, joined, low_later, high_later):
    for slot, part in enumerate((own, opposite, next_1, next_3)):
        joined[ROWS * slot : ROWS * slot + ROWS, :] = part[...]
    low_later[...] = low[...]
    high_later[...] = high[...]


def joined(*parts):
    return pl.pallas_call(
        join_kernel,
        in_specs=[IN_VMEM] * 6,
        out_specs=[IN_VMEM] * 3,
        out_shape=[jax.ShapeDtypeStruct((HALF, WIDTH), bf16)]
        + [jax.ShapeDtypeStruct((HALF // 2, WIDTH), bf16)] * 2,
        compiler_params=params(),
        cost_estimate=cost(WORK, 0),
        name="join",
    )(*parts)


def pass_kernel(low, high, after, low_on, high_on):
    low_on[...] = low[...]
    high_on[...] = high[...]


def passed(*parts):
    return pl.pallas_call(
        pass_kernel,
        in_specs=[IN_VMEM] * 3,
        out_specs=[IN_VMEM] * 2,
        out_shape=[jax.ShapeDtypeStruct((HALF // 2, WIDTH), bf16)] * 2,
        compiler_params=params(),
        name="pass_on",
    )(*parts)


def project_kernel(images, proj, unit, unit_f, inverse, turned, mark):
    mark[...] = jnp.zeros(mark.shape, f32)
    emb = jnp.dot(images[...], proj[...], preferred_element_type=f32)
    inv = lax.rsqrt(jnp.sum(emb * emb, axis=1, keepdims=True) + epsilon)
    emb = emb * inv
    unit_f[...] = emb
    inverse[...] = jnp.broadcast_to(inv, inverse.shape)
    unit[...] = emb.astype(bf16)
    turned[...] = images[...].T


def projected(images, proj_w):
    return pl.pallas_call(
        project_kernel,
        in_specs=[IN_VMEM] * 2,
        out_specs=[IN_VMEM] * 5,
        out_shape=[
            jax.ShapeDtypeStruct((HALF, WIDTH), bf16),
            jax.ShapeDtypeStruct((HALF, WIDTH), f32),
            jax.ShapeDtypeStruct((HALF, 128), f32),
            jax.ShapeDtypeStruct((WIDTH, HALF), bf16),
            MARK,
        ],
        compiler_params=params(),
        cost_estimate=cost(PROJ, 0),
        name="project_images",
    )(images, proj_w)


def wave_body(cuts, texts, units, scalars, scratch, diagonal, take):
    text, sim, weights = scratch
    stack(cuts, texts, text)

    def similar(step):
        sim[HALF * step : HALF * step + HALF, :] = lax.dot_general(
            units[step][...], text[...], (((1,), (1,)), ((), ())), preferred_element_type=f32
        )

    similar(0)
    half = 0.5 * jnp.exp(scalars[0:1, 0:1])
    half_shift = 0.5 * scalars[1:2, 0:1]

    def weigh(step):
        rows = slice(HALF * step, HALF * step + HALF)
        weights[rows, :] = (half + half * jnp.tanh(half * sim[rows, :] + half_shift)).astype(bf16)

    weigh(0)
    if diagonal:
        tanh = jnp.tanh(half * sim[:ROWS, :256] + half_shift)
        row = lax.broadcasted_iota(jnp.int32, (ROWS, 256), 0)
        column = lax.broadcasted_iota(jnp.int32, (ROWS, 256), 1)
        pair = jnp.where(row == column, half * tanh - half, half + half * tanh)
        weights[:ROWS, :256] = pair.astype(bf16)
    for step in range(1, len(units)):
        similar(step)
        weigh(step)
    for step in range(len(units)):
        rows = slice(HALF * step, HALF * step + HALF)
        take(step, jnp.dot(weights[rows, :], text[...], preferred_element_type=f32))


def first_wave_kernel(cuts, count, *refs):
    scalars, texts, units = refs[0], refs[1 : count + 1], refs[count + 1 : count + 3]
    totals, scratch = refs[count + 3 : count + 5], refs[count + 5 :]

    def take(step, product):
        totals[step][...] = product

    wave_body(cuts, texts, units, scalars, scratch, True, take)


def next_wave_kernel(cuts, count, *refs):
    scalars, texts, units = refs[0], refs[1 : count + 1], refs[count + 1 : count + 3]
    before, totals, scratch = refs[count + 3 : count + 5], refs[count + 5 : count + 7], refs[count + 7 :]

    def take(step, product):
        totals[step][...] = before[step][...] + product

    wave_body(cuts, texts, units, scalars, scratch, False, take)


def last_wave_kernel(cuts, count, *refs):
    scalars, texts, units = refs[0], refs[1 : count + 1], refs[count + 1 : count + 2]
    before, unit_f, inverse, projected_f, projected_b = refs[count + 2 : count + 7]
    scratch = refs[count + 7 :]

    def take(step, product):
        gradient = before[...] + product
        image = unit_f[...]
        along = jnp.sum(image * gradient, axis=1, keepdims=True)
        projection = (gradient - image * along) * inverse[:, 0:1]
        projected_f[...] = projection
        projected_b[...] = projection.astype(bf16)

    wave_body(cuts, texts, units, scalars, scratch, False, take)


def wave(kernel, scalars, cuts, texts, units, extra, out_shape, aliases, name):
    rows = sum(cut[2] for cut in cuts)
    images = HALF * len(units)
    return pl.pallas_call(
        lambda *refs: kernel(cuts, len(texts), *refs),
        in_specs=[IN_VMEM] * (1 + len(texts) + len(units) + len(extra)),
        out_specs=[IN_VMEM] * len(out_shape),
        out_shape=out_shape,
        input_output_aliases=aliases,
        scratch_shapes=[
            pltpu.VMEM((rows, WIDTH), bf16),
            pltpu.VMEM((images, rows), f32),
            pltpu.VMEM((images, rows), bf16),
        ],
        compiler_params=params(),
        cost_estimate=cost(WAVES[name], 0),
        name=name,
    )(scalars, *texts, *units, *extra)


def terms(turned, projected_f, other):
    both = (projected_f[...] + other[...].astype(f32)).astype(bf16)
    core = my_core()
    return [
        jnp.dot(
            turned[pl.ds(pl.multiple_of(576 * high + 288 * core, 16), 288), :],
            both,
            preferred_element_type=f32,
        )
        for high in range(2)
    ]


def first_terms_kernel(turned, projected_f, other, out):
    for high, term in enumerate(terms(turned, projected_f, other)):
        out[288 * high : 288 * high + 288, :] = term


def first_terms(*parts):
    return pl.pallas_call(
        first_terms_kernel,
        in_specs=[IN_VMEM] * 3,
        out_specs=IN_VMEM,
        out_shape=jax.ShapeDtypeStruct((HALF, WIDTH), f32),
        compiler_params=params(),
        cost_estimate=cost(1000, 1000),
        name="first_terms",
    )(*parts)


def cut_terms_kernel(turned, projected_f, other, first, mine, two, one, three, total):
    for high, term in enumerate(terms(turned, projected_f, other)):
        rows = slice(288 * high, 288 * high + 288)
        for tile in range(9):
            lanes = slice(128 * tile, 128 * tile + 128)
            total[tile, rows, :] = first[rows, lanes] + term[:, lanes]
    index = lax.axis_index(AXIS)
    outs = ((0, mine), (2, two), (1, one), (3, three))

    @pl.when(my_core() == 0)
    def _():
        for steps, out in outs:
            first = 72 * (((index >> 3) + steps) & 3)
            for tile in range(9):
                for row in range(9):
                    parts = [
                        total[tile, pl.ds(288 * high + first + row, 8, stride=9), :]
                        for high in range(2)
                    ]
                    out[16 * row : 16 * row + 16, 128 * tile : 128 * tile + 128] = (
                        jnp.concatenate(parts).astype(out.dtype)
                    )

    @pl.when(my_core() == 1)
    def _():
        for steps, out in outs:
            first = 9 * ((index + steps) & 3)
            for tile in range(9):
                for row in range(9):
                    part = total[tile, pl.ds(first + row, 16, stride=36), :]
                    out[16 * row : 16 * row + 16, 128 * tile : 128 * tile + 128] = part.astype(
                        out.dtype
                    )


def cut_terms(*parts):
    return pl.pallas_call(
        cut_terms_kernel,
        in_specs=[IN_VMEM] * 4,
        out_specs=[IN_VMEM] * 4,
        out_shape=[jax.ShapeDtypeStruct((ROWS, WIDTH), f32)]
        + [jax.ShapeDtypeStruct((ROWS, WIDTH), bf16)] * 3,
        scratch_shapes=[pltpu.VMEM((9, HALF, 128), f32)],
        compiler_params=params(),
        name="cut_terms",
    )(*parts)


def ring_sum_kernel(mine, two, one, three, out, eights, ninth):
    ninth[...] = jnp.zeros(ninth.shape, f32)
    for tile in range(9):
        lanes = slice(128 * tile, 128 * tile + 128)
        value = mine[:, lanes]
        for part in (two, one, three):
            value = value + part[:, lanes].astype(f32)
        for row in range(8):
            eights[tile, pl.ds(row, 16, stride=8), :] = value[16 * row : 16 * row + 16]
        ninth[tile // 8, pl.ds(tile % 8, 16, stride=8), :] = value[128:]
        out[:, lanes] = eights[tile].astype(bf16)
    out[:, WIDTH : WIDTH + 128] = ninth[0].astype(bf16)
    out[:, WIDTH + 128 :] = ninth[1].astype(bf16)


def ring_sum(*parts):
    return pl.pallas_call(
        ring_sum_kernel,
        out_shape=jax.ShapeDtypeStruct((128, SLAB), bf16),
        scratch_shapes=[pltpu.VMEM((9, 128, 128), f32), pltpu.VMEM((2, 128, 128), f32)],
        compiler_params=params(),
        name="ring_sum",
    )(*parts)


def last_sum_kernel(pieces, out):
    total = jnp.zeros((16, SLAB), f32)
    for step in range(8):
        total = total + pieces[16 * step : 16 * step + 16, :].astype(f32)
    total = total[:8] + total[8:]
    out[:8, :] = total[:, :WIDTH]
    for tile in range(9):
        sublane, lane = tile % 8, WIDTH + 128 * (tile // 8)
        out[8:9, 128 * tile : 128 * tile + 128] = total[sublane : sublane + 1, lane : lane + 128]


def last_sum(pieces):
    return pl.pallas_call(
        last_sum_kernel,
        out_shape=jax.ShapeDtypeStruct((9, WIDTH), f32),
        compiler_params=params(),
        name="last_sum",
    )(pieces)


def ring(value, axis):
    return [send(value, axis(steps)) for steps in (2, 1, 3)]


def per_device(features, text_emb, proj_w, log_scale, bias):
    text, images, scalars = held(text_emb, features, log_scale, bias)
    low, high = normalized(text, *ring(text_emb, along_y_or_z))
    here, low_later, high_later = joined(images, *ring(features, along_x), low, high)
    there = send(here, other_core)
    low_1, high_3 = send(low, along_z_or_y(1)), send(high, along_z_or_y(3))
    high_1, low_3 = send(high_later, along_z_or_y(1)), send(low_later, along_z_or_y(3))
    units, units_f, inverses, turns, marks = zip(
        projected(here, proj_w), projected(there, proj_w)
    )
    low_on, high_on = passed(low_1, high_3, marks[0])
    low_2, high_2 = send(low_on, along_z_or_y(1)), send(high_on, along_z_or_y(3))

    sums = [jax.ShapeDtypeStruct((HALF, WIDTH), f32)] * 2
    totals = wave(
        first_wave_kernel,
        scalars,
        ((0, 0, 288), (1, 0, 224)),
        (low, high),
        units,
        (),
        sums,
        {},
        "first_wave",
    )
    totals = wave(
        next_wave_kernel,
        scalars,
        ((0, 224, 64), (1, 0, 288), (2, 0, 288), (3, 0, 288), (4, 0, 96)),
        (high, low_1, high_3, high_1, low_3),
        units,
        totals,
        sums,
        {8: 0, 9: 1},
        "second_wave",
    )
    own, sent = zip(
        *(
            wave(
                last_wave_kernel,
                scalars,
                ((0, 96, 192), (1, 0, 288), (2, 0, 288)),
                (low_3, low_2, high_2),
                units[half : half + 1],
                (totals[half], units_f[half], inverses[half]),
                [
                    jax.ShapeDtypeStruct((HALF, WIDTH), f32),
                    jax.ShapeDtypeStruct((HALF, WIDTH), bf16),
                ],
                {},
                "last_wave",
            )
            for half in range(2)
        )
    )
    got = [send(half, other_core) for half in sent]
    first = first_terms(turns[1], own[1], got[0])
    mine, two, one, three = cut_terms(turns[0], own[0], got[1], first)
    parts = [send(part, along_z_or_y(steps)) for part, steps in ((two, 2), (one, 1), (three, 3))]
    pieces = ring_sum(mine, *parts)
    pieces = lax.all_to_all(pieces, AXIS, 0, 0, axis_index_groups=LAST_GROUPS, tiled=True)
    return last_sum(pieces)


def solution(mesh):
    flat = Mesh(mesh.devices.reshape(-1), (AXIS,))
    rows = P(AXIS, None)
    return jax.shard_map(
        per_device,
        mesh=flat,
        in_specs=(rows, rows, P(), P(), P()),
        out_specs=rows,
        check_vma=False,
    )
```

```python
import jax
import jax.numpy as jnp
from jax import lax
from jax.experimental import pallas as pl
from jax.experimental.pallas import tpu as pltpu
from jax.sharding import Mesh, PartitionSpec as P

epsilon = 1e-06
bf16 = jnp.bfloat16
f32 = jnp.float32

AXIS = "d"
ROWS = 144
WIDTH = 1152
HALF = 4 * ROWS
IMAGES = 2 * HALF
TURNED = 512
SLAB = 1408
VMEM_LIMIT = 20 << 20
WORK = 12_000_000_000
PROJ = 20_000_000_000
W1 = 30_000_000_000
WAVES = {"first_wave": W1, "second_wave": 1000, "last_wave": 1000}
HOLD = 12_000_000_000
MARK = jax.ShapeDtypeStruct((8, 128), f32)


def place(index):
    y, xl, z = index & 3, (index >> 2) & 1, (index >> 3) & 3
    core, xh = (index >> 5) & 1, (index >> 6) & 1
    return 2 * xh + xl, y, z, core


def index_of(x, y, z, core):
    return (x >> 1) * 64 + core * 32 + z * 8 + (x & 1) * 4 + y


def send(value, target):
    pairs = [(source, index_of(*target(*place(source)))) for source in range(128)]
    return lax.ppermute(value, AXIS, pairs)


def along_x(steps):
    return lambda x, y, z, core: ((x + steps) % 4, y, z, core)


def along_y_or_z(steps):
    return lambda x, y, z, core: (
        (x, y, (z + steps) % 4, core) if core else (x, (y + steps) % 4, z, core)
    )


def along_z_or_y(steps):
    return lambda x, y, z, core: (
        (x, (y + steps) % 4, z, core) if core else (x, y, (z + steps) % 4, core)
    )


def other_core(x, y, z, core):
    return (x, y, z, 1 - core)


LAST_GROUPS = [
    [index_of(2 * xh + xl, y, z, 0) for xh in range(2) for xl in range(2) for y in range(4)]
    for z in range(4)
] + [
    [index_of(2 * xh + xl, y, z, 1) for xh in range(2) for z in range(4) for xl in range(2)]
    for y in range(4)
]


def my_core():
    return (lax.axis_index(AXIS) >> 5) & 1


IN_VMEM = pl.BlockSpec(memory_space=pltpu.VMEM)
IN_SMEM = pl.BlockSpec(memory_space=pltpu.SMEM)


def params():
    return pltpu.CompilerParams(vmem_limit_bytes=VMEM_LIMIT)


def cost(flops, bytes_accessed):
    return pl.CostEstimate(flops=flops, bytes_accessed=bytes_accessed, transcendentals=0)


def begin(pairs, sems, first=0):
    copies = [
        pltpu.make_async_copy(source, target, sems.at[first + slot])
        for slot, (source, target) in enumerate(pairs)
    ]
    for copy in copies:
        copy.start()
    return copies


def finish(copies):
    for copy in copies:
        copy.wait()


def stack(cuts, refs, target):
    offset = 0
    for which, start, rows in cuts:
        target[offset : offset + rows, :] = refs[which][start : start + rows, :]
        offset += rows


def hold_kernel(text, features, log_scale, bias, text_held, features_held, scalars):
    text_held[...] = text[...]
    features_held[...] = features[...]
    scalars[0:1, :] = jnp.full((1, 128), log_scale[0], f32)
    scalars[1:2, :] = jnp.full((1, 128), bias[0], f32)


def held(*arrays):
    return pl.pallas_call(
        hold_kernel,
        in_specs=[IN_VMEM] * 2 + [IN_SMEM] * 2,
        out_specs=[IN_VMEM] * 3,
        out_shape=[jax.ShapeDtypeStruct((ROWS, WIDTH), bf16)] * 2 + [MARK],
        compiler_params=params(),
        cost_estimate=cost(HOLD, 0),
        name="hold",
    )(*arrays)


def normalize_kernel(own, opposite, next_1, next_3, after, low, high):
    for line, parts in ((low, (own, opposite)), (high, (next_1, next_3))):
        for slot, part in enumerate(parts):
            values = part[...].astype(f32)
            inverse = lax.rsqrt(jnp.sum(values * values, axis=1, keepdims=True) + epsilon)
            line[ROWS * slot : ROWS * slot + ROWS, :] = (values * inverse).astype(bf16)


def normalized(*parts):
    return pl.pallas_call(
        normalize_kernel,
        in_specs=[IN_VMEM] * 5,
        out_specs=[IN_VMEM] * 2,
        out_shape=[jax.ShapeDtypeStruct((HALF // 2, WIDTH), bf16)] * 2,
        compiler_params=params(),
        name="normalize_texts",
    )(*parts)


def join_kernel(own, opposite, next_1, next_3, joined):
    for slot, part in enumerate((own, opposite, next_1, next_3)):
        joined[ROWS * slot : ROWS * slot + ROWS, :] = part[...]


def joined(*parts):
    return pl.pallas_call(
        join_kernel,
        in_specs=[IN_VMEM] * 4,
        out_specs=IN_VMEM,
        out_shape=jax.ShapeDtypeStruct((HALF, WIDTH), bf16),
        compiler_params=params(),
        cost_estimate=cost(WORK, 0),
        name="join",
    )(*parts)


def pass_kernel(low, high, after, low_on, high_on):
    low_on[...] = low[...]
    high_on[...] = high[...]


def passed(*parts):
    return pl.pallas_call(
        pass_kernel,
        in_specs=[IN_VMEM] * 3,
        out_specs=[IN_VMEM] * 2,
        out_shape=[jax.ShapeDtypeStruct((HALF // 2, WIDTH), bf16)] * 2,
        compiler_params=params(),
        name="pass_on",
    )(*parts)


def project_kernel(images, proj, *refs):
    count = (len(refs) - 5) // 2
    unit, unit_f, inverse, turned, mark = refs[count : count + 5]
    emb = jnp.dot(images[...], proj[...], preferred_element_type=f32)
    inv = lax.rsqrt(jnp.sum(emb * emb, axis=1, keepdims=True) + epsilon)
    emb = emb * inv
    unit_f[...] = emb
    inverse[...] = jnp.broadcast_to(inv, inverse.shape)
    unit[...] = emb.astype(bf16)
    turned[...] = images[...].T
    mark[...] = jnp.zeros(mark.shape, f32)
    for later, now in zip(refs[count + 5 :], refs[:count]):
        later[...] = now[...]


def projected(images, proj_w, *later):
    return pl.pallas_call(
        project_kernel,
        in_specs=[IN_VMEM] * (2 + len(later)),
        out_specs=[IN_VMEM] * (5 + len(later)),
        out_shape=[
            jax.ShapeDtypeStruct((HALF, WIDTH), bf16),
            jax.ShapeDtypeStruct((HALF, WIDTH), f32),
            jax.ShapeDtypeStruct((HALF, 128), f32),
            jax.ShapeDtypeStruct((WIDTH, HALF), bf16),
            MARK,
        ]
        + [jax.ShapeDtypeStruct(part.shape, part.dtype) for part in later],
        compiler_params=params(),
        cost_estimate=cost(PROJ, 0),
        name="project_images",
    )(images, proj_w, *later)


def wave_body(cuts, texts, units, scalars, scratch, diagonal, take):
    text, sim, weights = scratch
    stack(cuts, texts, text)

    def similar(step):
        sim[HALF * step : HALF * step + HALF, :] = lax.dot_general(
            units[step][...], text[...], (((1,), (1,)), ((), ())), preferred_element_type=f32
        )

    similar(0)
    half = 0.5 * jnp.exp(scalars[0:1, 0:1])
    half_shift = 0.5 * scalars[1:2, 0:1]

    def weigh(step):
        rows = slice(HALF * step, HALF * step + HALF)
        weights[rows, :] = (half + half * jnp.tanh(half * sim[rows, :] + half_shift)).astype(bf16)

    weigh(0)
    if diagonal:
        tanh = jnp.tanh(half * sim[:ROWS, :256] + half_shift)
        row = lax.broadcasted_iota(jnp.int32, (ROWS, 256), 0)
        column = lax.broadcasted_iota(jnp.int32, (ROWS, 256), 1)
        pair = jnp.where(row == column, half * tanh - half, half + half * tanh)
        weights[:ROWS, :256] = pair.astype(bf16)
    for step in range(1, len(units)):
        similar(step)
        weigh(step)
    for step in range(len(units)):
        rows = slice(HALF * step, HALF * step + HALF)
        take(step, jnp.dot(weights[rows, :], text[...], preferred_element_type=f32))


def first_wave_kernel(cuts, count, *refs):
    scalars, texts, units = refs[0], refs[1 : count + 1], refs[count + 1 : count + 3]
    totals, mark, scratch = refs[count + 3 : count + 5], refs[count + 5], refs[count + 6 :]
    mark[...] = jnp.zeros(mark.shape, f32)

    def take(step, product):
        totals[step][...] = product

    wave_body(cuts, texts, units, scalars, scratch, True, take)


def next_wave_kernel(cuts, count, *refs):
    scalars, texts, units = refs[0], refs[1 : count + 1], refs[count + 1 : count + 3]
    before, totals, scratch = refs[count + 3 : count + 5], refs[count + 5 : count + 7], refs[count + 7 :]

    def take(step, product):
        totals[step][...] = before[step][...] + product

    wave_body(cuts, texts, units, scalars, scratch, False, take)


def last_wave_kernel(cuts, count, *refs):
    scalars, texts, units = refs[0], refs[1 : count + 1], refs[count + 1 : count + 2]
    before, unit_f, inverse, projected_f, projected_b = refs[count + 2 : count + 7]
    scratch = refs[count + 7 :]

    def take(step, product):
        gradient = before[...] + product
        image = unit_f[...]
        along = jnp.sum(image * gradient, axis=1, keepdims=True)
        projection = (gradient - image * along) * inverse[:, 0:1]
        projected_f[...] = projection
        projected_b[...] = projection.astype(bf16)

    wave_body(cuts, texts, units, scalars, scratch, False, take)


def wave(kernel, scalars, cuts, texts, units, extra, out_shape, aliases, name):
    rows = sum(cut[2] for cut in cuts)
    images = HALF * len(units)
    return pl.pallas_call(
        lambda *refs: kernel(cuts, len(texts), *refs),
        in_specs=[IN_VMEM] * (1 + len(texts) + len(units) + len(extra)),
        out_specs=[IN_VMEM] * len(out_shape),
        out_shape=out_shape,
        input_output_aliases=aliases,
        scratch_shapes=[
            pltpu.VMEM((rows, WIDTH), bf16),
            pltpu.VMEM((images, rows), f32),
            pltpu.VMEM((images, rows), bf16),
        ],
        compiler_params=params(),
        cost_estimate=cost(WAVES[name], 0),
        name=name,
    )(scalars, *texts, *units, *extra)


def terms(turned, projected_f, other):
    both = (projected_f[...] + other[...].astype(f32)).astype(bf16)
    core = my_core()
    return [
        jnp.dot(
            turned[pl.ds(pl.multiple_of(576 * high + 288 * core, 16), 288), :],
            both,
            preferred_element_type=f32,
        )
        for high in range(2)
    ]


def first_terms_kernel(turned, projected_f, other, out):
    for high, term in enumerate(terms(turned, projected_f, other)):
        out[288 * high : 288 * high + 288, :] = term


def first_terms(*parts):
    return pl.pallas_call(
        first_terms_kernel,
        in_specs=[IN_VMEM] * 3,
        out_specs=IN_VMEM,
        out_shape=jax.ShapeDtypeStruct((HALF, WIDTH), f32),
        compiler_params=params(),
        cost_estimate=cost(1000, 1000),
        name="first_terms",
    )(*parts)


def cut_terms_kernel(turned, projected_f, other, first, mine, two, one, three, total):
    for high, term in enumerate(terms(turned, projected_f, other)):
        rows = slice(288 * high, 288 * high + 288)
        for tile in range(9):
            lanes = slice(128 * tile, 128 * tile + 128)
            total[tile, rows, :] = first[rows, lanes] + term[:, lanes]
    index = lax.axis_index(AXIS)
    outs = ((0, mine), (2, two), (1, one), (3, three))

    @pl.when(my_core() == 0)
    def _():
        for steps, out in outs:
            first = 72 * (((index >> 3) + steps) & 3)
            for tile in range(9):
                for row in range(9):
                    parts = [
                        total[tile, pl.ds(288 * high + first + row, 8, stride=9), :]
                        for high in range(2)
                    ]
                    out[16 * row : 16 * row + 16, 128 * tile : 128 * tile + 128] = (
                        jnp.concatenate(parts).astype(out.dtype)
                    )

    @pl.when(my_core() == 1)
    def _():
        for steps, out in outs:
            first = 9 * ((index + steps) & 3)
            for tile in range(9):
                for row in range(9):
                    part = total[tile, pl.ds(first + row, 16, stride=36), :]
                    out[16 * row : 16 * row + 16, 128 * tile : 128 * tile + 128] = part.astype(
                        out.dtype
                    )


def cut_terms(*parts):
    return pl.pallas_call(
        cut_terms_kernel,
        in_specs=[IN_VMEM] * 4,
        out_specs=[IN_VMEM] * 4,
        out_shape=[jax.ShapeDtypeStruct((ROWS, WIDTH), f32)]
        + [jax.ShapeDtypeStruct((ROWS, WIDTH), bf16)] * 3,
        scratch_shapes=[pltpu.VMEM((9, HALF, 128), f32)],
        compiler_params=params(),
        name="cut_terms",
    )(*parts)


def ring_sum_kernel(mine, two, one, three, out, eights, ninth):
    ninth[...] = jnp.zeros(ninth.shape, f32)
    for tile in range(9):
        lanes = slice(128 * tile, 128 * tile + 128)
        value = mine[:, lanes]
        for part in (two, one, three):
            value = value + part[:, lanes].astype(f32)
        for row in range(8):
            eights[tile, pl.ds(row, 16, stride=8), :] = value[16 * row : 16 * row + 16]
        ninth[tile // 8, pl.ds(tile % 8, 16, stride=8), :] = value[128:]
        out[:, lanes] = eights[tile].astype(bf16)
    out[:, WIDTH : WIDTH + 128] = ninth[0].astype(bf16)
    out[:, WIDTH + 128 :] = ninth[1].astype(bf16)


def ring_sum(*parts):
    return pl.pallas_call(
        ring_sum_kernel,
        out_shape=jax.ShapeDtypeStruct((128, SLAB), bf16),
        scratch_shapes=[pltpu.VMEM((9, 128, 128), f32), pltpu.VMEM((2, 128, 128), f32)],
        compiler_params=params(),
        name="ring_sum",
    )(*parts)


def last_sum_kernel(pieces, out):
    total = jnp.zeros((16, SLAB), f32)
    for step in range(8):
        total = total + pieces[16 * step : 16 * step + 16, :].astype(f32)
    total = total[:8] + total[8:]
    out[:8, :] = total[:, :WIDTH]
    for tile in range(9):
        sublane, lane = tile % 8, WIDTH + 128 * (tile // 8)
        out[8:9, 128 * tile : 128 * tile + 128] = total[sublane : sublane + 1, lane : lane + 128]


def last_sum(pieces):
    return pl.pallas_call(
        last_sum_kernel,
        out_shape=jax.ShapeDtypeStruct((9, WIDTH), f32),
        compiler_params=params(),
        name="last_sum",
    )(pieces)


def ring(value, axis):
    return [send(value, axis(steps)) for steps in (2, 1, 3)]


def per_device(features, text_emb, proj_w, log_scale, bias):
    text, images, scalars = held(text_emb, features, log_scale, bias)
    here = joined(images, *ring(features, along_x))
    there = send(here, other_core)
    *here, mark = projected(here, proj_w)
    low, high = normalized(text, *ring(text_emb, along_y_or_z), mark)
    low_1, high_3 = send(low, along_z_or_y(1)), send(high, along_z_or_y(3))
    *there, _, low_later, high_later = projected(there, proj_w, low, high)
    high_1, low_3 = send(high_later, along_z_or_y(1)), send(low_later, along_z_or_y(3))
    units, units_f, inverses, turns = zip(here, there)

    sums = [jax.ShapeDtypeStruct((HALF, WIDTH), f32)] * 2
    *totals, mark = wave(
        first_wave_kernel,
        scalars,
        ((0, 0, 288), (1, 0, 224)),
        (low, high),
        units,
        (),
        sums + [MARK],
        {},
        "first_wave",
    )
    low_on, high_on = passed(low_1, high_3, mark)
    low_2, high_2 = send(low_on, along_z_or_y(1)), send(high_on, along_z_or_y(3))
    totals = wave(
        next_wave_kernel,
        scalars,
        ((0, 224, 64), (1, 0, 288), (2, 0, 288), (3, 0, 288), (4, 0, 96)),
        (high, low_1, high_3, high_1, low_3),
        units,
        totals,
        sums,
        {8: 0, 9: 1},
        "second_wave",
    )
    own, sent = zip(
        *(
            wave(
                last_wave_kernel,
                scalars,
                ((0, 96, 192), (1, 0, 288), (2, 0, 288)),
                (low_3, low_2, high_2),
                units[half : half + 1],
                (totals[half], units_f[half], inverses[half]),
                [
                    jax.ShapeDtypeStruct((HALF, WIDTH), f32),
                    jax.ShapeDtypeStruct((HALF, WIDTH), bf16),
                ],
                {},
                "last_wave",
            )
            for half in range(2)
        )
    )
    got = [send(half, other_core) for half in sent]
    first = first_terms(turns[1], own[1], got[0])
    mine, two, one, three = cut_terms(turns[0], own[0], got[1], first)
    parts = [send(part, along_z_or_y(steps)) for part, steps in ((two, 2), (one, 1), (three, 3))]
    pieces = ring_sum(mine, *parts)
    pieces = lax.all_to_all(pieces, AXIS, 0, 0, axis_index_groups=LAST_GROUPS, tiled=True)
    return last_sum(pieces)


def solution(mesh):
    flat = Mesh(mesh.devices.reshape(-1), (AXIS,))
    rows = P(AXIS, None)
    return jax.shard_map(
        per_device,
        mesh=flat,
        in_specs=(rows, rows, P(), P(), P()),
        out_specs=rows,
        check_vma=False,
    )
```

```python
import jax
import jax.numpy as jnp
from jax import lax
from jax.experimental import pallas as pl
from jax.experimental.pallas import tpu as pltpu
from jax.sharding import Mesh, PartitionSpec as P

epsilon = 1e-06
bf16 = jnp.bfloat16
f32 = jnp.float32

AXIS = "d"
ROWS = 144
WIDTH = 1152
HALF = 4 * ROWS
IMAGES = 2 * HALF
TURNED = 512
SLAB = 1408
VMEM_LIMIT = 20 << 20
WORK = 12_000_000_000
PROJ = 20_000_000_000
W1 = 30_000_000_000
WAVES = {"first_wave": W1, "second_wave": 1000, "last_wave": 1000}
HOLD = 1000
MARK = jax.ShapeDtypeStruct((8, 128), f32)


def place(index):
    y, xl, z = index & 3, (index >> 2) & 1, (index >> 3) & 3
    core, xh = (index >> 5) & 1, (index >> 6) & 1
    return 2 * xh + xl, y, z, core


def index_of(x, y, z, core):
    return (x >> 1) * 64 + core * 32 + z * 8 + (x & 1) * 4 + y


def send(value, target):
    pairs = [(source, index_of(*target(*place(source)))) for source in range(128)]
    return lax.ppermute(value, AXIS, pairs)


def along_x(steps):
    return lambda x, y, z, core: ((x + steps) % 4, y, z, core)


def along_y_or_z(steps):
    return lambda x, y, z, core: (
        (x, y, (z + steps) % 4, core) if core else (x, (y + steps) % 4, z, core)
    )


def along_z_or_y(steps):
    return lambda x, y, z, core: (
        (x, (y + steps) % 4, z, core) if core else (x, y, (z + steps) % 4, core)
    )


def other_core(x, y, z, core):
    return (x, y, z, 1 - core)


LAST_GROUPS = [
    [index_of(2 * xh + xl, y, z, 0) for xh in range(2) for xl in range(2) for y in range(4)]
    for z in range(4)
] + [
    [index_of(2 * xh + xl, y, z, 1) for xh in range(2) for z in range(4) for xl in range(2)]
    for y in range(4)
]


def my_core():
    return (lax.axis_index(AXIS) >> 5) & 1


IN_VMEM = pl.BlockSpec(memory_space=pltpu.VMEM)
IN_SMEM = pl.BlockSpec(memory_space=pltpu.SMEM)


def params():
    return pltpu.CompilerParams(vmem_limit_bytes=VMEM_LIMIT)


def cost(flops, bytes_accessed):
    return pl.CostEstimate(flops=flops, bytes_accessed=bytes_accessed, transcendentals=0)


def begin(pairs, sems, first=0):
    copies = [
        pltpu.make_async_copy(source, target, sems.at[first + slot])
        for slot, (source, target) in enumerate(pairs)
    ]
    for copy in copies:
        copy.start()
    return copies


def finish(copies):
    for copy in copies:
        copy.wait()


def stack(cuts, refs, target):
    offset = 0
    for which, start, rows in cuts:
        target[offset : offset + rows, :] = refs[which][start : start + rows, :]
        offset += rows


def hold_kernel(text, features, log_scale, bias, text_held, features_held, scalars):
    text_held[...] = text[...]
    features_held[...] = features[...]
    scalars[0:1, :] = jnp.full((1, 128), log_scale[0], f32)
    scalars[1:2, :] = jnp.full((1, 128), bias[0], f32)


def held(*arrays):
    return pl.pallas_call(
        hold_kernel,
        in_specs=[IN_VMEM] * 2 + [IN_SMEM] * 2,
        out_specs=[IN_VMEM] * 3,
        out_shape=[jax.ShapeDtypeStruct((ROWS, WIDTH), bf16)] * 2 + [MARK],
        compiler_params=params(),
        cost_estimate=cost(HOLD, 0),
        name="hold",
    )(*arrays)


def normalize_kernel(own, opposite, next_1, next_3, low, high):
    for line, parts in ((low, (own, opposite)), (high, (next_1, next_3))):
        for slot, part in enumerate(parts):
            values = part[...].astype(f32)
            inverse = lax.rsqrt(jnp.sum(values * values, axis=1, keepdims=True) + epsilon)
            line[ROWS * slot : ROWS * slot + ROWS, :] = (values * inverse).astype(bf16)


def normalized(*parts):
    return pl.pallas_call(
        normalize_kernel,
        in_specs=[IN_VMEM] * 4,
        out_specs=[IN_VMEM] * 2,
        out_shape=[jax.ShapeDtypeStruct((HALF // 2, WIDTH), bf16)] * 2,
        compiler_params=params(),
        name="normalize_texts",
    )(*parts)


def join_kernel(own, opposite, next_1, next_3, low, high, joined, low_later, high_later):
    for slot, part in enumerate((own, opposite, next_1, next_3)):
        joined[ROWS * slot : ROWS * slot + ROWS, :] = part[...]
    low_later[...] = low[...]
    high_later[...] = high[...]


def joined(*parts):
    return pl.pallas_call(
        join_kernel,
        in_specs=[IN_VMEM] * 6,
        out_specs=[IN_VMEM] * 3,
        out_shape=[jax.ShapeDtypeStruct((HALF, WIDTH), bf16)]
        + [jax.ShapeDtypeStruct((HALF // 2, WIDTH), bf16)] * 2,
        compiler_params=params(),
        cost_estimate=cost(WORK, 0),
        name="join",
    )(*parts)


def pass_kernel(low, high, after, low_on, high_on):
    low_on[...] = low[...]
    high_on[...] = high[...]


def passed(*parts):
    return pl.pallas_call(
        pass_kernel,
        in_specs=[IN_VMEM] * 3,
        out_specs=[IN_VMEM] * 2,
        out_shape=[jax.ShapeDtypeStruct((HALF // 2, WIDTH), bf16)] * 2,
        compiler_params=params(),
        name="pass_on",
    )(*parts)


def project_kernel(images, proj, unit, unit_f, inverse, turned, mark):
    mark[...] = jnp.zeros(mark.shape, f32)
    emb = jnp.dot(images[...], proj[...], preferred_element_type=f32)
    inv = lax.rsqrt(jnp.sum(emb * emb, axis=1, keepdims=True) + epsilon)
    emb = emb * inv
    unit_f[...] = emb
    inverse[...] = jnp.broadcast_to(inv, inverse.shape)
    unit[...] = emb.astype(bf16)
    turned[...] = images[...].T


def projected(images, proj_w):
    return pl.pallas_call(
        project_kernel,
        in_specs=[IN_VMEM] * 2,
        out_specs=[IN_VMEM] * 5,
        out_shape=[
            jax.ShapeDtypeStruct((HALF, WIDTH), bf16),
            jax.ShapeDtypeStruct((HALF, WIDTH), f32),
            jax.ShapeDtypeStruct((HALF, 128), f32),
            jax.ShapeDtypeStruct((WIDTH, HALF), bf16),
            MARK,
        ],
        compiler_params=params(),
        cost_estimate=cost(PROJ, 0),
        name="project_images",
    )(images, proj_w)


def wave_body(cuts, texts, units, scalars, scratch, diagonal, take):
    text, sim, weights = scratch
    stack(cuts, texts, text)

    def similar(step):
        sim[HALF * step : HALF * step + HALF, :] = lax.dot_general(
            units[step][...], text[...], (((1,), (1,)), ((), ())), preferred_element_type=f32
        )

    similar(0)
    half = 0.5 * jnp.exp(scalars[0:1, 0:1])
    half_shift = 0.5 * scalars[1:2, 0:1]

    def weigh(step):
        rows = slice(HALF * step, HALF * step + HALF)
        weights[rows, :] = (half + half * jnp.tanh(half * sim[rows, :] + half_shift)).astype(bf16)

    weigh(0)
    if diagonal:
        tanh = jnp.tanh(half * sim[:ROWS, :256] + half_shift)
        row = lax.broadcasted_iota(jnp.int32, (ROWS, 256), 0)
        column = lax.broadcasted_iota(jnp.int32, (ROWS, 256), 1)
        pair = jnp.where(row == column, half * tanh - half, half + half * tanh)
        weights[:ROWS, :256] = pair.astype(bf16)
    for step in range(1, len(units)):
        similar(step)
        weigh(step)
    for step in range(len(units)):
        rows = slice(HALF * step, HALF * step + HALF)
        take(step, jnp.dot(weights[rows, :], text[...], preferred_element_type=f32))


def first_wave_kernel(cuts, count, *refs):
    scalars, texts, units = refs[0], refs[1 : count + 1], refs[count + 1 : count + 3]
    totals, scratch = refs[count + 3 : count + 5], refs[count + 5 :]

    def take(step, product):
        totals[step][...] = product

    wave_body(cuts, texts, units, scalars, scratch, True, take)


def next_wave_kernel(cuts, count, *refs):
    scalars, texts, units = refs[0], refs[1 : count + 1], refs[count + 1 : count + 3]
    before, totals, scratch = refs[count + 3 : count + 5], refs[count + 5 : count + 7], refs[count + 7 :]

    def take(step, product):
        totals[step][...] = before[step][...] + product

    wave_body(cuts, texts, units, scalars, scratch, False, take)


def last_wave_kernel(cuts, count, *refs):
    scalars, texts, units = refs[0], refs[1 : count + 1], refs[count + 1 : count + 2]
    before, unit_f, inverse, projected_f, projected_b = refs[count + 2 : count + 7]
    scratch = refs[count + 7 :]

    def take(step, product):
        gradient = before[...] + product
        image = unit_f[...]
        along = jnp.sum(image * gradient, axis=1, keepdims=True)
        projection = (gradient - image * along) * inverse[:, 0:1]
        projected_f[...] = projection
        projected_b[...] = projection.astype(bf16)

    wave_body(cuts, texts, units, scalars, scratch, False, take)


def wave(kernel, scalars, cuts, texts, units, extra, out_shape, aliases, name):
    rows = sum(cut[2] for cut in cuts)
    images = HALF * len(units)
    return pl.pallas_call(
        lambda *refs: kernel(cuts, len(texts), *refs),
        in_specs=[IN_VMEM] * (1 + len(texts) + len(units) + len(extra)),
        out_specs=[IN_VMEM] * len(out_shape),
        out_shape=out_shape,
        input_output_aliases=aliases,
        scratch_shapes=[
            pltpu.VMEM((rows, WIDTH), bf16),
            pltpu.VMEM((images, rows), f32),
            pltpu.VMEM((images, rows), bf16),
        ],
        compiler_params=params(),
        cost_estimate=cost(WAVES[name], 0),
        name=name,
    )(scalars, *texts, *units, *extra)


def terms(turned, projected_f, other):
    both = (projected_f[...] + other[...].astype(f32)).astype(bf16)
    core = my_core()
    return [
        jnp.dot(
            turned[pl.ds(pl.multiple_of(576 * high + 288 * core, 16), 288), :],
            both,
            preferred_element_type=f32,
        )
        for high in range(2)
    ]


def first_terms_kernel(turned, projected_f, other, out):
    for high, term in enumerate(terms(turned, projected_f, other)):
        out[288 * high : 288 * high + 288, :] = term


def first_terms(*parts):
    return pl.pallas_call(
        first_terms_kernel,
        in_specs=[IN_VMEM] * 3,
        out_specs=IN_VMEM,
        out_shape=jax.ShapeDtypeStruct((HALF, WIDTH), f32),
        compiler_params=params(),
        cost_estimate=cost(1000, 1000),
        name="first_terms",
    )(*parts)


def cut_terms_kernel(turned, projected_f, other, first, mine, two, one, three, total):
    for high, term in enumerate(terms(turned, projected_f, other)):
        rows = slice(288 * high, 288 * high + 288)
        for tile in range(9):
            lanes = slice(128 * tile, 128 * tile + 128)
            total[tile, rows, :] = first[rows, lanes] + term[:, lanes]
    index = lax.axis_index(AXIS)
    outs = ((0, mine), (2, two), (1, one), (3, three))

    @pl.when(my_core() == 0)
    def _():
        for steps, out in outs:
            first = 72 * (((index >> 3) + steps) & 3)
            for tile in range(9):
                for row in range(9):
                    parts = [
                        total[tile, pl.ds(288 * high + first + row, 8, stride=9), :]
                        for high in range(2)
                    ]
                    out[16 * row : 16 * row + 16, 128 * tile : 128 * tile + 128] = (
                        jnp.concatenate(parts).astype(out.dtype)
                    )

    @pl.when(my_core() == 1)
    def _():
        for steps, out in outs:
            first = 9 * ((index + steps) & 3)
            for tile in range(9):
                for row in range(9):
                    part = total[tile, pl.ds(first + row, 16, stride=36), :]
                    out[16 * row : 16 * row + 16, 128 * tile : 128 * tile + 128] = part.astype(
                        out.dtype
                    )


def cut_terms(*parts):
    return pl.pallas_call(
        cut_terms_kernel,
        in_specs=[IN_VMEM] * 4,
        out_specs=[IN_VMEM] * 4,
        out_shape=[jax.ShapeDtypeStruct((ROWS, WIDTH), f32)]
        + [jax.ShapeDtypeStruct((ROWS, WIDTH), bf16)] * 3,
        scratch_shapes=[pltpu.VMEM((9, HALF, 128), f32)],
        compiler_params=params(),
        name="cut_terms",
    )(*parts)


def ring_sum_kernel(mine, two, one, three, out, eights, ninth):
    ninth[...] = jnp.zeros(ninth.shape, f32)
    for tile in range(9):
        lanes = slice(128 * tile, 128 * tile + 128)
        value = mine[:, lanes]
        for part in (two, one, three):
            value = value + part[:, lanes].astype(f32)
        for row in range(8):
            eights[tile, pl.ds(row, 16, stride=8), :] = value[16 * row : 16 * row + 16]
        ninth[tile // 8, pl.ds(tile % 8, 16, stride=8), :] = value[128:]
        out[:, lanes] = eights[tile].astype(bf16)
    out[:, WIDTH : WIDTH + 128] = ninth[0].astype(bf16)
    out[:, WIDTH + 128 :] = ninth[1].astype(bf16)


def ring_sum(*parts):
    return pl.pallas_call(
        ring_sum_kernel,
        out_shape=jax.ShapeDtypeStruct((128, SLAB), bf16),
        scratch_shapes=[pltpu.VMEM((9, 128, 128), f32), pltpu.VMEM((2, 128, 128), f32)],
        compiler_params=params(),
        name="ring_sum",
    )(*parts)


def last_sum_kernel(pieces, out):
    total = jnp.zeros((16, SLAB), f32)
    for step in range(8):
        total = total + pieces[16 * step : 16 * step + 16, :].astype(f32)
    total = total[:8] + total[8:]
    out[:8, :] = total[:, :WIDTH]
    for tile in range(9):
        sublane, lane = tile % 8, WIDTH + 128 * (tile // 8)
        out[8:9, 128 * tile : 128 * tile + 128] = total[sublane : sublane + 1, lane : lane + 128]


def last_sum(pieces):
    return pl.pallas_call(
        last_sum_kernel,
        out_shape=jax.ShapeDtypeStruct((9, WIDTH), f32),
        compiler_params=params(),
        name="last_sum",
    )(pieces)


def ring(value, axis):
    return [send(value, axis(steps)) for steps in (2, 1, 3)]


def per_device(features, text_emb, proj_w, log_scale, bias):
    text, images, scalars = held(text_emb, features, log_scale, bias)
    low, high = normalized(text, *ring(text_emb, along_y_or_z))
    here, low_later, high_later = joined(images, *ring(features, along_x), low, high)
    there = send(here, other_core)
    low_1, high_3 = send(low, along_z_or_y(1)), send(high, along_z_or_y(3))
    high_1, low_3 = send(high_later, along_z_or_y(1)), send(low_later, along_z_or_y(3))
    units, units_f, inverses, turns, marks = zip(
        projected(here, proj_w), projected(there, proj_w)
    )
    low_on, high_on = passed(low_1, high_3, marks[1])
    low_2, high_2 = send(low_on, along_z_or_y(1)), send(high_on, along_z_or_y(3))

    sums = [jax.ShapeDtypeStruct((HALF, WIDTH), f32)] * 2
    totals = wave(
        first_wave_kernel,
        scalars,
        ((0, 0, 288), (1, 0, 224)),
        (low, high),
        units,
        (),
        sums,
        {},
        "first_wave",
    )
    totals = wave(
        next_wave_kernel,
        scalars,
        ((0, 224, 64), (1, 0, 288), (2, 0, 288), (3, 0, 288), (4, 0, 96)),
        (high, low_1, high_3, high_1, low_3),
        units,
        totals,
        sums,
        {8: 0, 9: 1},
        "second_wave",
    )
    own, sent = zip(
        *(
            wave(
                last_wave_kernel,
                scalars,
                ((0, 96, 192), (1, 0, 288), (2, 0, 288)),
                (low_3, low_2, high_2),
                units[half : half + 1],
                (totals[half], units_f[half], inverses[half]),
                [
                    jax.ShapeDtypeStruct((HALF, WIDTH), f32),
                    jax.ShapeDtypeStruct((HALF, WIDTH), bf16),
                ],
                {},
                "last_wave",
            )
            for half in range(2)
        )
    )
    got = [send(half, other_core) for half in sent]
    first = first_terms(turns[1], own[1], got[0])
    mine, two, one, three = cut_terms(turns[0], own[0], got[1], first)
    parts = [send(part, along_z_or_y(steps)) for part, steps in ((two, 2), (one, 1), (three, 3))]
    pieces = ring_sum(mine, *parts)
    pieces = lax.all_to_all(pieces, AXIS, 0, 0, axis_index_groups=LAST_GROUPS, tiled=True)
    return last_sum(pieces)


def solution(mesh):
    flat = Mesh(mesh.devices.reshape(-1), (AXIS,))
    rows = P(AXIS, None)
    return jax.shard_map(
        per_device,
        mesh=flat,
        in_specs=(rows, rows, P(), P(), P()),
        out_specs=rows,
        check_vma=False,
    )
```

```python
import jax
import jax.numpy as jnp
from jax import lax
from jax.experimental import pallas as pl
from jax.experimental.pallas import tpu as pltpu
from jax.sharding import Mesh, PartitionSpec as P

epsilon = 1e-06
bf16 = jnp.bfloat16
f32 = jnp.float32

AXIS = "d"
ROWS = 144
WIDTH = 1152
HALF = 4 * ROWS
IMAGES = 2 * HALF
TURNED = 512
EARLY = 384
SLAB = 1408
VMEM_LIMIT = 20 << 20
WORK = 12_000_000_000
PROJ = 20_000_000_000
W1 = 30_000_000_000
WAVES = {"first_wave": W1, "second_wave": 1000, "last_wave": 1000, "rest_wave": 1000}
HOLD = 1000
MARK = jax.ShapeDtypeStruct((8, 128), f32)


def place(index):
    y, xl, z = index & 3, (index >> 2) & 1, (index >> 3) & 3
    core, xh = (index >> 5) & 1, (index >> 6) & 1
    return 2 * xh + xl, y, z, core


def index_of(x, y, z, core):
    return (x >> 1) * 64 + core * 32 + z * 8 + (x & 1) * 4 + y


def send(value, target):
    pairs = [(source, index_of(*target(*place(source)))) for source in range(128)]
    return lax.ppermute(value, AXIS, pairs)


def along_x(steps):
    return lambda x, y, z, core: ((x + steps) % 4, y, z, core)


def along_y_or_z(steps):
    return lambda x, y, z, core: (
        (x, y, (z + steps) % 4, core) if core else (x, (y + steps) % 4, z, core)
    )


def along_z_or_y(steps):
    return lambda x, y, z, core: (
        (x, (y + steps) % 4, z, core) if core else (x, y, (z + steps) % 4, core)
    )


def other_core(x, y, z, core):
    return (x, y, z, 1 - core)


LAST_GROUPS = [
    [index_of(2 * xh + xl, y, z, 0) for xh in range(2) for xl in range(2) for y in range(4)]
    for z in range(4)
] + [
    [index_of(2 * xh + xl, y, z, 1) for xh in range(2) for z in range(4) for xl in range(2)]
    for y in range(4)
]


def my_core():
    return (lax.axis_index(AXIS) >> 5) & 1


IN_VMEM = pl.BlockSpec(memory_space=pltpu.VMEM)
IN_SMEM = pl.BlockSpec(memory_space=pltpu.SMEM)


def params():
    return pltpu.CompilerParams(vmem_limit_bytes=VMEM_LIMIT)


def cost(flops, bytes_accessed):
    return pl.CostEstimate(flops=flops, bytes_accessed=bytes_accessed, transcendentals=0)


def begin(pairs, sems, first=0):
    copies = [
        pltpu.make_async_copy(source, target, sems.at[first + slot])
        for slot, (source, target) in enumerate(pairs)
    ]
    for copy in copies:
        copy.start()
    return copies


def finish(copies):
    for copy in copies:
        copy.wait()


def stack(cuts, refs, target):
    offset = 0
    for which, start, rows in cuts:
        target[offset : offset + rows, :] = refs[which][start : start + rows, :]
        offset += rows


def hold_kernel(text, features, log_scale, bias, text_held, features_held, scalars):
    text_held[...] = text[...]
    features_held[...] = features[...]
    scalars[0:1, :] = jnp.full((1, 128), log_scale[0], f32)
    scalars[1:2, :] = jnp.full((1, 128), bias[0], f32)


def held(*arrays):
    return pl.pallas_call(
        hold_kernel,
        in_specs=[IN_VMEM] * 2 + [IN_SMEM] * 2,
        out_specs=[IN_VMEM] * 3,
        out_shape=[jax.ShapeDtypeStruct((ROWS, WIDTH), bf16)] * 2 + [MARK],
        compiler_params=params(),
        cost_estimate=cost(HOLD, 0),
        name="hold",
    )(*arrays)


def normalize_kernel(own, opposite, next_1, next_3, low, high):
    for line, parts in ((low, (own, opposite)), (high, (next_1, next_3))):
        for slot, part in enumerate(parts):
            values = part[...].astype(f32)
            inverse = lax.rsqrt(jnp.sum(values * values, axis=1, keepdims=True) + epsilon)
            line[ROWS * slot : ROWS * slot + ROWS, :] = (values * inverse).astype(bf16)


def normalized(*parts):
    return pl.pallas_call(
        normalize_kernel,
        in_specs=[IN_VMEM] * 4,
        out_specs=[IN_VMEM] * 2,
        out_shape=[jax.ShapeDtypeStruct((HALF // 2, WIDTH), bf16)] * 2,
        compiler_params=params(),
        name="normalize_texts",
    )(*parts)


def join_kernel(own, opposite, next_1, next_3, low, high, joined, low_later, high_later):
    for slot, part in enumerate((own, opposite, next_1, next_3)):
        joined[ROWS * slot : ROWS * slot + ROWS, :] = part[...]
    low_later[...] = low[...]
    high_later[...] = high[...]


def joined(*parts):
    return pl.pallas_call(
        join_kernel,
        in_specs=[IN_VMEM] * 6,
        out_specs=[IN_VMEM] * 3,
        out_shape=[jax.ShapeDtypeStruct((HALF, WIDTH), bf16)]
        + [jax.ShapeDtypeStruct((HALF // 2, WIDTH), bf16)] * 2,
        compiler_params=params(),
        cost_estimate=cost(WORK, 0),
        name="join",
    )(*parts)


def pass_kernel(low, high, after, low_on, high_on):
    low_on[...] = low[...]
    high_on[...] = high[...]


def passed(*parts):
    return pl.pallas_call(
        pass_kernel,
        in_specs=[IN_VMEM] * 3,
        out_specs=[IN_VMEM] * 2,
        out_shape=[jax.ShapeDtypeStruct((HALF // 2, WIDTH), bf16)] * 2,
        compiler_params=params(),
        name="pass_on",
    )(*parts)


def project_kernel(images, proj, unit, unit_f, inverse, turned, mark):
    mark[...] = jnp.zeros(mark.shape, f32)
    emb = jnp.dot(images[...], proj[...], preferred_element_type=f32)
    inv = lax.rsqrt(jnp.sum(emb * emb, axis=1, keepdims=True) + epsilon)
    emb = emb * inv
    unit_f[...] = emb
    inverse[...] = jnp.broadcast_to(inv, inverse.shape)
    unit[...] = emb.astype(bf16)
    turned[...] = images[...].T


def projected(images, proj_w):
    return pl.pallas_call(
        project_kernel,
        in_specs=[IN_VMEM] * 2,
        out_specs=[IN_VMEM] * 5,
        out_shape=[
            jax.ShapeDtypeStruct((HALF, WIDTH), bf16),
            jax.ShapeDtypeStruct((HALF, WIDTH), f32),
            jax.ShapeDtypeStruct((HALF, 128), f32),
            jax.ShapeDtypeStruct((WIDTH, HALF), bf16),
            MARK,
        ],
        compiler_params=params(),
        cost_estimate=cost(PROJ, 0),
        name="project_images",
    )(images, proj_w)


def wave_body(blocks, text, scalars, sim, weights, diagonal, take):
    half = 0.5 * jnp.exp(scalars[0:1, 0:1])
    half_shift = 0.5 * scalars[1:2, 0:1]
    rows, offset = [], 0
    for unit, start, count in blocks:
        rows.append(slice(offset, offset + count))
        offset += count
    for which, (unit, start, count) in enumerate(blocks):
        sim[rows[which], :] = lax.dot_general(
            unit[start : start + count, :],
            text[...],
            (((1,), (1,)), ((), ())),
            preferred_element_type=f32,
        )
        weights[rows[which], :] = (
            half + half * jnp.tanh(half * sim[rows[which], :] + half_shift)
        ).astype(bf16)
        if diagonal and which == 0:
            tanh = jnp.tanh(half * sim[:ROWS, :256] + half_shift)
            row = lax.broadcasted_iota(jnp.int32, (ROWS, 256), 0)
            column = lax.broadcasted_iota(jnp.int32, (ROWS, 256), 1)
            pair = jnp.where(row == column, half * tanh - half, half + half * tanh)
            weights[:ROWS, :256] = pair.astype(bf16)
    for which in range(len(blocks)):
        take(which, jnp.dot(weights[rows[which], :], text[...], preferred_element_type=f32))


def first_wave_kernel(cuts, scalars, low, high, unit_a, unit_b, total_a, total_b, text, sim, weights):
    stack(cuts, (low, high), text)
    totals = (total_a, total_b)

    def take(which, product):
        totals[which][...] = product

    blocks = ((unit_a, 0, HALF), (unit_b, 0, HALF))
    wave_body(blocks, text, scalars, sim, weights, True, take)


def next_wave_kernel(cuts, scalars, *refs):
    count = len(refs) - 9
    texts, (unit_a, unit_b), before, totals = (
        refs[:count],
        refs[count : count + 2],
        refs[count + 2 : count + 4],
        refs[count + 4 : count + 6],
    )
    text, sim, weights = refs[count + 6 :]
    stack(cuts, texts, text)

    def take(which, product):
        totals[which][...] = before[which][...] + product

    blocks = ((unit_a, 0, HALF), (unit_b, 0, HALF))
    wave_body(blocks, text, scalars, sim, weights, False, take)


def project_gradient(start, count, scalars, text, states, projected_f, projected_b, sim, weights):
    units, totals, units_f, inverses = (states[2 * slot : 2 * slot + 2] for slot in range(4))
    rows = slice(start, start + count)

    def take(which, product):
        gradient = totals[which][rows, :] + product
        image = units_f[which][rows, :]
        along = jnp.sum(image * gradient, axis=1, keepdims=True)
        projection = (gradient - image * along) * inverses[which][rows, 0:1]
        out = slice(which * count, which * count + count)
        projected_f[out, :] = projection
        projected_b[out, :] = projection.astype(bf16)

    blocks = tuple((unit, start, count) for unit in units)
    wave_body(blocks, text, scalars, sim, weights, False, take)


def last_wave_kernel(cuts, scalars, *refs):
    count = len(refs) - 13
    projected_f, projected_b, text, sim, weights = refs[count + 8 :]
    stack(cuts, refs[:count], text)
    project_gradient(
        0, EARLY, scalars, text, refs[count : count + 8], projected_f, projected_b, sim, weights
    )


def rest_wave_kernel(cuts, scalars, text, *refs):
    project_gradient(EARLY, HALF - EARLY, scalars, text, refs[:8], *refs[8:])


def wave(kernel, cuts, operands, images, out_shape, aliases, name, stacked=True):
    rows = sum(cut[2] for cut in cuts)
    return pl.pallas_call(
        lambda *refs: kernel(cuts, *refs),
        in_specs=[IN_VMEM] * len(operands),
        out_specs=[IN_VMEM] * len(out_shape),
        out_shape=out_shape,
        input_output_aliases=aliases,
        scratch_shapes=[pltpu.VMEM((rows, WIDTH), bf16)] * stacked
        + [pltpu.VMEM((images, rows), f32), pltpu.VMEM((images, rows), bf16)],
        compiler_params=params(),
        cost_estimate=cost(WAVES[name], 0),
        name=name,
    )(*operands)


def chip_projection(projected_f, other, count):
    return [
        (projected_f[first : first + count, :] + other[count - first : 2 * count - first, :].astype(f32)).astype(bf16)
        for first in (0, count)
    ]


def my_rows(high):
    return pl.ds(pl.multiple_of(576 * high + 288 * my_core(), 16), 288)


def first_terms_kernel(turned_a, turned_b, projected_f, other, out):
    both = jnp.concatenate(chip_projection(projected_f, other, EARLY))
    for high in range(2):
        left = jnp.concatenate([turned[my_rows(high), :EARLY] for turned in (turned_a, turned_b)], axis=1)
        out[288 * high : 288 * high + 288, :] = jnp.dot(left, both, preferred_element_type=f32)


def first_terms(*parts):
    return pl.pallas_call(
        first_terms_kernel,
        in_specs=[IN_VMEM] * 4,
        out_specs=IN_VMEM,
        out_shape=jax.ShapeDtypeStruct((HALF, WIDTH), f32),
        compiler_params=params(),
        cost_estimate=cost(1000, 1000),
        name="first_terms",
    )(*parts)


def cut_terms_kernel(turned_a, turned_b, projected_f, other, first, mine, two, one, three, total):
    both_a, both_b = chip_projection(projected_f, other, HALF - EARLY)
    for high in range(2):
        rows = slice(288 * high, 288 * high + 288)
        term = first[rows, :]
        for turned, both in ((turned_a, both_a), (turned_b, both_b)):
            term = term + jnp.dot(turned[my_rows(high), EARLY:], both, preferred_element_type=f32)
        for tile in range(9):
            total[tile, rows, :] = term[:, 128 * tile : 128 * tile + 128]
    index = lax.axis_index(AXIS)
    outs = ((0, mine), (2, two), (1, one), (3, three))

    @pl.when(my_core() == 0)
    def _():
        for steps, out in outs:
            first = 72 * (((index >> 3) + steps) & 3)
            for tile in range(9):
                for row in range(9):
                    parts = [
                        total[tile, pl.ds(288 * high + first + row, 8, stride=9), :]
                        for high in range(2)
                    ]
                    out[16 * row : 16 * row + 16, 128 * tile : 128 * tile + 128] = (
                        jnp.concatenate(parts).astype(out.dtype)
                    )

    @pl.when(my_core() == 1)
    def _():
        for steps, out in outs:
            first = 9 * ((index + steps) & 3)
            for tile in range(9):
                for row in range(9):
                    part = total[tile, pl.ds(first + row, 16, stride=36), :]
                    out[16 * row : 16 * row + 16, 128 * tile : 128 * tile + 128] = part.astype(
                        out.dtype
                    )


def cut_terms(*parts):
    return pl.pallas_call(
        cut_terms_kernel,
        in_specs=[IN_VMEM] * 5,
        out_specs=[IN_VMEM] * 4,
        out_shape=[jax.ShapeDtypeStruct((ROWS, WIDTH), f32)]
        + [jax.ShapeDtypeStruct((ROWS, WIDTH), bf16)] * 3,
        scratch_shapes=[pltpu.VMEM((9, HALF, 128), f32)],
        compiler_params=params(),
        name="cut_terms",
    )(*parts)


def ring_sum_kernel(mine, two, one, three, out, eights, ninth):
    ninth[...] = jnp.zeros(ninth.shape, f32)
    for tile in range(9):
        lanes = slice(128 * tile, 128 * tile + 128)
        value = mine[:, lanes]
        for part in (two, one, three):
            value = value + part[:, lanes].astype(f32)
        for row in range(8):
            eights[tile, pl.ds(row, 16, stride=8), :] = value[16 * row : 16 * row + 16]
        ninth[tile // 8, pl.ds(tile % 8, 16, stride=8), :] = value[128:]
        out[:, lanes] = eights[tile].astype(bf16)
    out[:, WIDTH : WIDTH + 128] = ninth[0].astype(bf16)
    out[:, WIDTH + 128 :] = ninth[1].astype(bf16)


def ring_sum(*parts):
    return pl.pallas_call(
        ring_sum_kernel,
        out_shape=jax.ShapeDtypeStruct((128, SLAB), bf16),
        scratch_shapes=[pltpu.VMEM((9, 128, 128), f32), pltpu.VMEM((2, 128, 128), f32)],
        compiler_params=params(),
        name="ring_sum",
    )(*parts)


def last_sum_kernel(pieces, out):
    total = jnp.zeros((16, SLAB), f32)
    for step in range(8):
        total = total + pieces[16 * step : 16 * step + 16, :].astype(f32)
    total = total[:8] + total[8:]
    out[:8, :] = total[:, :WIDTH]
    for tile in range(9):
        sublane, lane = tile % 8, WIDTH + 128 * (tile // 8)
        out[8:9, 128 * tile : 128 * tile + 128] = total[sublane : sublane + 1, lane : lane + 128]


def last_sum(pieces):
    return pl.pallas_call(
        last_sum_kernel,
        out_shape=jax.ShapeDtypeStruct((9, WIDTH), f32),
        compiler_params=params(),
        name="last_sum",
    )(pieces)


def ring(value, axis):
    return [send(value, axis(steps)) for steps in (2, 1, 3)]


def per_device(features, text_emb, proj_w, log_scale, bias):
    text, images, scalars = held(text_emb, features, log_scale, bias)
    low, high = normalized(text, *ring(text_emb, along_y_or_z))
    here, low_later, high_later = joined(images, *ring(features, along_x), low, high)
    there = send(here, other_core)
    low_1, high_3 = send(low, along_z_or_y(1)), send(high, along_z_or_y(3))
    high_1, low_3 = send(high_later, along_z_or_y(1)), send(low_later, along_z_or_y(3))
    units, units_f, inverses, turns, marks = zip(
        projected(here, proj_w), projected(there, proj_w)
    )
    low_on, high_on = passed(low_1, high_3, marks[1])
    low_2, high_2 = send(low_on, along_z_or_y(1)), send(high_on, along_z_or_y(3))

    sums = [jax.ShapeDtypeStruct((HALF, WIDTH), f32)] * 2
    totals = wave(
        first_wave_kernel,
        ((0, 0, 288), (1, 0, 224)),
        (scalars, low, high, *units),
        IMAGES,
        sums,
        {},
        "first_wave",
    )
    totals = wave(
        next_wave_kernel,
        ((0, 224, 64), (1, 0, 288), (2, 0, 288), (3, 0, 288), (4, 0, 96)),
        (scalars, high, low_1, high_3, high_1, low_3, *units, *totals),
        IMAGES,
        sums,
        {8: 0, 9: 1},
        "second_wave",
    )
    states = (*units, *totals, *units_f, *inverses)
    texts = jax.ShapeDtypeStruct((768, WIDTH), bf16)
    own_1, sent_1, text = wave(
        last_wave_kernel,
        ((0, 96, 192), (1, 0, 288), (2, 0, 288)),
        (scalars, low_3, low_2, high_2, *states),
        2 * EARLY,
        [
            jax.ShapeDtypeStruct((2 * EARLY, WIDTH), f32),
            jax.ShapeDtypeStruct((2 * EARLY, WIDTH), bf16),
            texts,
        ],
        {},
        "last_wave",
        stacked=False,
    )
    own_2, sent_2 = wave(
        rest_wave_kernel,
        ((0, 0, 768),),
        (scalars, text, *states),
        IMAGES - 2 * EARLY,
        [
            jax.ShapeDtypeStruct((IMAGES - 2 * EARLY, WIDTH), f32),
            jax.ShapeDtypeStruct((IMAGES - 2 * EARLY, WIDTH), bf16),
        ],
        {},
        "rest_wave",
        stacked=False,
    )
    got_1, got_2 = send(sent_1, other_core), send(sent_2, other_core)
    first = first_terms(*turns, own_1, got_1)
    mine, two, one, three = cut_terms(*turns, own_2, got_2, first)
    parts = [send(part, along_z_or_y(steps)) for part, steps in ((two, 2), (one, 1), (three, 3))]
    pieces = ring_sum(mine, *parts)
    pieces = lax.all_to_all(pieces, AXIS, 0, 0, axis_index_groups=LAST_GROUPS, tiled=True)
    return last_sum(pieces)


def solution(mesh):
    flat = Mesh(mesh.devices.reshape(-1), (AXIS,))
    rows = P(AXIS, None)
    return jax.shard_map(
        per_device,
        mesh=flat,
        in_specs=(rows, rows, P(), P(), P()),
        out_specs=rows,
        check_vma=False,
    )
```

```python
import jax
import jax.numpy as jnp
from jax import lax
from jax.experimental import pallas as pl
from jax.experimental.pallas import tpu as pltpu
from jax.sharding import Mesh, PartitionSpec as P

epsilon = 1e-06
bf16 = jnp.bfloat16
f32 = jnp.float32

AXIS = "d"
ROWS = 144
WIDTH = 1152
HALF = 4 * ROWS
IMAGES = 2 * HALF
TURNED = 512
EARLY = 384
SLAB = 1408
VMEM_LIMIT = 20 << 20
WORK = 12_000_000_000
PROJ = 20_000_000_000
W1 = 30_000_000_000
WAVES = {"first_wave": W1, "second_wave": 1000, "last_wave": 1000, "rest_wave": 1000}
HOLD = 12_000_000_000
NORM = 1000
MARK = jax.ShapeDtypeStruct((8, 128), f32)


def place(index):
    y, xl, z = index & 3, (index >> 2) & 1, (index >> 3) & 3
    core, xh = (index >> 5) & 1, (index >> 6) & 1
    return 2 * xh + xl, y, z, core


def index_of(x, y, z, core):
    return (x >> 1) * 64 + core * 32 + z * 8 + (x & 1) * 4 + y


def send(value, target):
    pairs = [(source, index_of(*target(*place(source)))) for source in range(128)]
    return lax.ppermute(value, AXIS, pairs)


def along_x(steps):
    return lambda x, y, z, core: ((x + steps) % 4, y, z, core)


def along_y_or_z(steps):
    return lambda x, y, z, core: (
        (x, y, (z + steps) % 4, core) if core else (x, (y + steps) % 4, z, core)
    )


def along_z_or_y(steps):
    return lambda x, y, z, core: (
        (x, (y + steps) % 4, z, core) if core else (x, y, (z + steps) % 4, core)
    )


def other_core(x, y, z, core):
    return (x, y, z, 1 - core)


LAST_GROUPS = [
    [index_of(2 * xh + xl, y, z, 0) for xh in range(2) for xl in range(2) for y in range(4)]
    for z in range(4)
] + [
    [index_of(2 * xh + xl, y, z, 1) for xh in range(2) for z in range(4) for xl in range(2)]
    for y in range(4)
]


def my_core():
    return (lax.axis_index(AXIS) >> 5) & 1


IN_VMEM = pl.BlockSpec(memory_space=pltpu.VMEM)
IN_SMEM = pl.BlockSpec(memory_space=pltpu.SMEM)


def params():
    return pltpu.CompilerParams(vmem_limit_bytes=VMEM_LIMIT)


def cost(flops, bytes_accessed):
    return pl.CostEstimate(flops=flops, bytes_accessed=bytes_accessed, transcendentals=0)


def begin(pairs, sems, first=0):
    copies = [
        pltpu.make_async_copy(source, target, sems.at[first + slot])
        for slot, (source, target) in enumerate(pairs)
    ]
    for copy in copies:
        copy.start()
    return copies


def finish(copies):
    for copy in copies:
        copy.wait()


def stack(cuts, refs, target):
    offset = 0
    for which, start, rows in cuts:
        target[offset : offset + rows, :] = refs[which][start : start + rows, :]
        offset += rows


def hold_kernel(text, features, log_scale, bias, text_held, features_held, scalars):
    text_held[...] = text[...]
    features_held[...] = features[...]
    scalars[0:1, :] = jnp.full((1, 128), log_scale[0], f32)
    scalars[1:2, :] = jnp.full((1, 128), bias[0], f32)


def held(*arrays):
    return pl.pallas_call(
        hold_kernel,
        in_specs=[IN_VMEM] * 2 + [IN_SMEM] * 2,
        out_specs=[IN_VMEM] * 3,
        out_shape=[jax.ShapeDtypeStruct((ROWS, WIDTH), bf16)] * 2 + [MARK],
        compiler_params=params(),
        cost_estimate=cost(HOLD, 0),
        name="hold",
    )(*arrays)


def normalize_kernel(upper, lower, *refs):
    unit = refs[-1]
    for slot, part in enumerate((upper, lower)):
        values = part[...].astype(f32)
        inverse = lax.rsqrt(jnp.sum(values * values, axis=1, keepdims=True) + epsilon)
        unit[ROWS * slot : ROWS * slot + ROWS, :] = (values * inverse).astype(bf16)


def normalized(*parts):
    return pl.pallas_call(
        normalize_kernel,
        in_specs=[IN_VMEM] * len(parts),
        out_specs=IN_VMEM,
        out_shape=jax.ShapeDtypeStruct((HALF // 2, WIDTH), bf16),
        compiler_params=params(),
        cost_estimate=cost(NORM, 0),
        name="normalize_texts",
    )(*parts)


def join_kernel(own, opposite, next_1, next_3, low, high, joined, low_later, high_later):
    for slot, part in enumerate((own, opposite, next_1, next_3)):
        joined[ROWS * slot : ROWS * slot + ROWS, :] = part[...]
    low_later[...] = low[...]
    high_later[...] = high[...]


def joined(*parts):
    return pl.pallas_call(
        join_kernel,
        in_specs=[IN_VMEM] * 6,
        out_specs=[IN_VMEM] * 3,
        out_shape=[jax.ShapeDtypeStruct((HALF, WIDTH), bf16)]
        + [jax.ShapeDtypeStruct((HALF // 2, WIDTH), bf16)] * 2,
        compiler_params=params(),
        cost_estimate=cost(WORK, 0),
        name="join",
    )(*parts)


def pass_kernel(low, high, after, low_on, high_on):
    low_on[...] = low[...]
    high_on[...] = high[...]


def passed(*parts):
    return pl.pallas_call(
        pass_kernel,
        in_specs=[IN_VMEM] * 3,
        out_specs=[IN_VMEM] * 2,
        out_shape=[jax.ShapeDtypeStruct((HALF // 2, WIDTH), bf16)] * 2,
        compiler_params=params(),
        name="pass_on",
    )(*parts)


def project_kernel(images, proj, unit, unit_f, inverse, turned, mark):
    mark[...] = jnp.zeros(mark.shape, f32)
    emb = jnp.dot(images[...], proj[...], preferred_element_type=f32)
    inv = lax.rsqrt(jnp.sum(emb * emb, axis=1, keepdims=True) + epsilon)
    emb = emb * inv
    unit_f[...] = emb
    inverse[...] = jnp.broadcast_to(inv, inverse.shape)
    unit[...] = emb.astype(bf16)
    turned[...] = images[...].T


def projected(images, proj_w):
    return pl.pallas_call(
        project_kernel,
        in_specs=[IN_VMEM] * 2,
        out_specs=[IN_VMEM] * 5,
        out_shape=[
            jax.ShapeDtypeStruct((HALF, WIDTH), bf16),
            jax.ShapeDtypeStruct((HALF, WIDTH), f32),
            jax.ShapeDtypeStruct((HALF, 128), f32),
            jax.ShapeDtypeStruct((WIDTH, HALF), bf16),
            MARK,
        ],
        compiler_params=params(),
        cost_estimate=cost(PROJ, 0),
        name="project_images",
    )(images, proj_w)


def wave_body(blocks, text, scalars, sim, weights, diagonal, take):
    half = 0.5 * jnp.exp(scalars[0:1, 0:1])
    half_shift = 0.5 * scalars[1:2, 0:1]
    rows, offset = [], 0
    for unit, start, count in blocks:
        rows.append(slice(offset, offset + count))
        offset += count
    for which, (unit, start, count) in enumerate(blocks):
        sim[rows[which], :] = lax.dot_general(
            unit[start : start + count, :],
            text[...],
            (((1,), (1,)), ((), ())),
            preferred_element_type=f32,
        )
        weights[rows[which], :] = (
            half + half * jnp.tanh(half * sim[rows[which], :] + half_shift)
        ).astype(bf16)
        if diagonal and which == 0:
            tanh = jnp.tanh(half * sim[:ROWS, :256] + half_shift)
            row = lax.broadcasted_iota(jnp.int32, (ROWS, 256), 0)
            column = lax.broadcasted_iota(jnp.int32, (ROWS, 256), 1)
            pair = jnp.where(row == column, half * tanh - half, half + half * tanh)
            weights[:ROWS, :256] = pair.astype(bf16)
    for which in range(len(blocks)):
        take(which, jnp.dot(weights[rows[which], :], text[...], preferred_element_type=f32))


def first_wave_kernel(cuts, scalars, low, high, unit_a, unit_b, total_a, total_b, text, sim, weights):
    stack(cuts, (low, high), text)
    totals = (total_a, total_b)

    def take(which, product):
        totals[which][...] = product

    blocks = ((unit_a, 0, HALF), (unit_b, 0, HALF))
    wave_body(blocks, text, scalars, sim, weights, True, take)


def next_wave_kernel(cuts, scalars, *refs):
    count = len(refs) - 9
    texts, (unit_a, unit_b), before, totals = (
        refs[:count],
        refs[count : count + 2],
        refs[count + 2 : count + 4],
        refs[count + 4 : count + 6],
    )
    text, sim, weights = refs[count + 6 :]
    stack(cuts, texts, text)

    def take(which, product):
        totals[which][...] = before[which][...] + product

    blocks = ((unit_a, 0, HALF), (unit_b, 0, HALF))
    wave_body(blocks, text, scalars, sim, weights, False, take)


def project_gradient(start, count, scalars, text, states, projected_f, projected_b, sim, weights):
    units, totals, units_f, inverses = (states[2 * slot : 2 * slot + 2] for slot in range(4))
    rows = slice(start, start + count)

    def take(which, product):
        gradient = totals[which][rows, :] + product
        image = units_f[which][rows, :]
        along = jnp.sum(image * gradient, axis=1, keepdims=True)
        projection = (gradient - image * along) * inverses[which][rows, 0:1]
        out = slice(which * count, which * count + count)
        projected_f[out, :] = projection
        projected_b[out, :] = projection.astype(bf16)

    blocks = tuple((unit, start, count) for unit in units)
    wave_body(blocks, text, scalars, sim, weights, False, take)


def last_wave_kernel(cuts, scalars, *refs):
    count = len(refs) - 13
    projected_f, projected_b, text, sim, weights = refs[count + 8 :]
    stack(cuts, refs[:count], text)
    project_gradient(
        0, EARLY, scalars, text, refs[count : count + 8], projected_f, projected_b, sim, weights
    )


def rest_wave_kernel(cuts, scalars, text, *refs):
    project_gradient(EARLY, HALF - EARLY, scalars, text, refs[:8], *refs[8:])


def wave(kernel, cuts, operands, images, out_shape, aliases, name, stacked=True):
    rows = sum(cut[2] for cut in cuts)
    return pl.pallas_call(
        lambda *refs: kernel(cuts, *refs),
        in_specs=[IN_VMEM] * len(operands),
        out_specs=[IN_VMEM] * len(out_shape),
        out_shape=out_shape,
        input_output_aliases=aliases,
        scratch_shapes=[pltpu.VMEM((rows, WIDTH), bf16)] * stacked
        + [pltpu.VMEM((images, rows), f32), pltpu.VMEM((images, rows), bf16)],
        compiler_params=params(),
        cost_estimate=cost(WAVES[name], 0),
        name=name,
    )(*operands)


def chip_projection(projected_f, other, count):
    return [
        (projected_f[first : first + count, :] + other[count - first : 2 * count - first, :].astype(f32)).astype(bf16)
        for first in (0, count)
    ]


def my_rows(high):
    return pl.ds(pl.multiple_of(576 * high + 288 * my_core(), 16), 288)


def first_terms_kernel(turned_a, turned_b, projected_f, other, out):
    both = jnp.concatenate(chip_projection(projected_f, other, EARLY))
    for high in range(2):
        left = jnp.concatenate([turned[my_rows(high), :EARLY] for turned in (turned_a, turned_b)], axis=1)
        out[288 * high : 288 * high + 288, :] = jnp.dot(left, both, preferred_element_type=f32)


def first_terms(*parts):
    return pl.pallas_call(
        first_terms_kernel,
        in_specs=[IN_VMEM] * 4,
        out_specs=IN_VMEM,
        out_shape=jax.ShapeDtypeStruct((HALF, WIDTH), f32),
        compiler_params=params(),
        cost_estimate=cost(1000, 1000),
        name="first_terms",
    )(*parts)


def cut_terms_kernel(turned_a, turned_b, projected_f, other, first, mine, two, one, three, total):
    both_a, both_b = chip_projection(projected_f, other, HALF - EARLY)
    for high in range(2):
        rows = slice(288 * high, 288 * high + 288)
        term = first[rows, :]
        for turned, both in ((turned_a, both_a), (turned_b, both_b)):
            term = term + jnp.dot(turned[my_rows(high), EARLY:], both, preferred_element_type=f32)
        for tile in range(9):
            total[tile, rows, :] = term[:, 128 * tile : 128 * tile + 128]
    index = lax.axis_index(AXIS)
    outs = ((0, mine), (2, two), (1, one), (3, three))

    @pl.when(my_core() == 0)
    def _():
        for steps, out in outs:
            first = 72 * (((index >> 3) + steps) & 3)
            for tile in range(9):
                for row in range(9):
                    parts = [
                        total[tile, pl.ds(288 * high + first + row, 8, stride=9), :]
                        for high in range(2)
                    ]
                    out[16 * row : 16 * row + 16, 128 * tile : 128 * tile + 128] = (
                        jnp.concatenate(parts).astype(out.dtype)
                    )

    @pl.when(my_core() == 1)
    def _():
        for steps, out in outs:
            first = 9 * ((index + steps) & 3)
            for tile in range(9):
                for row in range(9):
                    part = total[tile, pl.ds(first + row, 16, stride=36), :]
                    out[16 * row : 16 * row + 16, 128 * tile : 128 * tile + 128] = part.astype(
                        out.dtype
                    )


def cut_terms(*parts):
    return pl.pallas_call(
        cut_terms_kernel,
        in_specs=[IN_VMEM] * 5,
        out_specs=[IN_VMEM] * 4,
        out_shape=[jax.ShapeDtypeStruct((ROWS, WIDTH), f32)]
        + [jax.ShapeDtypeStruct((ROWS, WIDTH), bf16)] * 3,
        scratch_shapes=[pltpu.VMEM((9, HALF, 128), f32)],
        compiler_params=params(),
        name="cut_terms",
    )(*parts)


def ring_sum_kernel(mine, two, one, three, out, eights, ninth):
    ninth[...] = jnp.zeros(ninth.shape, f32)
    for tile in range(9):
        lanes = slice(128 * tile, 128 * tile + 128)
        value = mine[:, lanes]
        for part in (two, one, three):
            value = value + part[:, lanes].astype(f32)
        for row in range(8):
            eights[tile, pl.ds(row, 16, stride=8), :] = value[16 * row : 16 * row + 16]
        ninth[tile // 8, pl.ds(tile % 8, 16, stride=8), :] = value[128:]
        out[:, lanes] = eights[tile].astype(bf16)
    out[:, WIDTH : WIDTH + 128] = ninth[0].astype(bf16)
    out[:, WIDTH + 128 :] = ninth[1].astype(bf16)


def ring_sum(*parts):
    return pl.pallas_call(
        ring_sum_kernel,
        out_shape=jax.ShapeDtypeStruct((128, SLAB), bf16),
        scratch_shapes=[pltpu.VMEM((9, 128, 128), f32), pltpu.VMEM((2, 128, 128), f32)],
        compiler_params=params(),
        name="ring_sum",
    )(*parts)


def last_sum_kernel(pieces, out):
    total = jnp.zeros((16, SLAB), f32)
    for step in range(8):
        total = total + pieces[16 * step : 16 * step + 16, :].astype(f32)
    total = total[:8] + total[8:]
    out[:8, :] = total[:, :WIDTH]
    for tile in range(9):
        sublane, lane = tile % 8, WIDTH + 128 * (tile // 8)
        out[8:9, 128 * tile : 128 * tile + 128] = total[sublane : sublane + 1, lane : lane + 128]


def last_sum(pieces):
    return pl.pallas_call(
        last_sum_kernel,
        out_shape=jax.ShapeDtypeStruct((9, WIDTH), f32),
        compiler_params=params(),
        name="last_sum",
    )(pieces)


def ring(value, axis):
    return [send(value, axis(steps)) for steps in (2, 1, 3)]


def per_device(features, text_emb, proj_w, log_scale, bias):
    image_ring = ring(features, along_x)
    text, images, scalars = held(text_emb, features, log_scale, bias)
    next_1, opposite, next_3 = (send(text_emb, along_y_or_z(steps)) for steps in (1, 2, 3))
    low, high = normalized(text, next_1, image_ring[0]), normalized(opposite, next_3)
    here, low_later, high_later = joined(images, *image_ring, low, high)
    there = send(here, other_core)
    low_1, high_3 = send(low, along_z_or_y(1)), send(high, along_z_or_y(3))
    high_1, low_3 = send(high_later, along_z_or_y(1)), send(low_later, along_z_or_y(3))
    units, units_f, inverses, turns, marks = zip(
        projected(here, proj_w), projected(there, proj_w)
    )
    low_on, high_on = passed(low_1, high_3, marks[1])
    low_2, high_2 = send(low_on, along_z_or_y(1)), send(high_on, along_z_or_y(3))

    sums = [jax.ShapeDtypeStruct((HALF, WIDTH), f32)] * 2
    totals = wave(
        first_wave_kernel,
        ((0, 0, 288), (1, 0, 224)),
        (scalars, low, high, *units),
        IMAGES,
        sums,
        {},
        "first_wave",
    )
    totals = wave(
        next_wave_kernel,
        ((0, 224, 64), (1, 0, 288), (2, 0, 288), (3, 0, 288), (4, 0, 96)),
        (scalars, high, low_1, high_3, high_1, low_3, *units, *totals),
        IMAGES,
        sums,
        {8: 0, 9: 1},
        "second_wave",
    )
    states = (*units, *totals, *units_f, *inverses)
    texts = jax.ShapeDtypeStruct((768, WIDTH), bf16)
    own_1, sent_1, text = wave(
        last_wave_kernel,
        ((0, 96, 192), (1, 0, 288), (2, 0, 288)),
        (scalars, low_3, low_2, high_2, *states),
        2 * EARLY,
        [
            jax.ShapeDtypeStruct((2 * EARLY, WIDTH), f32),
            jax.ShapeDtypeStruct((2 * EARLY, WIDTH), bf16),
            texts,
        ],
        {},
        "last_wave",
        stacked=False,
    )
    own_2, sent_2 = wave(
        rest_wave_kernel,
        ((0, 0, 768),),
        (scalars, text, *states),
        IMAGES - 2 * EARLY,
        [
            jax.ShapeDtypeStruct((IMAGES - 2 * EARLY, WIDTH), f32),
            jax.ShapeDtypeStruct((IMAGES - 2 * EARLY, WIDTH), bf16),
        ],
        {},
        "rest_wave",
        stacked=False,
    )
    got_1, got_2 = send(sent_1, other_core), send(sent_2, other_core)
    first = first_terms(*turns, own_1, got_1)
    mine, two, one, three = cut_terms(*turns, own_2, got_2, first)
    parts = [send(part, along_z_or_y(steps)) for part, steps in ((two, 2), (one, 1), (three, 3))]
    pieces = ring_sum(mine, *parts)
    pieces = lax.all_to_all(pieces, AXIS, 0, 0, axis_index_groups=LAST_GROUPS, tiled=True)
    return last_sum(pieces)


def solution(mesh):
    flat = Mesh(mesh.devices.reshape(-1), (AXIS,))
    rows = P(AXIS, None)
    return jax.shard_map(
        per_device,
        mesh=flat,
        in_specs=(rows, rows, P(), P(), P()),
        out_specs=rows,
        check_vma=False,
    )
```

```python
import jax
import jax.numpy as jnp
from jax import lax
from jax.experimental import pallas as pl
from jax.experimental.pallas import tpu as pltpu
from jax.sharding import Mesh, PartitionSpec as P

epsilon = 1e-06
bf16 = jnp.bfloat16
f32 = jnp.float32

AXIS = "d"
ROWS = 144
WIDTH = 1152
HALF = 4 * ROWS
IMAGES = 2 * HALF
TURNED = 512
EARLY = 384
SLAB = 1408
VMEM_LIMIT = 20 << 20
WORK = 12_000_000_000
PROJ = 20_000_000_000
W1 = 30_000_000_000
WAVES = {"first_wave": W1, "second_wave": 1000, "last_wave": 1000, "rest_wave": 1000}
HOLD = 12_000_000_000
NORM = 6_000_000_000
KEEP = 1000
MARK = jax.ShapeDtypeStruct((8, 128), f32)


def place(index):
    y, xl, z = index & 3, (index >> 2) & 1, (index >> 3) & 3
    core, xh = (index >> 5) & 1, (index >> 6) & 1
    return 2 * xh + xl, y, z, core


def index_of(x, y, z, core):
    return (x >> 1) * 64 + core * 32 + z * 8 + (x & 1) * 4 + y


def send(value, target):
    pairs = [(source, index_of(*target(*place(source)))) for source in range(128)]
    return lax.ppermute(value, AXIS, pairs)


def along_x(steps):
    return lambda x, y, z, core: ((x + steps) % 4, y, z, core)


def along_y_or_z(steps):
    return lambda x, y, z, core: (
        (x, y, (z + steps) % 4, core) if core else (x, (y + steps) % 4, z, core)
    )


def along_z_or_y(steps):
    return lambda x, y, z, core: (
        (x, (y + steps) % 4, z, core) if core else (x, y, (z + steps) % 4, core)
    )


def other_core(x, y, z, core):
    return (x, y, z, 1 - core)


LAST_GROUPS = [
    [index_of(2 * xh + xl, y, z, 0) for xh in range(2) for xl in range(2) for y in range(4)]
    for z in range(4)
] + [
    [index_of(2 * xh + xl, y, z, 1) for xh in range(2) for z in range(4) for xl in range(2)]
    for y in range(4)
]


def my_core():
    return (lax.axis_index(AXIS) >> 5) & 1


IN_VMEM = pl.BlockSpec(memory_space=pltpu.VMEM)
IN_SMEM = pl.BlockSpec(memory_space=pltpu.SMEM)


def params():
    return pltpu.CompilerParams(vmem_limit_bytes=VMEM_LIMIT)


def cost(flops, bytes_accessed):
    return pl.CostEstimate(flops=flops, bytes_accessed=bytes_accessed, transcendentals=0)


def begin(pairs, sems, first=0):
    copies = [
        pltpu.make_async_copy(source, target, sems.at[first + slot])
        for slot, (source, target) in enumerate(pairs)
    ]
    for copy in copies:
        copy.start()
    return copies


def finish(copies):
    for copy in copies:
        copy.wait()


def stack(cuts, refs, target):
    offset = 0
    for which, start, rows in cuts:
        target[offset : offset + rows, :] = refs[which][start : start + rows, :]
        offset += rows


def keep_kernel(text, after, held):
    held[...] = text[...]


def kept(text, after):
    return pl.pallas_call(
        keep_kernel,
        in_specs=[IN_VMEM] * 2,
        out_specs=IN_VMEM,
        out_shape=jax.ShapeDtypeStruct((ROWS, WIDTH), bf16),
        compiler_params=params(),
        cost_estimate=cost(KEEP, 0),
        name="hold_text",
    )(text, after)


def hold_kernel(features, log_scale, bias, after, features_held, scalars):
    features_held[...] = features[...]
    scalars[0:1, :] = jnp.full((1, 128), log_scale[0], f32)
    scalars[1:2, :] = jnp.full((1, 128), bias[0], f32)


def held(*arrays):
    return pl.pallas_call(
        hold_kernel,
        in_specs=[IN_VMEM] + [IN_SMEM] * 2 + [IN_VMEM],
        out_specs=[IN_VMEM] * 2,
        out_shape=[jax.ShapeDtypeStruct((ROWS, WIDTH), bf16), MARK],
        compiler_params=params(),
        cost_estimate=cost(HOLD, 0),
        name="hold",
    )(*arrays)


def normalize_kernel(upper, lower, *refs):
    unit = refs[-1]
    for slot, part in enumerate((upper, lower)):
        values = part[...].astype(f32)
        inverse = lax.rsqrt(jnp.sum(values * values, axis=1, keepdims=True) + epsilon)
        unit[ROWS * slot : ROWS * slot + ROWS, :] = (values * inverse).astype(bf16)


def normalized(*parts):
    return pl.pallas_call(
        normalize_kernel,
        in_specs=[IN_VMEM] * len(parts),
        out_specs=IN_VMEM,
        out_shape=jax.ShapeDtypeStruct((HALF // 2, WIDTH), bf16),
        compiler_params=params(),
        cost_estimate=cost(NORM, 0),
        name="normalize_texts",
    )(*parts)


def join_kernel(own, opposite, next_1, next_3, low, high, joined, low_later, high_later):
    for slot, part in enumerate((own, opposite, next_1, next_3)):
        joined[ROWS * slot : ROWS * slot + ROWS, :] = part[...]
    low_later[...] = low[...]
    high_later[...] = high[...]


def joined(*parts):
    return pl.pallas_call(
        join_kernel,
        in_specs=[IN_VMEM] * 6,
        out_specs=[IN_VMEM] * 3,
        out_shape=[jax.ShapeDtypeStruct((HALF, WIDTH), bf16)]
        + [jax.ShapeDtypeStruct((HALF // 2, WIDTH), bf16)] * 2,
        compiler_params=params(),
        cost_estimate=cost(WORK, 0),
        name="join",
    )(*parts)


def pass_kernel(low, high, after, low_on, high_on):
    low_on[...] = low[...]
    high_on[...] = high[...]


def passed(*parts):
    return pl.pallas_call(
        pass_kernel,
        in_specs=[IN_VMEM] * 3,
        out_specs=[IN_VMEM] * 2,
        out_shape=[jax.ShapeDtypeStruct((HALF // 2, WIDTH), bf16)] * 2,
        compiler_params=params(),
        name="pass_on",
    )(*parts)


def project_kernel(images, proj, unit, unit_f, inverse, turned, mark):
    mark[...] = jnp.zeros(mark.shape, f32)
    emb = jnp.dot(images[...], proj[...], preferred_element_type=f32)
    inv = lax.rsqrt(jnp.sum(emb * emb, axis=1, keepdims=True) + epsilon)
    emb = emb * inv
    unit_f[...] = emb
    inverse[...] = jnp.broadcast_to(inv, inverse.shape)
    unit[...] = emb.astype(bf16)
    turned[...] = images[...].T


def projected(images, proj_w):
    return pl.pallas_call(
        project_kernel,
        in_specs=[IN_VMEM] * 2,
        out_specs=[IN_VMEM] * 5,
        out_shape=[
            jax.ShapeDtypeStruct((HALF, WIDTH), bf16),
            jax.ShapeDtypeStruct((HALF, WIDTH), f32),
            jax.ShapeDtypeStruct((HALF, 128), f32),
            jax.ShapeDtypeStruct((WIDTH, HALF), bf16),
            MARK,
        ],
        compiler_params=params(),
        cost_estimate=cost(PROJ, 0),
        name="project_images",
    )(images, proj_w)


def wave_body(blocks, text, scalars, sim, weights, diagonal, take):
    half = 0.5 * jnp.exp(scalars[0:1, 0:1])
    half_shift = 0.5 * scalars[1:2, 0:1]
    rows, offset = [], 0
    for unit, start, count in blocks:
        rows.append(slice(offset, offset + count))
        offset += count
    for which, (unit, start, count) in enumerate(blocks):
        sim[rows[which], :] = lax.dot_general(
            unit[start : start + count, :],
            text[...],
            (((1,), (1,)), ((), ())),
            preferred_element_type=f32,
        )
        weights[rows[which], :] = (
            half + half * jnp.tanh(half * sim[rows[which], :] + half_shift)
        ).astype(bf16)
        if diagonal and which == 0:
            tanh = jnp.tanh(half * sim[:ROWS, :256] + half_shift)
            row = lax.broadcasted_iota(jnp.int32, (ROWS, 256), 0)
            column = lax.broadcasted_iota(jnp.int32, (ROWS, 256), 1)
            pair = jnp.where(row == column, half * tanh - half, half + half * tanh)
            weights[:ROWS, :256] = pair.astype(bf16)
    for which in range(len(blocks)):
        take(which, jnp.dot(weights[rows[which], :], text[...], preferred_element_type=f32))


def first_wave_kernel(cuts, scalars, low, high, unit_a, unit_b, total_a, total_b, text, sim, weights):
    stack(cuts, (low, high), text)
    totals = (total_a, total_b)

    def take(which, product):
        totals[which][...] = product

    blocks = ((unit_a, 0, HALF), (unit_b, 0, HALF))
    wave_body(blocks, text, scalars, sim, weights, True, take)


def next_wave_kernel(cuts, scalars, *refs):
    count = len(refs) - 9
    texts, (unit_a, unit_b), before, totals = (
        refs[:count],
        refs[count : count + 2],
        refs[count + 2 : count + 4],
        refs[count + 4 : count + 6],
    )
    text, sim, weights = refs[count + 6 :]
    stack(cuts, texts, text)

    def take(which, product):
        totals[which][...] = before[which][...] + product

    blocks = ((unit_a, 0, HALF), (unit_b, 0, HALF))
    wave_body(blocks, text, scalars, sim, weights, False, take)


def project_gradient(start, count, scalars, text, states, projected_f, projected_b, sim, weights):
    units, totals, units_f, inverses = (states[2 * slot : 2 * slot + 2] for slot in range(4))
    rows = slice(start, start + count)

    def take(which, product):
        gradient = totals[which][rows, :] + product
        image = units_f[which][rows, :]
        along = jnp.sum(image * gradient, axis=1, keepdims=True)
        projection = (gradient - image * along) * inverses[which][rows, 0:1]
        out = slice(which * count, which * count + count)
        projected_f[out, :] = projection
        projected_b[out, :] = projection.astype(bf16)

    blocks = tuple((unit, start, count) for unit in units)
    wave_body(blocks, text, scalars, sim, weights, False, take)


def last_wave_kernel(cuts, scalars, *refs):
    count = len(refs) - 13
    projected_f, projected_b, text, sim, weights = refs[count + 8 :]
    stack(cuts, refs[:count], text)
    project_gradient(
        0, EARLY, scalars, text, refs[count : count + 8], projected_f, projected_b, sim, weights
    )


def rest_wave_kernel(cuts, scalars, text, *refs):
    project_gradient(EARLY, HALF - EARLY, scalars, text, refs[:8], *refs[8:])


def wave(kernel, cuts, operands, images, out_shape, aliases, name, stacked=True):
    rows = sum(cut[2] for cut in cuts)
    return pl.pallas_call(
        lambda *refs: kernel(cuts, *refs),
        in_specs=[IN_VMEM] * len(operands),
        out_specs=[IN_VMEM] * len(out_shape),
        out_shape=out_shape,
        input_output_aliases=aliases,
        scratch_shapes=[pltpu.VMEM((rows, WIDTH), bf16)] * stacked
        + [pltpu.VMEM((images, rows), f32), pltpu.VMEM((images, rows), bf16)],
        compiler_params=params(),
        cost_estimate=cost(WAVES[name], 0),
        name=name,
    )(*operands)


def chip_projection(projected_f, other, count):
    return [
        (projected_f[first : first + count, :] + other[count - first : 2 * count - first, :].astype(f32)).astype(bf16)
        for first in (0, count)
    ]


def my_rows(high):
    return pl.ds(pl.multiple_of(576 * high + 288 * my_core(), 16), 288)


def first_terms_kernel(turned_a, turned_b, projected_f, other, out):
    both = jnp.concatenate(chip_projection(projected_f, other, EARLY))
    for high in range(2):
        left = jnp.concatenate([turned[my_rows(high), :EARLY] for turned in (turned_a, turned_b)], axis=1)
        out[288 * high : 288 * high + 288, :] = jnp.dot(left, both, preferred_element_type=f32)


def first_terms(*parts):
    return pl.pallas_call(
        first_terms_kernel,
        in_specs=[IN_VMEM] * 4,
        out_specs=IN_VMEM,
        out_shape=jax.ShapeDtypeStruct((HALF, WIDTH), f32),
        compiler_params=params(),
        cost_estimate=cost(1000, 1000),
        name="first_terms",
    )(*parts)


def cut_terms_kernel(turned_a, turned_b, projected_f, other, first, mine, two, one, three, total):
    both_a, both_b = chip_projection(projected_f, other, HALF - EARLY)
    for high in range(2):
        rows = slice(288 * high, 288 * high + 288)
        term = first[rows, :]
        for turned, both in ((turned_a, both_a), (turned_b, both_b)):
            term = term + jnp.dot(turned[my_rows(high), EARLY:], both, preferred_element_type=f32)
        for tile in range(9):
            total[tile, rows, :] = term[:, 128 * tile : 128 * tile + 128]
    index = lax.axis_index(AXIS)
    outs = ((0, mine), (2, two), (1, one), (3, three))

    @pl.when(my_core() == 0)
    def _():
        for steps, out in outs:
            first = 72 * (((index >> 3) + steps) & 3)
            for tile in range(9):
                for row in range(9):
                    parts = [
                        total[tile, pl.ds(288 * high + first + row, 8, stride=9), :]
                        for high in range(2)
                    ]
                    out[16 * row : 16 * row + 16, 128 * tile : 128 * tile + 128] = (
                        jnp.concatenate(parts).astype(out.dtype)
                    )

    @pl.when(my_core() == 1)
    def _():
        for steps, out in outs:
            first = 9 * ((index + steps) & 3)
            for tile in range(9):
                for row in range(9):
                    part = total[tile, pl.ds(first + row, 16, stride=36), :]
                    out[16 * row : 16 * row + 16, 128 * tile : 128 * tile + 128] = part.astype(
                        out.dtype
                    )


def cut_terms(*parts):
    return pl.pallas_call(
        cut_terms_kernel,
        in_specs=[IN_VMEM] * 5,
        out_specs=[IN_VMEM] * 4,
        out_shape=[jax.ShapeDtypeStruct((ROWS, WIDTH), f32)]
        + [jax.ShapeDtypeStruct((ROWS, WIDTH), bf16)] * 3,
        scratch_shapes=[pltpu.VMEM((9, HALF, 128), f32)],
        compiler_params=params(),
        name="cut_terms",
    )(*parts)


def ring_sum_kernel(mine, two, one, three, out, eights, ninth):
    ninth[...] = jnp.zeros(ninth.shape, f32)
    for tile in range(9):
        lanes = slice(128 * tile, 128 * tile + 128)
        value = mine[:, lanes]
        for part in (two, one, three):
            value = value + part[:, lanes].astype(f32)
        for row in range(8):
            eights[tile, pl.ds(row, 16, stride=8), :] = value[16 * row : 16 * row + 16]
        ninth[tile // 8, pl.ds(tile % 8, 16, stride=8), :] = value[128:]
        out[:, lanes] = eights[tile].astype(bf16)
    out[:, WIDTH : WIDTH + 128] = ninth[0].astype(bf16)
    out[:, WIDTH + 128 :] = ninth[1].astype(bf16)


def ring_sum(*parts):
    return pl.pallas_call(
        ring_sum_kernel,
        out_shape=jax.ShapeDtypeStruct((128, SLAB), bf16),
        scratch_shapes=[pltpu.VMEM((9, 128, 128), f32), pltpu.VMEM((2, 128, 128), f32)],
        compiler_params=params(),
        name="ring_sum",
    )(*parts)


def last_sum_kernel(pieces, out):
    total = jnp.zeros((16, SLAB), f32)
    for step in range(8):
        total = total + pieces[16 * step : 16 * step + 16, :].astype(f32)
    total = total[:8] + total[8:]
    out[:8, :] = total[:, :WIDTH]
    for tile in range(9):
        sublane, lane = tile % 8, WIDTH + 128 * (tile // 8)
        out[8:9, 128 * tile : 128 * tile + 128] = total[sublane : sublane + 1, lane : lane + 128]


def last_sum(pieces):
    return pl.pallas_call(
        last_sum_kernel,
        out_shape=jax.ShapeDtypeStruct((9, WIDTH), f32),
        compiler_params=params(),
        name="last_sum",
    )(pieces)


def ring(value, axis):
    return [send(value, axis(steps)) for steps in (2, 1, 3)]


def per_device(features, text_emb, proj_w, log_scale, bias):
    image_ring = ring(features, along_x)
    next_1, next_3 = (send(text_emb, along_y_or_z(steps)) for steps in (1, 3))
    text = kept(text_emb, next_1)
    opposite = send(text, along_y_or_z(2))
    low, high = normalized(text, next_1), normalized(opposite, next_3)
    images, scalars = held(features, log_scale, bias, high)
    here, low_later, high_later = joined(images, *image_ring, low, high)
    there = send(here, other_core)
    low_1, high_3 = send(low, along_z_or_y(1)), send(high, along_z_or_y(3))
    high_1, low_3 = send(high_later, along_z_or_y(1)), send(low_later, along_z_or_y(3))
    units, units_f, inverses, turns, marks = zip(
        projected(here, proj_w), projected(there, proj_w)
    )
    low_on, high_on = passed(low_1, high_3, marks[1])
    low_2, high_2 = send(low_on, along_z_or_y(1)), send(high_on, along_z_or_y(3))

    sums = [jax.ShapeDtypeStruct((HALF, WIDTH), f32)] * 2
    totals = wave(
        first_wave_kernel,
        ((0, 0, 288), (1, 0, 224)),
        (scalars, low, high, *units),
        IMAGES,
        sums,
        {},
        "first_wave",
    )
    totals = wave(
        next_wave_kernel,
        ((0, 224, 64), (1, 0, 288), (2, 0, 288), (3, 0, 288), (4, 0, 96)),
        (scalars, high, low_1, high_3, high_1, low_3, *units, *totals),
        IMAGES,
        sums,
        {8: 0, 9: 1},
        "second_wave",
    )
    states = (*units, *totals, *units_f, *inverses)
    texts = jax.ShapeDtypeStruct((768, WIDTH), bf16)
    own_1, sent_1, text = wave(
        last_wave_kernel,
        ((0, 96, 192), (1, 0, 288), (2, 0, 288)),
        (scalars, low_3, low_2, high_2, *states),
        2 * EARLY,
        [
            jax.ShapeDtypeStruct((2 * EARLY, WIDTH), f32),
            jax.ShapeDtypeStruct((2 * EARLY, WIDTH), bf16),
            texts,
        ],
        {},
        "last_wave",
        stacked=False,
    )
    own_2, sent_2 = wave(
        rest_wave_kernel,
        ((0, 0, 768),),
        (scalars, text, *states),
        IMAGES - 2 * EARLY,
        [
            jax.ShapeDtypeStruct((IMAGES - 2 * EARLY, WIDTH), f32),
            jax.ShapeDtypeStruct((IMAGES - 2 * EARLY, WIDTH), bf16),
        ],
        {},
        "rest_wave",
        stacked=False,
    )
    got_1, got_2 = send(sent_1, other_core), send(sent_2, other_core)
    first = first_terms(*turns, own_1, got_1)
    mine, two, one, three = cut_terms(*turns, own_2, got_2, first)
    parts = [send(part, along_z_or_y(steps)) for part, steps in ((two, 2), (one, 1), (three, 3))]
    pieces = ring_sum(mine, *parts)
    pieces = lax.all_to_all(pieces, AXIS, 0, 0, axis_index_groups=LAST_GROUPS, tiled=True)
    return last_sum(pieces)


def solution(mesh):
    flat = Mesh(mesh.devices.reshape(-1), (AXIS,))
    rows = P(AXIS, None)
    return jax.shard_map(
        per_device,
        mesh=flat,
        in_specs=(rows, rows, P(), P(), P()),
        out_specs=rows,
        check_vma=False,
    )
```

```python
import jax
import jax.numpy as jnp
from jax import lax
from jax.experimental import pallas as pl
from jax.experimental.pallas import tpu as pltpu
from jax.sharding import Mesh, PartitionSpec as P

epsilon = 1e-06
bf16 = jnp.bfloat16
f32 = jnp.float32

AXIS = "d"
ROWS = 144
WIDTH = 1152
HALF = 4 * ROWS
IMAGES = 2 * HALF
TURNED = 512
EARLY = 384
SLAB = 1408
VMEM_LIMIT = 20 << 20
WORK = 12_000_000_000
PROJ = 20_000_000_000
W1 = 30_000_000_000
WAVES = {"first_wave": W1, "second_wave": 1000, "last_wave": 1000, "rest_wave": 1000}
HOLD = 12_000_000_000
NORM = 1000
KEEP = 1000
MARK = jax.ShapeDtypeStruct((8, 128), f32)


def place(index):
    y, xl, z = index & 3, (index >> 2) & 1, (index >> 3) & 3
    core, xh = (index >> 5) & 1, (index >> 6) & 1
    return 2 * xh + xl, y, z, core


def index_of(x, y, z, core):
    return (x >> 1) * 64 + core * 32 + z * 8 + (x & 1) * 4 + y


def send(value, target):
    pairs = [(source, index_of(*target(*place(source)))) for source in range(128)]
    return lax.ppermute(value, AXIS, pairs)


def along_x(steps):
    return lambda x, y, z, core: ((x + steps) % 4, y, z, core)


def along_y_or_z(steps):
    return lambda x, y, z, core: (
        (x, y, (z + steps) % 4, core) if core else (x, (y + steps) % 4, z, core)
    )


def along_z_or_y(steps):
    return lambda x, y, z, core: (
        (x, (y + steps) % 4, z, core) if core else (x, y, (z + steps) % 4, core)
    )


def other_core(x, y, z, core):
    return (x, y, z, 1 - core)


LAST_GROUPS = [
    [index_of(2 * xh + xl, y, z, 0) for xh in range(2) for xl in range(2) for y in range(4)]
    for z in range(4)
] + [
    [index_of(2 * xh + xl, y, z, 1) for xh in range(2) for z in range(4) for xl in range(2)]
    for y in range(4)
]


def my_core():
    return (lax.axis_index(AXIS) >> 5) & 1


IN_VMEM = pl.BlockSpec(memory_space=pltpu.VMEM)
IN_SMEM = pl.BlockSpec(memory_space=pltpu.SMEM)


def params():
    return pltpu.CompilerParams(vmem_limit_bytes=VMEM_LIMIT)


def cost(flops, bytes_accessed):
    return pl.CostEstimate(flops=flops, bytes_accessed=bytes_accessed, transcendentals=0)


def begin(pairs, sems, first=0):
    copies = [
        pltpu.make_async_copy(source, target, sems.at[first + slot])
        for slot, (source, target) in enumerate(pairs)
    ]
    for copy in copies:
        copy.start()
    return copies


def finish(copies):
    for copy in copies:
        copy.wait()


def stack(cuts, refs, target):
    offset = 0
    for which, start, rows in cuts:
        target[offset : offset + rows, :] = refs[which][start : start + rows, :]
        offset += rows


def keep_kernel(text, held):
    held[...] = text[...]


def kept(text):
    return pl.pallas_call(
        keep_kernel,
        in_specs=[IN_VMEM],
        out_specs=IN_VMEM,
        out_shape=jax.ShapeDtypeStruct((ROWS, WIDTH), bf16),
        compiler_params=params(),
        cost_estimate=cost(KEEP, 0),
        name="hold_text",
    )(text)


def hold_kernel(features, log_scale, bias, after, features_held, scalars):
    features_held[...] = features[...]
    scalars[0:1, :] = jnp.full((1, 128), log_scale[0], f32)
    scalars[1:2, :] = jnp.full((1, 128), bias[0], f32)


def held(*arrays):
    return pl.pallas_call(
        hold_kernel,
        in_specs=[IN_VMEM] + [IN_SMEM] * 2 + [IN_VMEM],
        out_specs=[IN_VMEM] * 2,
        out_shape=[jax.ShapeDtypeStruct((ROWS, WIDTH), bf16), MARK],
        compiler_params=params(),
        cost_estimate=cost(HOLD, 0),
        name="hold",
    )(*arrays)


def normalize_kernel(upper, lower, *refs):
    unit = refs[-1]
    for slot, part in enumerate((upper, lower)):
        values = part[...].astype(f32)
        inverse = lax.rsqrt(jnp.sum(values * values, axis=1, keepdims=True) + epsilon)
        unit[ROWS * slot : ROWS * slot + ROWS, :] = (values * inverse).astype(bf16)


def normalized(*parts):
    return pl.pallas_call(
        normalize_kernel,
        in_specs=[IN_VMEM] * len(parts),
        out_specs=IN_VMEM,
        out_shape=jax.ShapeDtypeStruct((HALF // 2, WIDTH), bf16),
        compiler_params=params(),
        cost_estimate=cost(NORM, 0),
        name="normalize_texts",
    )(*parts)


def join_kernel(own, opposite, next_1, next_3, low, high, joined, low_later, high_later):
    for slot, part in enumerate((own, opposite, next_1, next_3)):
        joined[ROWS * slot : ROWS * slot + ROWS, :] = part[...]
    low_later[...] = low[...]
    high_later[...] = high[...]


def joined(*parts):
    return pl.pallas_call(
        join_kernel,
        in_specs=[IN_VMEM] * 6,
        out_specs=[IN_VMEM] * 3,
        out_shape=[jax.ShapeDtypeStruct((HALF, WIDTH), bf16)]
        + [jax.ShapeDtypeStruct((HALF // 2, WIDTH), bf16)] * 2,
        compiler_params=params(),
        cost_estimate=cost(WORK, 0),
        name="join",
    )(*parts)


def pass_kernel(low, high, after, low_on, high_on):
    low_on[...] = low[...]
    high_on[...] = high[...]


def passed(*parts):
    return pl.pallas_call(
        pass_kernel,
        in_specs=[IN_VMEM] * 3,
        out_specs=[IN_VMEM] * 2,
        out_shape=[jax.ShapeDtypeStruct((HALF // 2, WIDTH), bf16)] * 2,
        compiler_params=params(),
        name="pass_on",
    )(*parts)


def project_kernel(images, proj, unit, unit_f, inverse, turned, mark):
    mark[...] = jnp.zeros(mark.shape, f32)
    emb = jnp.dot(images[...], proj[...], preferred_element_type=f32)
    inv = lax.rsqrt(jnp.sum(emb * emb, axis=1, keepdims=True) + epsilon)
    emb = emb * inv
    unit_f[...] = emb
    inverse[...] = jnp.broadcast_to(inv, inverse.shape)
    unit[...] = emb.astype(bf16)
    turned[...] = images[...].T


def projected(images, proj_w):
    return pl.pallas_call(
        project_kernel,
        in_specs=[IN_VMEM] * 2,
        out_specs=[IN_VMEM] * 5,
        out_shape=[
            jax.ShapeDtypeStruct((HALF, WIDTH), bf16),
            jax.ShapeDtypeStruct((HALF, WIDTH), f32),
            jax.ShapeDtypeStruct((HALF, 128), f32),
            jax.ShapeDtypeStruct((WIDTH, HALF), bf16),
            MARK,
        ],
        compiler_params=params(),
        cost_estimate=cost(PROJ, 0),
        name="project_images",
    )(images, proj_w)


def wave_body(blocks, text, scalars, sim, weights, diagonal, take):
    half = 0.5 * jnp.exp(scalars[0:1, 0:1])
    half_shift = 0.5 * scalars[1:2, 0:1]
    rows, offset = [], 0
    for unit, start, count in blocks:
        rows.append(slice(offset, offset + count))
        offset += count
    for which, (unit, start, count) in enumerate(blocks):
        sim[rows[which], :] = lax.dot_general(
            unit[start : start + count, :],
            text[...],
            (((1,), (1,)), ((), ())),
            preferred_element_type=f32,
        )
        weights[rows[which], :] = (
            half + half * jnp.tanh(half * sim[rows[which], :] + half_shift)
        ).astype(bf16)
        if diagonal and which == 0:
            tanh = jnp.tanh(half * sim[:ROWS, :256] + half_shift)
            row = lax.broadcasted_iota(jnp.int32, (ROWS, 256), 0)
            column = lax.broadcasted_iota(jnp.int32, (ROWS, 256), 1)
            pair = jnp.where(row == column, half * tanh - half, half + half * tanh)
            weights[:ROWS, :256] = pair.astype(bf16)
    for which in range(len(blocks)):
        take(which, jnp.dot(weights[rows[which], :], text[...], preferred_element_type=f32))


def first_wave_kernel(cuts, scalars, low, high, unit_a, unit_b, total_a, total_b, text, sim, weights):
    stack(cuts, (low, high), text)
    totals = (total_a, total_b)

    def take(which, product):
        totals[which][...] = product

    blocks = ((unit_a, 0, HALF), (unit_b, 0, HALF))
    wave_body(blocks, text, scalars, sim, weights, True, take)


def next_wave_kernel(cuts, scalars, *refs):
    count = len(refs) - 9
    texts, (unit_a, unit_b), before, totals = (
        refs[:count],
        refs[count : count + 2],
        refs[count + 2 : count + 4],
        refs[count + 4 : count + 6],
    )
    text, sim, weights = refs[count + 6 :]
    stack(cuts, texts, text)

    def take(which, product):
        totals[which][...] = before[which][...] + product

    blocks = ((unit_a, 0, HALF), (unit_b, 0, HALF))
    wave_body(blocks, text, scalars, sim, weights, False, take)


def project_gradient(start, count, scalars, text, states, projected_f, projected_b, sim, weights):
    units, totals, units_f, inverses = (states[2 * slot : 2 * slot + 2] for slot in range(4))
    rows = slice(start, start + count)

    def take(which, product):
        gradient = totals[which][rows, :] + product
        image = units_f[which][rows, :]
        along = jnp.sum(image * gradient, axis=1, keepdims=True)
        projection = (gradient - image * along) * inverses[which][rows, 0:1]
        out = slice(which * count, which * count + count)
        projected_f[out, :] = projection
        projected_b[out, :] = projection.astype(bf16)

    blocks = tuple((unit, start, count) for unit in units)
    wave_body(blocks, text, scalars, sim, weights, False, take)


def last_wave_kernel(cuts, scalars, *refs):
    count = len(refs) - 13
    projected_f, projected_b, text, sim, weights = refs[count + 8 :]
    stack(cuts, refs[:count], text)
    project_gradient(
        0, EARLY, scalars, text, refs[count : count + 8], projected_f, projected_b, sim, weights
    )


def rest_wave_kernel(cuts, scalars, text, *refs):
    project_gradient(EARLY, HALF - EARLY, scalars, text, refs[:8], *refs[8:])


def wave(kernel, cuts, operands, images, out_shape, aliases, name, stacked=True):
    rows = sum(cut[2] for cut in cuts)
    return pl.pallas_call(
        lambda *refs: kernel(cuts, *refs),
        in_specs=[IN_VMEM] * len(operands),
        out_specs=[IN_VMEM] * len(out_shape),
        out_shape=out_shape,
        input_output_aliases=aliases,
        scratch_shapes=[pltpu.VMEM((rows, WIDTH), bf16)] * stacked
        + [pltpu.VMEM((images, rows), f32), pltpu.VMEM((images, rows), bf16)],
        compiler_params=params(),
        cost_estimate=cost(WAVES[name], 0),
        name=name,
    )(*operands)


def chip_projection(projected_f, other, count):
    return [
        (projected_f[first : first + count, :] + other[count - first : 2 * count - first, :].astype(f32)).astype(bf16)
        for first in (0, count)
    ]


def my_rows(high):
    return pl.ds(pl.multiple_of(576 * high + 288 * my_core(), 16), 288)


def first_terms_kernel(turned_a, turned_b, projected_f, other, out):
    both = jnp.concatenate(chip_projection(projected_f, other, EARLY))
    for high in range(2):
        left = jnp.concatenate([turned[my_rows(high), :EARLY] for turned in (turned_a, turned_b)], axis=1)
        out[288 * high : 288 * high + 288, :] = jnp.dot(left, both, preferred_element_type=f32)


def first_terms(*parts):
    return pl.pallas_call(
        first_terms_kernel,
        in_specs=[IN_VMEM] * 4,
        out_specs=IN_VMEM,
        out_shape=jax.ShapeDtypeStruct((HALF, WIDTH), f32),
        compiler_params=params(),
        cost_estimate=cost(1000, 1000),
        name="first_terms",
    )(*parts)


def cut_terms_kernel(turned_a, turned_b, projected_f, other, first, mine, two, one, three, total):
    both_a, both_b = chip_projection(projected_f, other, HALF - EARLY)
    for high in range(2):
        rows = slice(288 * high, 288 * high + 288)
        term = first[rows, :]
        for turned, both in ((turned_a, both_a), (turned_b, both_b)):
            term = term + jnp.dot(turned[my_rows(high), EARLY:], both, preferred_element_type=f32)
        for tile in range(9):
            total[tile, rows, :] = term[:, 128 * tile : 128 * tile + 128]
    index = lax.axis_index(AXIS)
    outs = ((0, mine), (2, two), (1, one), (3, three))

    @pl.when(my_core() == 0)
    def _():
        for steps, out in outs:
            first = 72 * (((index >> 3) + steps) & 3)
            for tile in range(9):
                for row in range(9):
                    parts = [
                        total[tile, pl.ds(288 * high + first + row, 8, stride=9), :]
                        for high in range(2)
                    ]
                    out[16 * row : 16 * row + 16, 128 * tile : 128 * tile + 128] = (
                        jnp.concatenate(parts).astype(out.dtype)
                    )

    @pl.when(my_core() == 1)
    def _():
        for steps, out in outs:
            first = 9 * ((index + steps) & 3)
            for tile in range(9):
                for row in range(9):
                    part = total[tile, pl.ds(first + row, 16, stride=36), :]
                    out[16 * row : 16 * row + 16, 128 * tile : 128 * tile + 128] = part.astype(
                        out.dtype
                    )


def cut_terms(*parts):
    return pl.pallas_call(
        cut_terms_kernel,
        in_specs=[IN_VMEM] * 5,
        out_specs=[IN_VMEM] * 4,
        out_shape=[jax.ShapeDtypeStruct((ROWS, WIDTH), f32)]
        + [jax.ShapeDtypeStruct((ROWS, WIDTH), bf16)] * 3,
        scratch_shapes=[pltpu.VMEM((9, HALF, 128), f32)],
        compiler_params=params(),
        name="cut_terms",
    )(*parts)


def ring_sum_kernel(mine, two, one, three, out, eights, ninth):
    ninth[...] = jnp.zeros(ninth.shape, f32)
    for tile in range(9):
        lanes = slice(128 * tile, 128 * tile + 128)
        value = mine[:, lanes]
        for part in (two, one, three):
            value = value + part[:, lanes].astype(f32)
        for row in range(8):
            eights[tile, pl.ds(row, 16, stride=8), :] = value[16 * row : 16 * row + 16]
        ninth[tile // 8, pl.ds(tile % 8, 16, stride=8), :] = value[128:]
        out[:, lanes] = eights[tile].astype(bf16)
    out[:, WIDTH : WIDTH + 128] = ninth[0].astype(bf16)
    out[:, WIDTH + 128 :] = ninth[1].astype(bf16)


def ring_sum(*parts):
    return pl.pallas_call(
        ring_sum_kernel,
        out_shape=jax.ShapeDtypeStruct((128, SLAB), bf16),
        scratch_shapes=[pltpu.VMEM((9, 128, 128), f32), pltpu.VMEM((2, 128, 128), f32)],
        compiler_params=params(),
        name="ring_sum",
    )(*parts)


def last_sum_kernel(pieces, out):
    total = jnp.zeros((16, SLAB), f32)
    for step in range(8):
        total = total + pieces[16 * step : 16 * step + 16, :].astype(f32)
    total = total[:8] + total[8:]
    out[:8, :] = total[:, :WIDTH]
    for tile in range(9):
        sublane, lane = tile % 8, WIDTH + 128 * (tile // 8)
        out[8:9, 128 * tile : 128 * tile + 128] = total[sublane : sublane + 1, lane : lane + 128]


def last_sum(pieces):
    return pl.pallas_call(
        last_sum_kernel,
        out_shape=jax.ShapeDtypeStruct((9, WIDTH), f32),
        compiler_params=params(),
        name="last_sum",
    )(pieces)


def ring(value, axis):
    return [send(value, axis(steps)) for steps in (2, 1, 3)]


def per_device(features, text_emb, proj_w, log_scale, bias):
    image_ring = ring(features, along_x)
    next_1, opposite, next_3 = (send(text_emb, along_y_or_z(steps)) for steps in (1, 2, 3))
    low = normalized(kept(text_emb), next_1, image_ring[0])
    high = normalized(opposite, next_3)
    images, scalars = held(features, log_scale, bias, high)
    here, low_later, high_later = joined(images, *image_ring, low, high)
    there = send(here, other_core)
    low_1, high_3 = send(low, along_z_or_y(1)), send(high, along_z_or_y(3))
    high_1, low_3 = send(high_later, along_z_or_y(1)), send(low_later, along_z_or_y(3))
    units, units_f, inverses, turns, marks = zip(
        projected(here, proj_w), projected(there, proj_w)
    )
    low_on, high_on = passed(low_1, high_3, marks[1])
    low_2, high_2 = send(low_on, along_z_or_y(1)), send(high_on, along_z_or_y(3))

    sums = [jax.ShapeDtypeStruct((HALF, WIDTH), f32)] * 2
    totals = wave(
        first_wave_kernel,
        ((0, 0, 288), (1, 0, 224)),
        (scalars, low, high, *units),
        IMAGES,
        sums,
        {},
        "first_wave",
    )
    totals = wave(
        next_wave_kernel,
        ((0, 224, 64), (1, 0, 288), (2, 0, 288), (3, 0, 288), (4, 0, 96)),
        (scalars, high, low_1, high_3, high_1, low_3, *units, *totals),
        IMAGES,
        sums,
        {8: 0, 9: 1},
        "second_wave",
    )
    states = (*units, *totals, *units_f, *inverses)
    texts = jax.ShapeDtypeStruct((768, WIDTH), bf16)
    own_1, sent_1, text = wave(
        last_wave_kernel,
        ((0, 96, 192), (1, 0, 288), (2, 0, 288)),
        (scalars, low_3, low_2, high_2, *states),
        2 * EARLY,
        [
            jax.ShapeDtypeStruct((2 * EARLY, WIDTH), f32),
            jax.ShapeDtypeStruct((2 * EARLY, WIDTH), bf16),
            texts,
        ],
        {},
        "last_wave",
        stacked=False,
    )
    own_2, sent_2 = wave(
        rest_wave_kernel,
        ((0, 0, 768),),
        (scalars, text, *states),
        IMAGES - 2 * EARLY,
        [
            jax.ShapeDtypeStruct((IMAGES - 2 * EARLY, WIDTH), f32),
            jax.ShapeDtypeStruct((IMAGES - 2 * EARLY, WIDTH), bf16),
        ],
        {},
        "rest_wave",
        stacked=False,
    )
    got_1, got_2 = send(sent_1, other_core), send(sent_2, other_core)
    first = first_terms(*turns, own_1, got_1)
    mine, two, one, three = cut_terms(*turns, own_2, got_2, first)
    parts = [send(part, along_z_or_y(steps)) for part, steps in ((two, 2), (one, 1), (three, 3))]
    pieces = ring_sum(mine, *parts)
    pieces = lax.all_to_all(pieces, AXIS, 0, 0, axis_index_groups=LAST_GROUPS, tiled=True)
    return last_sum(pieces)


def solution(mesh):
    flat = Mesh(mesh.devices.reshape(-1), (AXIS,))
    rows = P(AXIS, None)
    return jax.shard_map(
        per_device,
        mesh=flat,
        in_specs=(rows, rows, P(), P(), P()),
        out_specs=rows,
        check_vma=False,
    )
```

```python
import jax
import jax.numpy as jnp
from jax import lax
from jax.experimental import pallas as pl
from jax.experimental.pallas import tpu as pltpu
from jax.sharding import Mesh, PartitionSpec as P

epsilon = 1e-06
bf16 = jnp.bfloat16
f32 = jnp.float32

AXIS = "d"
ROWS = 144
WIDTH = 1152
HALF = 4 * ROWS
IMAGES = 2 * HALF
TURNED = 512
EARLY = 384
SLAB = 1408
VMEM_LIMIT = 20 << 20
WORK = 12_000_000_000
PROJ = 20_000_000_000
W1 = 30_000_000_000
WAVES = {"first_wave": W1, "second_wave": 1000, "last_wave": 1000, "rest_wave": 1000}
HOLD = 12_000_000_000
NORM = 1000
KEEP = 1000
MARK = jax.ShapeDtypeStruct((8, 128), f32)


def place(index):
    y, xl, z = index & 3, (index >> 2) & 1, (index >> 3) & 3
    core, xh = (index >> 5) & 1, (index >> 6) & 1
    return 2 * xh + xl, y, z, core


def index_of(x, y, z, core):
    return (x >> 1) * 64 + core * 32 + z * 8 + (x & 1) * 4 + y


def send(value, target):
    pairs = [(source, index_of(*target(*place(source)))) for source in range(128)]
    return lax.ppermute(value, AXIS, pairs)


def along_x(steps):
    return lambda x, y, z, core: ((x + steps) % 4, y, z, core)


def along_y_or_z(steps):
    return lambda x, y, z, core: (
        (x, y, (z + steps) % 4, core) if core else (x, (y + steps) % 4, z, core)
    )


def along_z_or_y(steps):
    return lambda x, y, z, core: (
        (x, (y + steps) % 4, z, core) if core else (x, y, (z + steps) % 4, core)
    )


def other_core(x, y, z, core):
    return (x, y, z, 1 - core)


LAST_GROUPS = [
    [index_of(2 * xh + xl, y, z, 0) for xh in range(2) for xl in range(2) for y in range(4)]
    for z in range(4)
] + [
    [index_of(2 * xh + xl, y, z, 1) for xh in range(2) for z in range(4) for xl in range(2)]
    for y in range(4)
]


def my_core():
    return (lax.axis_index(AXIS) >> 5) & 1


IN_VMEM = pl.BlockSpec(memory_space=pltpu.VMEM)
IN_SMEM = pl.BlockSpec(memory_space=pltpu.SMEM)


def params():
    return pltpu.CompilerParams(vmem_limit_bytes=VMEM_LIMIT)


def cost(flops, bytes_accessed):
    return pl.CostEstimate(flops=flops, bytes_accessed=bytes_accessed, transcendentals=0)


def begin(pairs, sems, first=0):
    copies = [
        pltpu.make_async_copy(source, target, sems.at[first + slot])
        for slot, (source, target) in enumerate(pairs)
    ]
    for copy in copies:
        copy.start()
    return copies


def finish(copies):
    for copy in copies:
        copy.wait()


def stack(cuts, refs, target):
    offset = 0
    for which, start, rows in cuts:
        target[offset : offset + rows, :] = refs[which][start : start + rows, :]
        offset += rows


def keep_kernel(text, after, held):
    held[...] = text[...]


def kept(text, after):
    return pl.pallas_call(
        keep_kernel,
        in_specs=[IN_VMEM] * 2,
        out_specs=IN_VMEM,
        out_shape=jax.ShapeDtypeStruct((ROWS, WIDTH), bf16),
        compiler_params=params(),
        cost_estimate=cost(KEEP, 0),
        name="hold_text",
    )(text, after)


def hold_kernel(features, log_scale, bias, after, features_held, scalars):
    features_held[...] = features[...]
    scalars[0:1, :] = jnp.full((1, 128), log_scale[0], f32)
    scalars[1:2, :] = jnp.full((1, 128), bias[0], f32)


def held(*arrays):
    return pl.pallas_call(
        hold_kernel,
        in_specs=[IN_VMEM] + [IN_SMEM] * 2 + [IN_VMEM],
        out_specs=[IN_VMEM] * 2,
        out_shape=[jax.ShapeDtypeStruct((ROWS, WIDTH), bf16), MARK],
        compiler_params=params(),
        cost_estimate=cost(HOLD, 0),
        name="hold",
    )(*arrays)


def normalize_kernel(upper, lower, *refs):
    unit = refs[-1]
    for slot, part in enumerate((upper, lower)):
        values = part[...].astype(f32)
        inverse = lax.rsqrt(jnp.sum(values * values, axis=1, keepdims=True) + epsilon)
        unit[ROWS * slot : ROWS * slot + ROWS, :] = (values * inverse).astype(bf16)


def normalized(*parts):
    return pl.pallas_call(
        normalize_kernel,
        in_specs=[IN_VMEM] * len(parts),
        out_specs=IN_VMEM,
        out_shape=jax.ShapeDtypeStruct((HALF // 2, WIDTH), bf16),
        compiler_params=params(),
        cost_estimate=cost(NORM, 0),
        name="normalize_texts",
    )(*parts)


def join_kernel(own, opposite, next_1, next_3, low, high, joined, low_later, high_later):
    for slot, part in enumerate((own, opposite, next_1, next_3)):
        joined[ROWS * slot : ROWS * slot + ROWS, :] = part[...]
    low_later[...] = low[...]
    high_later[...] = high[...]


def joined(*parts):
    return pl.pallas_call(
        join_kernel,
        in_specs=[IN_VMEM] * 6,
        out_specs=[IN_VMEM] * 3,
        out_shape=[jax.ShapeDtypeStruct((HALF, WIDTH), bf16)]
        + [jax.ShapeDtypeStruct((HALF // 2, WIDTH), bf16)] * 2,
        compiler_params=params(),
        cost_estimate=cost(WORK, 0),
        name="join",
    )(*parts)


def pass_kernel(low, high, after, low_on, high_on):
    low_on[...] = low[...]
    high_on[...] = high[...]


def passed(*parts):
    return pl.pallas_call(
        pass_kernel,
        in_specs=[IN_VMEM] * 3,
        out_specs=[IN_VMEM] * 2,
        out_shape=[jax.ShapeDtypeStruct((HALF // 2, WIDTH), bf16)] * 2,
        compiler_params=params(),
        name="pass_on",
    )(*parts)


def project_kernel(images, proj, unit, unit_f, inverse, turned, mark):
    mark[...] = jnp.zeros(mark.shape, f32)
    emb = jnp.dot(images[...], proj[...], preferred_element_type=f32)
    inv = lax.rsqrt(jnp.sum(emb * emb, axis=1, keepdims=True) + epsilon)
    emb = emb * inv
    unit_f[...] = emb
    inverse[...] = jnp.broadcast_to(inv, inverse.shape)
    unit[...] = emb.astype(bf16)
    turned[...] = images[...].T


def projected(images, proj_w):
    return pl.pallas_call(
        project_kernel,
        in_specs=[IN_VMEM] * 2,
        out_specs=[IN_VMEM] * 5,
        out_shape=[
            jax.ShapeDtypeStruct((HALF, WIDTH), bf16),
            jax.ShapeDtypeStruct((HALF, WIDTH), f32),
            jax.ShapeDtypeStruct((HALF, 128), f32),
            jax.ShapeDtypeStruct((WIDTH, HALF), bf16),
            MARK,
        ],
        compiler_params=params(),
        cost_estimate=cost(PROJ, 0),
        name="project_images",
    )(images, proj_w)


def wave_body(blocks, text, scalars, sim, weights, diagonal, take):
    half = 0.5 * jnp.exp(scalars[0:1, 0:1])
    half_shift = 0.5 * scalars[1:2, 0:1]
    rows, offset = [], 0
    for unit, start, count in blocks:
        rows.append(slice(offset, offset + count))
        offset += count
    for which, (unit, start, count) in enumerate(blocks):
        sim[rows[which], :] = lax.dot_general(
            unit[start : start + count, :],
            text[...],
            (((1,), (1,)), ((), ())),
            preferred_element_type=f32,
        )
        weights[rows[which], :] = (
            half + half * jnp.tanh(half * sim[rows[which], :] + half_shift)
        ).astype(bf16)
        if diagonal and which == 0:
            tanh = jnp.tanh(half * sim[:ROWS, :256] + half_shift)
            row = lax.broadcasted_iota(jnp.int32, (ROWS, 256), 0)
            column = lax.broadcasted_iota(jnp.int32, (ROWS, 256), 1)
            pair = jnp.where(row == column, half * tanh - half, half + half * tanh)
            weights[:ROWS, :256] = pair.astype(bf16)
    for which in range(len(blocks)):
        take(which, jnp.dot(weights[rows[which], :], text[...], preferred_element_type=f32))


def first_wave_kernel(cuts, scalars, low, high, unit_a, unit_b, total_a, total_b, text, sim, weights):
    stack(cuts, (low, high), text)
    totals = (total_a, total_b)

    def take(which, product):
        totals[which][...] = product

    blocks = ((unit_a, 0, HALF), (unit_b, 0, HALF))
    wave_body(blocks, text, scalars, sim, weights, True, take)


def next_wave_kernel(cuts, scalars, *refs):
    count = len(refs) - 9
    texts, (unit_a, unit_b), before, totals = (
        refs[:count],
        refs[count : count + 2],
        refs[count + 2 : count + 4],
        refs[count + 4 : count + 6],
    )
    text, sim, weights = refs[count + 6 :]
    stack(cuts, texts, text)

    def take(which, product):
        totals[which][...] = before[which][...] + product

    blocks = ((unit_a, 0, HALF), (unit_b, 0, HALF))
    wave_body(blocks, text, scalars, sim, weights, False, take)


def project_gradient(start, count, scalars, text, states, projected_f, projected_b, sim, weights):
    units, totals, units_f, inverses = (states[2 * slot : 2 * slot + 2] for slot in range(4))
    rows = slice(start, start + count)

    def take(which, product):
        gradient = totals[which][rows, :] + product
        image = units_f[which][rows, :]
        along = jnp.sum(image * gradient, axis=1, keepdims=True)
        projection = (gradient - image * along) * inverses[which][rows, 0:1]
        out = slice(which * count, which * count + count)
        projected_f[out, :] = projection
        projected_b[out, :] = projection.astype(bf16)

    blocks = tuple((unit, start, count) for unit in units)
    wave_body(blocks, text, scalars, sim, weights, False, take)


def last_wave_kernel(cuts, scalars, *refs):
    count = len(refs) - 13
    projected_f, projected_b, text, sim, weights = refs[count + 8 :]
    stack(cuts, refs[:count], text)
    project_gradient(
        0, EARLY, scalars, text, refs[count : count + 8], projected_f, projected_b, sim, weights
    )


def rest_wave_kernel(cuts, scalars, text, *refs):
    project_gradient(EARLY, HALF - EARLY, scalars, text, refs[:8], *refs[8:])


def wave(kernel, cuts, operands, images, out_shape, aliases, name, stacked=True):
    rows = sum(cut[2] for cut in cuts)
    return pl.pallas_call(
        lambda *refs: kernel(cuts, *refs),
        in_specs=[IN_VMEM] * len(operands),
        out_specs=[IN_VMEM] * len(out_shape),
        out_shape=out_shape,
        input_output_aliases=aliases,
        scratch_shapes=[pltpu.VMEM((rows, WIDTH), bf16)] * stacked
        + [pltpu.VMEM((images, rows), f32), pltpu.VMEM((images, rows), bf16)],
        compiler_params=params(),
        cost_estimate=cost(WAVES[name], 0),
        name=name,
    )(*operands)


def chip_projection(projected_f, other, count):
    return [
        (projected_f[first : first + count, :] + other[count - first : 2 * count - first, :].astype(f32)).astype(bf16)
        for first in (0, count)
    ]


def my_rows(high):
    return pl.ds(pl.multiple_of(576 * high + 288 * my_core(), 16), 288)


def first_terms_kernel(turned_a, turned_b, projected_f, other, out):
    both = jnp.concatenate(chip_projection(projected_f, other, EARLY))
    for high in range(2):
        left = jnp.concatenate([turned[my_rows(high), :EARLY] for turned in (turned_a, turned_b)], axis=1)
        out[288 * high : 288 * high + 288, :] = jnp.dot(left, both, preferred_element_type=f32)


def first_terms(*parts):
    return pl.pallas_call(
        first_terms_kernel,
        in_specs=[IN_VMEM] * 4,
        out_specs=IN_VMEM,
        out_shape=jax.ShapeDtypeStruct((HALF, WIDTH), f32),
        compiler_params=params(),
        cost_estimate=cost(1000, 1000),
        name="first_terms",
    )(*parts)


def cut_terms_kernel(turned_a, turned_b, projected_f, other, first, mine, two, one, three, total):
    both_a, both_b = chip_projection(projected_f, other, HALF - EARLY)
    for high in range(2):
        rows = slice(288 * high, 288 * high + 288)
        term = first[rows, :]
        for turned, both in ((turned_a, both_a), (turned_b, both_b)):
            term = term + jnp.dot(turned[my_rows(high), EARLY:], both, preferred_element_type=f32)
        for tile in range(9):
            total[tile, rows, :] = term[:, 128 * tile : 128 * tile + 128]
    index = lax.axis_index(AXIS)
    outs = ((0, mine), (2, two), (1, one), (3, three))

    @pl.when(my_core() == 0)
    def _():
        for steps, out in outs:
            first = 72 * (((index >> 3) + steps) & 3)
            for tile in range(9):
                for row in range(9):
                    parts = [
                        total[tile, pl.ds(288 * high + first + row, 8, stride=9), :]
                        for high in range(2)
                    ]
                    out[16 * row : 16 * row + 16, 128 * tile : 128 * tile + 128] = (
                        jnp.concatenate(parts).astype(out.dtype)
                    )

    @pl.when(my_core() == 1)
    def _():
        for steps, out in outs:
            first = 9 * ((index + steps) & 3)
            for tile in range(9):
                for row in range(9):
                    part = total[tile, pl.ds(first + row, 16, stride=36), :]
                    out[16 * row : 16 * row + 16, 128 * tile : 128 * tile + 128] = part.astype(
                        out.dtype
                    )


def cut_terms(*parts):
    return pl.pallas_call(
        cut_terms_kernel,
        in_specs=[IN_VMEM] * 5,
        out_specs=[IN_VMEM] * 4,
        out_shape=[jax.ShapeDtypeStruct((ROWS, WIDTH), f32)]
        + [jax.ShapeDtypeStruct((ROWS, WIDTH), bf16)] * 3,
        scratch_shapes=[pltpu.VMEM((9, HALF, 128), f32)],
        compiler_params=params(),
        name="cut_terms",
    )(*parts)


def ring_sum_kernel(mine, two, one, three, out, eights, ninth):
    ninth[...] = jnp.zeros(ninth.shape, f32)
    for tile in range(9):
        lanes = slice(128 * tile, 128 * tile + 128)
        value = mine[:, lanes]
        for part in (two, one, three):
            value = value + part[:, lanes].astype(f32)
        for row in range(8):
            eights[tile, pl.ds(row, 16, stride=8), :] = value[16 * row : 16 * row + 16]
        ninth[tile // 8, pl.ds(tile % 8, 16, stride=8), :] = value[128:]
        out[:, lanes] = eights[tile].astype(bf16)
    out[:, WIDTH : WIDTH + 128] = ninth[0].astype(bf16)
    out[:, WIDTH + 128 :] = ninth[1].astype(bf16)


def ring_sum(*parts):
    return pl.pallas_call(
        ring_sum_kernel,
        out_shape=jax.ShapeDtypeStruct((128, SLAB), bf16),
        scratch_shapes=[pltpu.VMEM((9, 128, 128), f32), pltpu.VMEM((2, 128, 128), f32)],
        compiler_params=params(),
        name="ring_sum",
    )(*parts)


def last_sum_kernel(pieces, out):
    total = jnp.zeros((16, SLAB), f32)
    for step in range(8):
        total = total + pieces[16 * step : 16 * step + 16, :].astype(f32)
    total = total[:8] + total[8:]
    out[:8, :] = total[:, :WIDTH]
    for tile in range(9):
        sublane, lane = tile % 8, WIDTH + 128 * (tile // 8)
        out[8:9, 128 * tile : 128 * tile + 128] = total[sublane : sublane + 1, lane : lane + 128]


def last_sum(pieces):
    return pl.pallas_call(
        last_sum_kernel,
        out_shape=jax.ShapeDtypeStruct((9, WIDTH), f32),
        compiler_params=params(),
        name="last_sum",
    )(pieces)


def ring(value, axis):
    return [send(value, axis(steps)) for steps in (2, 1, 3)]


def per_device(features, text_emb, proj_w, log_scale, bias):
    image_ring = ring(features, along_x)
    opposite, next_3 = (send(text_emb, along_y_or_z(steps)) for steps in (2, 3))
    text = kept(text_emb, next_3)
    next_1 = send(text, along_y_or_z(1))
    low = normalized(text, next_1)
    high = normalized(opposite, next_3)
    images, scalars = held(features, log_scale, bias, high)
    here, low_later, high_later = joined(images, *image_ring, low, high)
    there = send(here, other_core)
    low_1, high_3 = send(low, along_z_or_y(1)), send(high, along_z_or_y(3))
    high_1, low_3 = send(high_later, along_z_or_y(1)), send(low_later, along_z_or_y(3))
    units, units_f, inverses, turns, marks = zip(
        projected(here, proj_w), projected(there, proj_w)
    )
    low_on, high_on = passed(low_1, high_3, marks[1])
    low_2, high_2 = send(low_on, along_z_or_y(1)), send(high_on, along_z_or_y(3))

    sums = [jax.ShapeDtypeStruct((HALF, WIDTH), f32)] * 2
    totals = wave(
        first_wave_kernel,
        ((0, 0, 288), (1, 0, 224)),
        (scalars, low, high, *units),
        IMAGES,
        sums,
        {},
        "first_wave",
    )
    totals = wave(
        next_wave_kernel,
        ((0, 224, 64), (1, 0, 288), (2, 0, 288), (3, 0, 288), (4, 0, 96)),
        (scalars, high, low_1, high_3, high_1, low_3, *units, *totals),
        IMAGES,
        sums,
        {8: 0, 9: 1},
        "second_wave",
    )
    states = (*units, *totals, *units_f, *inverses)
    texts = jax.ShapeDtypeStruct((768, WIDTH), bf16)
    own_1, sent_1, text = wave(
        last_wave_kernel,
        ((0, 96, 192), (1, 0, 288), (2, 0, 288)),
        (scalars, low_3, low_2, high_2, *states),
        2 * EARLY,
        [
            jax.ShapeDtypeStruct((2 * EARLY, WIDTH), f32),
            jax.ShapeDtypeStruct((2 * EARLY, WIDTH), bf16),
            texts,
        ],
        {},
        "last_wave",
        stacked=False,
    )
    own_2, sent_2 = wave(
        rest_wave_kernel,
        ((0, 0, 768),),
        (scalars, text, *states),
        IMAGES - 2 * EARLY,
        [
            jax.ShapeDtypeStruct((IMAGES - 2 * EARLY, WIDTH), f32),
            jax.ShapeDtypeStruct((IMAGES - 2 * EARLY, WIDTH), bf16),
        ],
        {},
        "rest_wave",
        stacked=False,
    )
    got_1, got_2 = send(sent_1, other_core), send(sent_2, other_core)
    first = first_terms(*turns, own_1, got_1)
    mine, two, one, three = cut_terms(*turns, own_2, got_2, first)
    parts = [send(part, along_z_or_y(steps)) for part, steps in ((two, 2), (one, 1), (three, 3))]
    pieces = ring_sum(mine, *parts)
    pieces = lax.all_to_all(pieces, AXIS, 0, 0, axis_index_groups=LAST_GROUPS, tiled=True)
    return last_sum(pieces)


def solution(mesh):
    flat = Mesh(mesh.devices.reshape(-1), (AXIS,))
    rows = P(AXIS, None)
    return jax.shard_map(
        per_device,
        mesh=flat,
        in_specs=(rows, rows, P(), P(), P()),
        out_specs=rows,
        check_vma=False,
    )
```

```python
import jax
import jax.numpy as jnp
from jax import lax
from jax.experimental import pallas as pl
from jax.experimental.pallas import tpu as pltpu
from jax.sharding import Mesh, PartitionSpec as P

epsilon = 1e-06
bf16 = jnp.bfloat16
f32 = jnp.float32

AXIS = "d"
ROWS = 144
WIDTH = 1152
HALF = 4 * ROWS
IMAGES = 2 * HALF
TURNED = 512
EARLY = 384
SLAB = 1408
VMEM_LIMIT = 20 << 20
WORK = 12_000_000_000
PROJ = 20_000_000_000
W1 = 30_000_000_000
WAVES = {"first_wave": W1, "second_wave": 1000, "last_wave": 1000, "rest_wave": 1000}
HOLD = 12_000_000_000
NORM = 1000
KEEP = 1000
MARK = jax.ShapeDtypeStruct((8, 128), f32)


def place(index):
    y, xl, z = index & 3, (index >> 2) & 1, (index >> 3) & 3
    core, xh = (index >> 5) & 1, (index >> 6) & 1
    return 2 * xh + xl, y, z, core


def index_of(x, y, z, core):
    return (x >> 1) * 64 + core * 32 + z * 8 + (x & 1) * 4 + y


def send(value, target):
    pairs = [(source, index_of(*target(*place(source)))) for source in range(128)]
    return lax.ppermute(value, AXIS, pairs)


def along_x(steps):
    return lambda x, y, z, core: ((x + steps) % 4, y, z, core)


def along_y_or_z(steps):
    return lambda x, y, z, core: (
        (x, y, (z + steps) % 4, core) if core else (x, (y + steps) % 4, z, core)
    )


def along_z_or_y(steps):
    return lambda x, y, z, core: (
        (x, (y + steps) % 4, z, core) if core else (x, y, (z + steps) % 4, core)
    )


def other_core(x, y, z, core):
    return (x, y, z, 1 - core)


LAST_GROUPS = [
    [index_of(2 * xh + xl, y, z, 0) for xh in range(2) for xl in range(2) for y in range(4)]
    for z in range(4)
] + [
    [index_of(2 * xh + xl, y, z, 1) for xh in range(2) for z in range(4) for xl in range(2)]
    for y in range(4)
]


def my_core():
    return (lax.axis_index(AXIS) >> 5) & 1


IN_VMEM = pl.BlockSpec(memory_space=pltpu.VMEM)
IN_SMEM = pl.BlockSpec(memory_space=pltpu.SMEM)


def params():
    return pltpu.CompilerParams(vmem_limit_bytes=VMEM_LIMIT)


def cost(flops, bytes_accessed):
    return pl.CostEstimate(flops=flops, bytes_accessed=bytes_accessed, transcendentals=0)


def begin(pairs, sems, first=0):
    copies = [
        pltpu.make_async_copy(source, target, sems.at[first + slot])
        for slot, (source, target) in enumerate(pairs)
    ]
    for copy in copies:
        copy.start()
    return copies


def finish(copies):
    for copy in copies:
        copy.wait()


def stack(cuts, refs, target):
    offset = 0
    for which, start, rows in cuts:
        target[offset : offset + rows, :] = refs[which][start : start + rows, :]
        offset += rows


def keep_kernel(text, held):
    held[...] = text[...]


def kept(text):
    return pl.pallas_call(
        keep_kernel,
        in_specs=[IN_VMEM],
        out_specs=IN_VMEM,
        out_shape=jax.ShapeDtypeStruct((ROWS, WIDTH), bf16),
        compiler_params=params(),
        cost_estimate=cost(KEEP, 0),
        name="hold_text",
    )(text)


def hold_kernel(features, log_scale, bias, after, features_held, scalars):
    features_held[...] = features[...]
    scalars[0:1, :] = jnp.full((1, 128), log_scale[0], f32)
    scalars[1:2, :] = jnp.full((1, 128), bias[0], f32)


def held(*arrays):
    return pl.pallas_call(
        hold_kernel,
        in_specs=[IN_VMEM] + [IN_SMEM] * 2 + [IN_VMEM],
        out_specs=[IN_VMEM] * 2,
        out_shape=[jax.ShapeDtypeStruct((ROWS, WIDTH), bf16), MARK],
        compiler_params=params(),
        cost_estimate=cost(HOLD, 0),
        name="hold",
    )(*arrays)


def normalize_kernel(upper, lower, *refs):
    unit = refs[-1]
    for slot, part in enumerate((upper, lower)):
        values = part[...].astype(f32)
        inverse = lax.rsqrt(jnp.sum(values * values, axis=1, keepdims=True) + epsilon)
        unit[ROWS * slot : ROWS * slot + ROWS, :] = (values * inverse).astype(bf16)


def normalized(*parts):
    return pl.pallas_call(
        normalize_kernel,
        in_specs=[IN_VMEM] * len(parts),
        out_specs=IN_VMEM,
        out_shape=jax.ShapeDtypeStruct((HALF // 2, WIDTH), bf16),
        compiler_params=params(),
        cost_estimate=cost(NORM, 0),
        name="normalize_texts",
    )(*parts)


def join_kernel(own, opposite, next_1, next_3, low, high, joined, low_later, high_later):
    for slot, part in enumerate((own, opposite, next_1, next_3)):
        joined[ROWS * slot : ROWS * slot + ROWS, :] = part[...]
    low_later[...] = low[...]
    high_later[...] = high[...]


def joined(*parts):
    return pl.pallas_call(
        join_kernel,
        in_specs=[IN_VMEM] * 6,
        out_specs=[IN_VMEM] * 3,
        out_shape=[jax.ShapeDtypeStruct((HALF, WIDTH), bf16)]
        + [jax.ShapeDtypeStruct((HALF // 2, WIDTH), bf16)] * 2,
        compiler_params=params(),
        cost_estimate=cost(WORK, 0),
        name="join",
    )(*parts)


def pass_kernel(low, high, after, low_on, high_on):
    low_on[...] = low[...]
    high_on[...] = high[...]


def passed(*parts):
    return pl.pallas_call(
        pass_kernel,
        in_specs=[IN_VMEM] * 3,
        out_specs=[IN_VMEM] * 2,
        out_shape=[jax.ShapeDtypeStruct((HALF // 2, WIDTH), bf16)] * 2,
        compiler_params=params(),
        name="pass_on",
    )(*parts)


def project_kernel(images, proj, unit, unit_f, inverse, turned, *marks):
    for mark in marks:
        mark[...] = jnp.zeros(mark.shape, f32)
    emb = jnp.dot(images[...], proj[...], preferred_element_type=f32)
    inv = lax.rsqrt(jnp.sum(emb * emb, axis=1, keepdims=True) + epsilon)
    emb = emb * inv
    unit_f[...] = emb
    inverse[...] = jnp.broadcast_to(inv, inverse.shape)
    unit[...] = emb.astype(bf16)
    turned[...] = images[...].T


def projected(images, proj_w, marks):
    return pl.pallas_call(
        project_kernel,
        in_specs=[IN_VMEM] * 2,
        out_specs=[IN_VMEM] * (4 + marks),
        out_shape=[
            jax.ShapeDtypeStruct((HALF, WIDTH), bf16),
            jax.ShapeDtypeStruct((HALF, WIDTH), f32),
            jax.ShapeDtypeStruct((HALF, 128), f32),
            jax.ShapeDtypeStruct((WIDTH, HALF), bf16),
        ]
        + [MARK] * marks,
        compiler_params=params(),
        cost_estimate=cost(PROJ, 0),
        name="project_images",
    )(images, proj_w)


def wave_body(blocks, text, scalars, sim, weights, diagonal, take):
    half = 0.5 * jnp.exp(scalars[0:1, 0:1])
    half_shift = 0.5 * scalars[1:2, 0:1]
    rows, offset = [], 0
    for unit, start, count in blocks:
        rows.append(slice(offset, offset + count))
        offset += count
    for which, (unit, start, count) in enumerate(blocks):
        sim[rows[which], :] = lax.dot_general(
            unit[start : start + count, :],
            text[...],
            (((1,), (1,)), ((), ())),
            preferred_element_type=f32,
        )
        weights[rows[which], :] = (
            half + half * jnp.tanh(half * sim[rows[which], :] + half_shift)
        ).astype(bf16)
        if diagonal and which == 0:
            tanh = jnp.tanh(half * sim[:ROWS, :256] + half_shift)
            row = lax.broadcasted_iota(jnp.int32, (ROWS, 256), 0)
            column = lax.broadcasted_iota(jnp.int32, (ROWS, 256), 1)
            pair = jnp.where(row == column, half * tanh - half, half + half * tanh)
            weights[:ROWS, :256] = pair.astype(bf16)
    for which in range(len(blocks)):
        take(which, jnp.dot(weights[rows[which], :], text[...], preferred_element_type=f32))


def first_wave_kernel(cuts, scalars, low, high, unit_a, unit_b, total_a, total_b, text, sim, weights):
    stack(cuts, (low, high), text)
    totals = (total_a, total_b)

    def take(which, product):
        totals[which][...] = product

    blocks = ((unit_a, 0, HALF), (unit_b, 0, HALF))
    wave_body(blocks, text, scalars, sim, weights, True, take)


def next_wave_kernel(cuts, scalars, *refs):
    count = len(refs) - 9
    texts, (unit_a, unit_b), before, totals = (
        refs[:count],
        refs[count : count + 2],
        refs[count + 2 : count + 4],
        refs[count + 4 : count + 6],
    )
    text, sim, weights = refs[count + 6 :]
    stack(cuts, texts, text)

    def take(which, product):
        totals[which][...] = before[which][...] + product

    blocks = ((unit_a, 0, HALF), (unit_b, 0, HALF))
    wave_body(blocks, text, scalars, sim, weights, False, take)


def project_gradient(start, count, scalars, text, states, projected_f, projected_b, sim, weights):
    units, totals, units_f, inverses = (states[2 * slot : 2 * slot + 2] for slot in range(4))
    rows = slice(start, start + count)

    def take(which, product):
        gradient = totals[which][rows, :] + product
        image = units_f[which][rows, :]
        along = jnp.sum(image * gradient, axis=1, keepdims=True)
        projection = (gradient - image * along) * inverses[which][rows, 0:1]
        out = slice(which * count, which * count + count)
        projected_f[out, :] = projection
        projected_b[out, :] = projection.astype(bf16)

    blocks = tuple((unit, start, count) for unit in units)
    wave_body(blocks, text, scalars, sim, weights, False, take)


def last_wave_kernel(cuts, scalars, *refs):
    count = len(refs) - 13
    projected_f, projected_b, text, sim, weights = refs[count + 8 :]
    stack(cuts, refs[:count], text)
    project_gradient(
        0, EARLY, scalars, text, refs[count : count + 8], projected_f, projected_b, sim, weights
    )


def rest_wave_kernel(cuts, scalars, text, *refs):
    project_gradient(EARLY, HALF - EARLY, scalars, text, refs[:8], *refs[8:])


def wave(kernel, cuts, operands, images, out_shape, aliases, name, stacked=True):
    rows = sum(cut[2] for cut in cuts)
    return pl.pallas_call(
        lambda *refs: kernel(cuts, *refs),
        in_specs=[IN_VMEM] * len(operands),
        out_specs=[IN_VMEM] * len(out_shape),
        out_shape=out_shape,
        input_output_aliases=aliases,
        scratch_shapes=[pltpu.VMEM((rows, WIDTH), bf16)] * stacked
        + [pltpu.VMEM((images, rows), f32), pltpu.VMEM((images, rows), bf16)],
        compiler_params=params(),
        cost_estimate=cost(WAVES[name], 0),
        name=name,
    )(*operands)


def chip_projection(projected_f, other, count):
    return [
        (projected_f[first : first + count, :] + other[count - first : 2 * count - first, :].astype(f32)).astype(bf16)
        for first in (0, count)
    ]


def my_rows(high):
    return pl.ds(pl.multiple_of(576 * high + 288 * my_core(), 16), 288)


def first_terms_kernel(turned_a, turned_b, projected_f, other, out):
    both = jnp.concatenate(chip_projection(projected_f, other, EARLY))
    for high in range(2):
        left = jnp.concatenate([turned[my_rows(high), :EARLY] for turned in (turned_a, turned_b)], axis=1)
        out[288 * high : 288 * high + 288, :] = jnp.dot(left, both, preferred_element_type=f32)


def first_terms(*parts):
    return pl.pallas_call(
        first_terms_kernel,
        in_specs=[IN_VMEM] * 4,
        out_specs=IN_VMEM,
        out_shape=jax.ShapeDtypeStruct((HALF, WIDTH), f32),
        compiler_params=params(),
        cost_estimate=cost(1000, 1000),
        name="first_terms",
    )(*parts)


def cut_terms_kernel(turned_a, turned_b, projected_f, other, first, mine, two, one, three, total):
    both_a, both_b = chip_projection(projected_f, other, HALF - EARLY)
    for high in range(2):
        rows = slice(288 * high, 288 * high + 288)
        term = first[rows, :]
        for turned, both in ((turned_a, both_a), (turned_b, both_b)):
            term = term + jnp.dot(turned[my_rows(high), EARLY:], both, preferred_element_type=f32)
        for tile in range(9):
            total[tile, rows, :] = term[:, 128 * tile : 128 * tile + 128]
    index = lax.axis_index(AXIS)
    outs = ((0, mine), (2, two), (1, one), (3, three))

    @pl.when(my_core() == 0)
    def _():
        for steps, out in outs:
            first = 72 * (((index >> 3) + steps) & 3)
            for tile in range(9):
                for row in range(9):
                    parts = [
                        total[tile, pl.ds(288 * high + first + row, 8, stride=9), :]
                        for high in range(2)
                    ]
                    out[16 * row : 16 * row + 16, 128 * tile : 128 * tile + 128] = (
                        jnp.concatenate(parts).astype(out.dtype)
                    )

    @pl.when(my_core() == 1)
    def _():
        for steps, out in outs:
            first = 9 * ((index + steps) & 3)
            for tile in range(9):
                for row in range(9):
                    part = total[tile, pl.ds(first + row, 16, stride=36), :]
                    out[16 * row : 16 * row + 16, 128 * tile : 128 * tile + 128] = part.astype(
                        out.dtype
                    )


def cut_terms(*parts):
    return pl.pallas_call(
        cut_terms_kernel,
        in_specs=[IN_VMEM] * 5,
        out_specs=[IN_VMEM] * 4,
        out_shape=[jax.ShapeDtypeStruct((ROWS, WIDTH), f32)]
        + [jax.ShapeDtypeStruct((ROWS, WIDTH), bf16)] * 3,
        scratch_shapes=[pltpu.VMEM((9, HALF, 128), f32)],
        compiler_params=params(),
        name="cut_terms",
    )(*parts)


def ring_sum_kernel(mine, two, one, three, out, eights, ninth):
    ninth[...] = jnp.zeros(ninth.shape, f32)
    for tile in range(9):
        lanes = slice(128 * tile, 128 * tile + 128)
        value = mine[:, lanes]
        for part in (two, one, three):
            value = value + part[:, lanes].astype(f32)
        for row in range(8):
            eights[tile, pl.ds(row, 16, stride=8), :] = value[16 * row : 16 * row + 16]
        ninth[tile // 8, pl.ds(tile % 8, 16, stride=8), :] = value[128:]
        out[:, lanes] = eights[tile].astype(bf16)
    out[:, WIDTH : WIDTH + 128] = ninth[0].astype(bf16)
    out[:, WIDTH + 128 :] = ninth[1].astype(bf16)


def ring_sum(*parts):
    return pl.pallas_call(
        ring_sum_kernel,
        out_shape=jax.ShapeDtypeStruct((128, SLAB), bf16),
        scratch_shapes=[pltpu.VMEM((9, 128, 128), f32), pltpu.VMEM((2, 128, 128), f32)],
        compiler_params=params(),
        name="ring_sum",
    )(*parts)


def last_sum_kernel(pieces, out):
    total = jnp.zeros((16, SLAB), f32)
    for step in range(8):
        total = total + pieces[16 * step : 16 * step + 16, :].astype(f32)
    total = total[:8] + total[8:]
    out[:8, :] = total[:, :WIDTH]
    for tile in range(9):
        sublane, lane = tile % 8, WIDTH + 128 * (tile // 8)
        out[8:9, 128 * tile : 128 * tile + 128] = total[sublane : sublane + 1, lane : lane + 128]


def last_sum(pieces):
    return pl.pallas_call(
        last_sum_kernel,
        out_shape=jax.ShapeDtypeStruct((9, WIDTH), f32),
        compiler_params=params(),
        name="last_sum",
    )(pieces)


def ring(value, axis):
    return [send(value, axis(steps)) for steps in (2, 1, 3)]


def per_device(features, text_emb, proj_w, log_scale, bias):
    image_ring = ring(features, along_x)
    next_1, opposite, next_3 = (send(text_emb, along_y_or_z(steps)) for steps in (1, 2, 3))
    low = normalized(kept(text_emb), next_1, image_ring[0])
    high = normalized(opposite, next_3)
    images, scalars = held(features, log_scale, bias, high)
    here, low_later, high_later = joined(images, *image_ring, low, high)
    there = send(here, other_core)
    low_1, high_3 = send(low, along_z_or_y(1)), send(high, along_z_or_y(3))
    high_1, low_3 = send(high_later, along_z_or_y(1)), send(low_later, along_z_or_y(3))
    *there, mark = projected(there, proj_w, 1)
    units, units_f, inverses, turns = zip(projected(here, proj_w, 0), there)
    low_on, high_on = passed(low_1, high_3, mark)
    low_2, high_2 = send(low_on, along_z_or_y(1)), send(high_on, along_z_or_y(3))

    sums = [jax.ShapeDtypeStruct((HALF, WIDTH), f32)] * 2
    totals = wave(
        first_wave_kernel,
        ((0, 0, 288), (1, 0, 224)),
        (scalars, low, high, *units),
        IMAGES,
        sums,
        {},
        "first_wave",
    )
    totals = wave(
        next_wave_kernel,
        ((0, 224, 64), (1, 0, 288), (2, 0, 288), (3, 0, 288), (4, 0, 96)),
        (scalars, high, low_1, high_3, high_1, low_3, *units, *totals),
        IMAGES,
        sums,
        {8: 0, 9: 1},
        "second_wave",
    )
    states = (*units, *totals, *units_f, *inverses)
    texts = jax.ShapeDtypeStruct((768, WIDTH), bf16)
    own_1, sent_1, text = wave(
        last_wave_kernel,
        ((0, 96, 192), (1, 0, 288), (2, 0, 288)),
        (scalars, low_3, low_2, high_2, *states),
        2 * EARLY,
        [
            jax.ShapeDtypeStruct((2 * EARLY, WIDTH), f32),
            jax.ShapeDtypeStruct((2 * EARLY, WIDTH), bf16),
            texts,
        ],
        {},
        "last_wave",
        stacked=False,
    )
    own_2, sent_2 = wave(
        rest_wave_kernel,
        ((0, 0, 768),),
        (scalars, text, *states),
        IMAGES - 2 * EARLY,
        [
            jax.ShapeDtypeStruct((IMAGES - 2 * EARLY, WIDTH), f32),
            jax.ShapeDtypeStruct((IMAGES - 2 * EARLY, WIDTH), bf16),
        ],
        {},
        "rest_wave",
        stacked=False,
    )
    got_1, got_2 = send(sent_1, other_core), send(sent_2, other_core)
    first = first_terms(*turns, own_1, got_1)
    mine, two, one, three = cut_terms(*turns, own_2, got_2, first)
    parts = [send(part, along_z_or_y(steps)) for part, steps in ((two, 2), (one, 1), (three, 3))]
    pieces = ring_sum(mine, *parts)
    pieces = lax.all_to_all(pieces, AXIS, 0, 0, axis_index_groups=LAST_GROUPS, tiled=True)
    return last_sum(pieces)


def solution(mesh):
    flat = Mesh(mesh.devices.reshape(-1), (AXIS,))
    rows = P(AXIS, None)
    return jax.shard_map(
        per_device,
        mesh=flat,
        in_specs=(rows, rows, P(), P(), P()),
        out_specs=rows,
        check_vma=False,
    )
```

```python
import jax
import jax.numpy as jnp
from jax import lax
from jax.experimental import pallas as pl
from jax.experimental.pallas import tpu as pltpu
from jax.sharding import Mesh, PartitionSpec as P

epsilon = 1e-06
bf16 = jnp.bfloat16
f32 = jnp.float32

AXIS = "d"
ROWS = 144
WIDTH = 1152
HALF = 4 * ROWS
IMAGES = 2 * HALF
TURNED = 512
EARLY = 384
SLAB = 1408
VMEM_LIMIT = 20 << 20
WORK = 12_000_000_000
PROJ = 20_000_000_000
W1 = 30_000_000_000
WAVES = {"first_wave": W1, "second_wave": 1000, "last_wave": 1000, "rest_wave": 1000}
HOLD = 12_000_000_000
NORM = 1000
KEEP = 1000
MARK = jax.ShapeDtypeStruct((8, 128), f32)


def place(index):
    y, xl, z = index & 3, (index >> 2) & 1, (index >> 3) & 3
    core, xh = (index >> 5) & 1, (index >> 6) & 1
    return 2 * xh + xl, y, z, core


def index_of(x, y, z, core):
    return (x >> 1) * 64 + core * 32 + z * 8 + (x & 1) * 4 + y


def send(value, target):
    pairs = [(source, index_of(*target(*place(source)))) for source in range(128)]
    return lax.ppermute(value, AXIS, pairs)


def along_x(steps):
    return lambda x, y, z, core: ((x + steps) % 4, y, z, core)


def along_y_or_z(steps):
    return lambda x, y, z, core: (
        (x, y, (z + steps) % 4, core) if core else (x, (y + steps) % 4, z, core)
    )


def along_z_or_y(steps):
    return lambda x, y, z, core: (
        (x, (y + steps) % 4, z, core) if core else (x, y, (z + steps) % 4, core)
    )


def other_core(x, y, z, core):
    return (x, y, z, 1 - core)


LAST_GROUPS = [
    [index_of(2 * xh + xl, y, z, 0) for xh in range(2) for xl in range(2) for y in range(4)]
    for z in range(4)
] + [
    [index_of(2 * xh + xl, y, z, 1) for xh in range(2) for z in range(4) for xl in range(2)]
    for y in range(4)
]


def my_core():
    return (lax.axis_index(AXIS) >> 5) & 1


IN_VMEM = pl.BlockSpec(memory_space=pltpu.VMEM)
IN_SMEM = pl.BlockSpec(memory_space=pltpu.SMEM)


def params():
    return pltpu.CompilerParams(vmem_limit_bytes=VMEM_LIMIT)


def cost(flops, bytes_accessed):
    return pl.CostEstimate(flops=flops, bytes_accessed=bytes_accessed, transcendentals=0)


def begin(pairs, sems, first=0):
    copies = [
        pltpu.make_async_copy(source, target, sems.at[first + slot])
        for slot, (source, target) in enumerate(pairs)
    ]
    for copy in copies:
        copy.start()
    return copies


def finish(copies):
    for copy in copies:
        copy.wait()


def stack(cuts, refs, target):
    offset = 0
    for which, start, rows in cuts:
        target[offset : offset + rows, :] = refs[which][start : start + rows, :]
        offset += rows


def keep_kernel(text, held):
    held[...] = text[...]


def kept(text):
    return pl.pallas_call(
        keep_kernel,
        in_specs=[IN_VMEM],
        out_specs=IN_VMEM,
        out_shape=jax.ShapeDtypeStruct((ROWS, WIDTH), bf16),
        compiler_params=params(),
        cost_estimate=cost(KEEP, 0),
        name="hold_text",
    )(text)


def hold_kernel(features, log_scale, bias, after, features_held, scalars):
    features_held[...] = features[...]
    scalars[0:1, :] = jnp.full((1, 128), log_scale[0], f32)
    scalars[1:2, :] = jnp.full((1, 128), bias[0], f32)


def held(*arrays):
    return pl.pallas_call(
        hold_kernel,
        in_specs=[IN_VMEM] + [IN_SMEM] * 2 + [IN_VMEM],
        out_specs=[IN_VMEM] * 2,
        out_shape=[jax.ShapeDtypeStruct((ROWS, WIDTH), bf16), MARK],
        compiler_params=params(),
        cost_estimate=cost(HOLD, 0),
        name="hold",
    )(*arrays)


def normalize_kernel(upper, lower, *refs):
    unit = refs[-1]
    for slot, part in enumerate((upper, lower)):
        values = part[...].astype(f32)
        inverse = lax.rsqrt(jnp.sum(values * values, axis=1, keepdims=True) + epsilon)
        unit[ROWS * slot : ROWS * slot + ROWS, :] = (values * inverse).astype(bf16)


def normalized(*parts):
    return pl.pallas_call(
        normalize_kernel,
        in_specs=[IN_VMEM] * len(parts),
        out_specs=IN_VMEM,
        out_shape=jax.ShapeDtypeStruct((HALF // 2, WIDTH), bf16),
        compiler_params=params(),
        cost_estimate=cost(NORM, 0),
        name="normalize_texts",
    )(*parts)


def join_kernel(own, opposite, next_1, next_3, low, high, joined, low_later, high_later):
    for slot, part in enumerate((own, opposite, next_1, next_3)):
        joined[ROWS * slot : ROWS * slot + ROWS, :] = part[...]
    low_later[...] = low[...]
    high_later[...] = high[...]


def joined(*parts):
    return pl.pallas_call(
        join_kernel,
        in_specs=[IN_VMEM] * 6,
        out_specs=[IN_VMEM] * 3,
        out_shape=[jax.ShapeDtypeStruct((HALF, WIDTH), bf16)]
        + [jax.ShapeDtypeStruct((HALF // 2, WIDTH), bf16)] * 2,
        compiler_params=params(),
        cost_estimate=cost(WORK, 0),
        name="join",
    )(*parts)


def pass_kernel(low, high, after, low_on, high_on):
    low_on[...] = low[...]
    high_on[...] = high[...]


def passed(*parts):
    return pl.pallas_call(
        pass_kernel,
        in_specs=[IN_VMEM] * 3,
        out_specs=[IN_VMEM] * 2,
        out_shape=[jax.ShapeDtypeStruct((HALF // 2, WIDTH), bf16)] * 2,
        compiler_params=params(),
        name="pass_on",
    )(*parts)


def project_kernel(images, proj, unit, unit_f, inverse, turned, *marks):
    for mark in marks:
        mark[...] = jnp.zeros(mark.shape, f32)
    emb = jnp.dot(images[...], proj[...], preferred_element_type=f32)
    inv = lax.rsqrt(jnp.sum(emb * emb, axis=1, keepdims=True) + epsilon)
    emb = emb * inv
    unit_f[...] = emb
    inverse[...] = jnp.broadcast_to(inv, inverse.shape)
    unit[...] = emb.astype(bf16)
    turned[...] = images[...].T


def projected(images, proj_w, marks):
    return pl.pallas_call(
        project_kernel,
        in_specs=[IN_VMEM] * 2,
        out_specs=[IN_VMEM] * (4 + marks),
        out_shape=[
            jax.ShapeDtypeStruct((HALF, WIDTH), bf16),
            jax.ShapeDtypeStruct((HALF, WIDTH), f32),
            jax.ShapeDtypeStruct((HALF, 128), f32),
            jax.ShapeDtypeStruct((WIDTH, HALF), bf16),
        ]
        + [MARK] * marks,
        compiler_params=params(),
        cost_estimate=cost(PROJ, 0),
        name="project_images",
    )(images, proj_w)


def wave_body(blocks, text, scalars, sim, weights, diagonal, take):
    half = 0.5 * jnp.exp(scalars[0:1, 0:1])
    half_shift = 0.5 * scalars[1:2, 0:1]
    rows, offset = [], 0
    for unit, start, count in blocks:
        rows.append(slice(offset, offset + count))
        offset += count
    for which, (unit, start, count) in enumerate(blocks):
        sim[rows[which], :] = lax.dot_general(
            unit[start : start + count, :],
            text[...],
            (((1,), (1,)), ((), ())),
            preferred_element_type=f32,
        )
        weights[rows[which], :] = (
            half + half * jnp.tanh(half * sim[rows[which], :] + half_shift)
        ).astype(bf16)
        if diagonal and which == 0:
            tanh = jnp.tanh(half * sim[:ROWS, :256] + half_shift)
            row = lax.broadcasted_iota(jnp.int32, (ROWS, 256), 0)
            column = lax.broadcasted_iota(jnp.int32, (ROWS, 256), 1)
            pair = jnp.where(row == column, half * tanh - half, half + half * tanh)
            weights[:ROWS, :256] = pair.astype(bf16)
    for which in range(len(blocks)):
        take(which, jnp.dot(weights[rows[which], :], text[...], preferred_element_type=f32))


def first_wave_kernel(cuts, scalars, low, high, unit_a, unit_b, total_a, total_b, text, sim, weights):
    stack(cuts, (low, high), text)
    totals = (total_a, total_b)

    def take(which, product):
        totals[which][...] = product

    blocks = ((unit_a, 0, HALF), (unit_b, 0, HALF))
    wave_body(blocks, text, scalars, sim, weights, True, take)


def next_wave_kernel(cuts, scalars, *refs):
    count = len(refs) - 9
    texts, (unit_a, unit_b), before, totals = (
        refs[:count],
        refs[count : count + 2],
        refs[count + 2 : count + 4],
        refs[count + 4 : count + 6],
    )
    text, sim, weights = refs[count + 6 :]
    stack(cuts, texts, text)

    def take(which, product):
        totals[which][...] = before[which][...] + product

    blocks = ((unit_a, 0, HALF), (unit_b, 0, HALF))
    wave_body(blocks, text, scalars, sim, weights, False, take)


def project_gradient(start, count, scalars, text, states, projected_f, projected_b, sim, weights):
    units, totals, units_f, inverses = (states[2 * slot : 2 * slot + 2] for slot in range(4))
    rows = slice(start, start + count)

    def take(which, product):
        gradient = totals[which][rows, :] + product
        image = units_f[which][rows, :]
        along = jnp.sum(image * gradient, axis=1, keepdims=True)
        projection = (gradient - image * along) * inverses[which][rows, 0:1]
        out = slice(which * count, which * count + count)
        projected_f[out, :] = projection
        projected_b[out, :] = projection.astype(bf16)

    blocks = tuple((unit, start, count) for unit in units)
    wave_body(blocks, text, scalars, sim, weights, False, take)


def last_wave_kernel(cuts, scalars, *refs):
    count = len(refs) - 13
    projected_f, projected_b, text, sim, weights = refs[count + 8 :]
    stack(cuts, refs[:count], text)
    project_gradient(
        0, EARLY, scalars, text, refs[count : count + 8], projected_f, projected_b, sim, weights
    )


def rest_wave_kernel(cuts, scalars, text, *refs):
    project_gradient(EARLY, HALF - EARLY, scalars, text, refs[:8], *refs[8:])


def wave(kernel, cuts, operands, images, out_shape, aliases, name, stacked=True):
    rows = sum(cut[2] for cut in cuts)
    return pl.pallas_call(
        lambda *refs: kernel(cuts, *refs),
        in_specs=[IN_VMEM] * len(operands),
        out_specs=[IN_VMEM] * len(out_shape),
        out_shape=out_shape,
        input_output_aliases=aliases,
        scratch_shapes=[pltpu.VMEM((rows, WIDTH), bf16)] * stacked
        + [pltpu.VMEM((images, rows), f32), pltpu.VMEM((images, rows), bf16)],
        compiler_params=params(),
        cost_estimate=cost(WAVES[name], 0),
        name=name,
    )(*operands)


def chip_projection(projected_f, other, count):
    return [
        (projected_f[first : first + count, :] + other[count - first : 2 * count - first, :].astype(f32)).astype(bf16)
        for first in (0, count)
    ]


def my_rows(high):
    return pl.ds(pl.multiple_of(576 * high + 288 * my_core(), 16), 288)


def first_terms_kernel(turned_a, turned_b, projected_f, other, out):
    both = jnp.concatenate(chip_projection(projected_f, other, EARLY))
    for high in range(2):
        left = jnp.concatenate([turned[my_rows(high), :EARLY] for turned in (turned_a, turned_b)], axis=1)
        out[288 * high : 288 * high + 288, :] = jnp.dot(left, both, preferred_element_type=f32)


def first_terms(*parts):
    return pl.pallas_call(
        first_terms_kernel,
        in_specs=[IN_VMEM] * 4,
        out_specs=IN_VMEM,
        out_shape=jax.ShapeDtypeStruct((HALF, WIDTH), f32),
        compiler_params=params(),
        cost_estimate=cost(1000, 1000),
        name="first_terms",
    )(*parts)


def cut_terms_kernel(turned_a, turned_b, projected_f, other, first, mine, two, one, three, total):
    both_a, both_b = chip_projection(projected_f, other, HALF - EARLY)
    for high in range(2):
        rows = slice(288 * high, 288 * high + 288)
        term = first[rows, :]
        for turned, both in ((turned_a, both_a), (turned_b, both_b)):
            term = term + jnp.dot(turned[my_rows(high), EARLY:], both, preferred_element_type=f32)
        for tile in range(9):
            total[tile, rows, :] = term[:, 128 * tile : 128 * tile + 128]
    index = lax.axis_index(AXIS)
    outs = ((0, mine), (2, two), (1, one), (3, three))

    @pl.when(my_core() == 0)
    def _():
        for steps, out in outs:
            first = 72 * (((index >> 3) + steps) & 3)
            for tile in range(9):
                for row in range(9):
                    parts = [
                        total[tile, pl.ds(288 * high + first + row, 8, stride=9), :]
                        for high in range(2)
                    ]
                    out[16 * row : 16 * row + 16, 128 * tile : 128 * tile + 128] = (
                        jnp.concatenate(parts).astype(out.dtype)
                    )

    @pl.when(my_core() == 1)
    def _():
        for steps, out in outs:
            first = 9 * ((index + steps) & 3)
            for tile in range(9):
                for row in range(9):
                    part = total[tile, pl.ds(first + row, 16, stride=36), :]
                    out[16 * row : 16 * row + 16, 128 * tile : 128 * tile + 128] = part.astype(
                        out.dtype
                    )


def cut_terms(*parts):
    return pl.pallas_call(
        cut_terms_kernel,
        in_specs=[IN_VMEM] * 5,
        out_specs=[IN_VMEM] * 4,
        out_shape=[jax.ShapeDtypeStruct((ROWS, WIDTH), f32)]
        + [jax.ShapeDtypeStruct((ROWS, WIDTH), bf16)] * 3,
        scratch_shapes=[pltpu.VMEM((9, HALF, 128), f32)],
        compiler_params=params(),
        name="cut_terms",
    )(*parts)


def ring_sum_kernel(mine, two, one, three, out, eights, ninth):
    ninth[...] = jnp.zeros(ninth.shape, f32)
    for tile in range(9):
        lanes = slice(128 * tile, 128 * tile + 128)
        value = mine[:, lanes]
        for part in (two, one, three):
            value = value + part[:, lanes].astype(f32)
        for row in range(8):
            eights[tile, pl.ds(row, 16, stride=8), :] = value[16 * row : 16 * row + 16]
        ninth[tile // 8, pl.ds(tile % 8, 16, stride=8), :] = value[128:]
        out[:, lanes] = eights[tile].astype(bf16)
    out[:, WIDTH : WIDTH + 128] = ninth[0].astype(bf16)
    out[:, WIDTH + 128 :] = ninth[1].astype(bf16)


def ring_sum(*parts):
    return pl.pallas_call(
        ring_sum_kernel,
        out_shape=jax.ShapeDtypeStruct((128, SLAB), bf16),
        scratch_shapes=[pltpu.VMEM((9, 128, 128), f32), pltpu.VMEM((2, 128, 128), f32)],
        compiler_params=params(),
        name="ring_sum",
    )(*parts)


def last_sum_kernel(pieces, out):
    total = jnp.zeros((16, SLAB), f32)
    for step in range(8):
        total = total + pieces[16 * step : 16 * step + 16, :].astype(f32)
    total = total[:8] + total[8:]
    out[:8, :] = total[:, :WIDTH]
    for tile in range(9):
        sublane, lane = tile % 8, WIDTH + 128 * (tile // 8)
        out[8:9, 128 * tile : 128 * tile + 128] = total[sublane : sublane + 1, lane : lane + 128]


def last_sum(pieces):
    return pl.pallas_call(
        last_sum_kernel,
        out_shape=jax.ShapeDtypeStruct((9, WIDTH), f32),
        compiler_params=params(),
        name="last_sum",
    )(pieces)


def ring(value, axis):
    return [send(value, axis(steps)) for steps in (2, 1, 3)]


def per_device(features, text_emb, proj_w, log_scale, bias):
    image_ring = ring(features, along_x)
    next_1, opposite, next_3 = (send(text_emb, along_y_or_z(steps)) for steps in (1, 2, 3))
    low = normalized(kept(text_emb), next_1)
    high = normalized(opposite, next_3, image_ring[0])
    images, scalars = held(features, log_scale, bias, high)
    here, low_later, high_later = joined(images, *image_ring, low, high)
    there = send(here, other_core)
    low_1, high_3 = send(low, along_z_or_y(1)), send(high, along_z_or_y(3))
    high_1, low_3 = send(high_later, along_z_or_y(1)), send(low_later, along_z_or_y(3))
    *there, mark = projected(there, proj_w, 1)
    units, units_f, inverses, turns = zip(projected(here, proj_w, 0), there)
    low_on, high_on = passed(low_1, high_3, mark)
    low_2, high_2 = send(low_on, along_z_or_y(1)), send(high_on, along_z_or_y(3))

    sums = [jax.ShapeDtypeStruct((HALF, WIDTH), f32)] * 2
    totals = wave(
        first_wave_kernel,
        ((0, 0, 288), (1, 0, 224)),
        (scalars, low, high, *units),
        IMAGES,
        sums,
        {},
        "first_wave",
    )
    totals = wave(
        next_wave_kernel,
        ((0, 224, 64), (1, 0, 288), (2, 0, 288), (3, 0, 288), (4, 0, 96)),
        (scalars, high, low_1, high_3, high_1, low_3, *units, *totals),
        IMAGES,
        sums,
        {8: 0, 9: 1},
        "second_wave",
    )
    states = (*units, *totals, *units_f, *inverses)
    texts = jax.ShapeDtypeStruct((768, WIDTH), bf16)
    own_1, sent_1, text = wave(
        last_wave_kernel,
        ((0, 96, 192), (1, 0, 288), (2, 0, 288)),
        (scalars, low_3, low_2, high_2, *states),
        2 * EARLY,
        [
            jax.ShapeDtypeStruct((2 * EARLY, WIDTH), f32),
            jax.ShapeDtypeStruct((2 * EARLY, WIDTH), bf16),
            texts,
        ],
        {},
        "last_wave",
        stacked=False,
    )
    own_2, sent_2 = wave(
        rest_wave_kernel,
        ((0, 0, 768),),
        (scalars, text, *states),
        IMAGES - 2 * EARLY,
        [
            jax.ShapeDtypeStruct((IMAGES - 2 * EARLY, WIDTH), f32),
            jax.ShapeDtypeStruct((IMAGES - 2 * EARLY, WIDTH), bf16),
        ],
        {},
        "rest_wave",
        stacked=False,
    )
    got_1, got_2 = send(sent_1, other_core), send(sent_2, other_core)
    first = first_terms(*turns, own_1, got_1)
    mine, two, one, three = cut_terms(*turns, own_2, got_2, first)
    parts = [send(part, along_z_or_y(steps)) for part, steps in ((two, 2), (one, 1), (three, 3))]
    pieces = ring_sum(mine, *parts)
    pieces = lax.all_to_all(pieces, AXIS, 0, 0, axis_index_groups=LAST_GROUPS, tiled=True)
    return last_sum(pieces)


def solution(mesh):
    flat = Mesh(mesh.devices.reshape(-1), (AXIS,))
    rows = P(AXIS, None)
    return jax.shard_map(
        per_device,
        mesh=flat,
        in_specs=(rows, rows, P(), P(), P()),
        out_specs=rows,
        check_vma=False,
    )
```

```python
import jax
import jax.numpy as jnp
from jax import lax
from jax.experimental import pallas as pl
from jax.experimental.pallas import tpu as pltpu
from jax.sharding import Mesh, PartitionSpec as P

epsilon = 1e-06
bf16 = jnp.bfloat16
f32 = jnp.float32

AXIS = "d"
ROWS = 144
WIDTH = 1152
HALF = 4 * ROWS
IMAGES = 2 * HALF
TURNED = 512
EARLY = 384
SLAB = 1408
VMEM_LIMIT = 20 << 20
WORK = 12_000_000_000
PROJ = 20_000_000_000
W1 = 30_000_000_000
WAVES = {"first_wave": W1, "second_wave": 1000, "last_wave": 1000, "rest_wave": 1000}
HOLD = 12_000_000_000
NORM = 1000
KEEP = 1000
MARK = jax.ShapeDtypeStruct((8, 128), f32)


def place(index):
    y, xl, z = index & 3, (index >> 2) & 1, (index >> 3) & 3
    core, xh = (index >> 5) & 1, (index >> 6) & 1
    return 2 * xh + xl, y, z, core


def index_of(x, y, z, core):
    return (x >> 1) * 64 + core * 32 + z * 8 + (x & 1) * 4 + y


def send(value, target):
    pairs = [(source, index_of(*target(*place(source)))) for source in range(128)]
    return lax.ppermute(value, AXIS, pairs)


def along_x(steps):
    return lambda x, y, z, core: ((x + steps) % 4, y, z, core)


def along_y_or_z(steps):
    return lambda x, y, z, core: (
        (x, y, (z + steps) % 4, core) if core else (x, (y + steps) % 4, z, core)
    )


def along_z_or_y(steps):
    return lambda x, y, z, core: (
        (x, (y + steps) % 4, z, core) if core else (x, y, (z + steps) % 4, core)
    )


def other_core(x, y, z, core):
    return (x, y, z, 1 - core)


LAST_GROUPS = [
    [index_of(2 * xh + xl, y, z, 0) for xh in range(2) for xl in range(2) for y in range(4)]
    for z in range(4)
] + [
    [index_of(2 * xh + xl, y, z, 1) for xh in range(2) for z in range(4) for xl in range(2)]
    for y in range(4)
]


def my_core():
    return (lax.axis_index(AXIS) >> 5) & 1


IN_VMEM = pl.BlockSpec(memory_space=pltpu.VMEM)
IN_SMEM = pl.BlockSpec(memory_space=pltpu.SMEM)


def params():
    return pltpu.CompilerParams(vmem_limit_bytes=VMEM_LIMIT)


def cost(flops, bytes_accessed):
    return pl.CostEstimate(flops=flops, bytes_accessed=bytes_accessed, transcendentals=0)


def begin(pairs, sems, first=0):
    copies = [
        pltpu.make_async_copy(source, target, sems.at[first + slot])
        for slot, (source, target) in enumerate(pairs)
    ]
    for copy in copies:
        copy.start()
    return copies


def finish(copies):
    for copy in copies:
        copy.wait()


def stack(cuts, refs, target):
    offset = 0
    for which, start, rows in cuts:
        target[offset : offset + rows, :] = refs[which][start : start + rows, :]
        offset += rows


def keep_kernel(text, held):
    held[...] = text[...]


def kept(text):
    return pl.pallas_call(
        keep_kernel,
        in_specs=[IN_VMEM],
        out_specs=IN_VMEM,
        out_shape=jax.ShapeDtypeStruct((ROWS, WIDTH), bf16),
        compiler_params=params(),
        cost_estimate=cost(KEEP, 0),
        name="hold_text",
    )(text)


def hold_kernel(features, log_scale, bias, after, features_held, scalars):
    features_held[...] = features[...]
    scalars[0:1, :] = jnp.full((1, 128), log_scale[0], f32)
    scalars[1:2, :] = jnp.full((1, 128), bias[0], f32)


def held(*arrays):
    return pl.pallas_call(
        hold_kernel,
        in_specs=[IN_VMEM] + [IN_SMEM] * 2 + [IN_VMEM],
        out_specs=[IN_VMEM] * 2,
        out_shape=[jax.ShapeDtypeStruct((ROWS, WIDTH), bf16), MARK],
        compiler_params=params(),
        cost_estimate=cost(HOLD, 0),
        name="hold",
    )(*arrays)


def normalize_kernel(upper, lower, *refs):
    unit = refs[-1]
    for slot, part in enumerate((upper, lower)):
        values = part[...].astype(f32)
        inverse = lax.rsqrt(jnp.sum(values * values, axis=1, keepdims=True) + epsilon)
        unit[ROWS * slot : ROWS * slot + ROWS, :] = (values * inverse).astype(bf16)


def normalized(*parts):
    return pl.pallas_call(
        normalize_kernel,
        in_specs=[IN_VMEM] * len(parts),
        out_specs=IN_VMEM,
        out_shape=jax.ShapeDtypeStruct((HALF // 2, WIDTH), bf16),
        compiler_params=params(),
        cost_estimate=cost(NORM, 0),
        name="normalize_texts",
    )(*parts)


def join_kernel(own, opposite, next_1, next_3, low, high, joined, low_later, high_later):
    for slot, part in enumerate((own, opposite, next_1, next_3)):
        joined[ROWS * slot : ROWS * slot + ROWS, :] = part[...]
    low_later[...] = low[...]
    high_later[...] = high[...]


def joined(*parts):
    return pl.pallas_call(
        join_kernel,
        in_specs=[IN_VMEM] * 6,
        out_specs=[IN_VMEM] * 3,
        out_shape=[jax.ShapeDtypeStruct((HALF, WIDTH), bf16)]
        + [jax.ShapeDtypeStruct((HALF // 2, WIDTH), bf16)] * 2,
        compiler_params=params(),
        cost_estimate=cost(WORK, 0),
        name="join",
    )(*parts)


def pass_kernel(low, high, after, low_on, high_on):
    low_on[...] = low[...]
    high_on[...] = high[...]


def passed(*parts):
    return pl.pallas_call(
        pass_kernel,
        in_specs=[IN_VMEM] * 3,
        out_specs=[IN_VMEM] * 2,
        out_shape=[jax.ShapeDtypeStruct((HALF // 2, WIDTH), bf16)] * 2,
        compiler_params=params(),
        name="pass_on",
    )(*parts)


def project_kernel(images, proj, unit, unit_f, inverse, turned, *marks):
    for mark in marks:
        mark[...] = jnp.zeros(mark.shape, f32)
    emb = jnp.dot(images[...], proj[...], preferred_element_type=f32)
    inv = lax.rsqrt(jnp.sum(emb * emb, axis=1, keepdims=True) + epsilon)
    emb = emb * inv
    unit_f[...] = emb
    inverse[...] = jnp.broadcast_to(inv, inverse.shape)
    unit[...] = emb.astype(bf16)
    turned[...] = images[...].T


def projected(images, proj_w, marks):
    return pl.pallas_call(
        project_kernel,
        in_specs=[IN_VMEM] * 2,
        out_specs=[IN_VMEM] * (4 + marks),
        out_shape=[
            jax.ShapeDtypeStruct((HALF, WIDTH), bf16),
            jax.ShapeDtypeStruct((HALF, WIDTH), f32),
            jax.ShapeDtypeStruct((HALF, 128), f32),
            jax.ShapeDtypeStruct((WIDTH, HALF), bf16),
        ]
        + [MARK] * marks,
        compiler_params=params(),
        cost_estimate=cost(PROJ, 0),
        name="project_images",
    )(images, proj_w)


def wave_body(blocks, text, scalars, sim, weights, diagonal, take):
    half = 0.5 * jnp.exp(scalars[0:1, 0:1])
    half_shift = 0.5 * scalars[1:2, 0:1]
    rows, offset = [], 0
    for unit, start, count in blocks:
        rows.append(slice(offset, offset + count))
        offset += count
    for which, (unit, start, count) in enumerate(blocks):
        sim[rows[which], :] = lax.dot_general(
            unit[start : start + count, :],
            text[...],
            (((1,), (1,)), ((), ())),
            preferred_element_type=f32,
        )
        weights[rows[which], :] = (
            half + half * jnp.tanh(half * sim[rows[which], :] + half_shift)
        ).astype(bf16)
        if diagonal and which == 0:
            tanh = jnp.tanh(half * sim[:ROWS, :256] + half_shift)
            row = lax.broadcasted_iota(jnp.int32, (ROWS, 256), 0)
            column = lax.broadcasted_iota(jnp.int32, (ROWS, 256), 1)
            pair = jnp.where(row == column, half * tanh - half, half + half * tanh)
            weights[:ROWS, :256] = pair.astype(bf16)
    for which in range(len(blocks)):
        take(which, jnp.dot(weights[rows[which], :], text[...], preferred_element_type=f32))


def first_wave_kernel(cuts, scalars, low, high, unit_a, unit_b, total_a, total_b, text, sim, weights):
    stack(cuts, (low, high), text)
    totals = (total_a, total_b)

    def take(which, product):
        totals[which][...] = product

    blocks = ((unit_a, 0, HALF), (unit_b, 0, HALF))
    wave_body(blocks, text, scalars, sim, weights, True, take)


def next_wave_kernel(cuts, scalars, *refs):
    count = len(refs) - 9
    texts, (unit_a, unit_b), before, totals = (
        refs[:count],
        refs[count : count + 2],
        refs[count + 2 : count + 4],
        refs[count + 4 : count + 6],
    )
    text, sim, weights = refs[count + 6 :]
    stack(cuts, texts, text)

    def take(which, product):
        totals[which][...] = before[which][...] + product

    blocks = ((unit_a, 0, HALF), (unit_b, 0, HALF))
    wave_body(blocks, text, scalars, sim, weights, False, take)


def project_gradient(start, count, scalars, text, states, projected_f, projected_b, sim, weights):
    units, totals, units_f, inverses = (states[2 * slot : 2 * slot + 2] for slot in range(4))
    rows = slice(start, start + count)

    def take(which, product):
        gradient = totals[which][rows, :] + product
        image = units_f[which][rows, :]
        along = jnp.sum(image * gradient, axis=1, keepdims=True)
        projection = (gradient - image * along) * inverses[which][rows, 0:1]
        out = slice(which * count, which * count + count)
        projected_f[out, :] = projection
        projected_b[out, :] = projection.astype(bf16)

    blocks = tuple((unit, start, count) for unit in units)
    wave_body(blocks, text, scalars, sim, weights, False, take)


def last_wave_kernel(cuts, scalars, *refs):
    count = len(refs) - 13
    projected_f, projected_b, text, sim, weights = refs[count + 8 :]
    stack(cuts, refs[:count], text)
    project_gradient(
        0, EARLY, scalars, text, refs[count : count + 8], projected_f, projected_b, sim, weights
    )


def rest_wave_kernel(cuts, scalars, text, *refs):
    project_gradient(EARLY, HALF - EARLY, scalars, text, refs[:8], *refs[8:])


def wave(kernel, cuts, operands, images, out_shape, aliases, name, stacked=True):
    rows = sum(cut[2] for cut in cuts)
    return pl.pallas_call(
        lambda *refs: kernel(cuts, *refs),
        in_specs=[IN_VMEM] * len(operands),
        out_specs=[IN_VMEM] * len(out_shape),
        out_shape=out_shape,
        input_output_aliases=aliases,
        scratch_shapes=[pltpu.VMEM((rows, WIDTH), bf16)] * stacked
        + [pltpu.VMEM((images, rows), f32), pltpu.VMEM((images, rows), bf16)],
        compiler_params=params(),
        cost_estimate=cost(WAVES[name], 0),
        name=name,
    )(*operands)


def chip_projection(projected_f, other, count):
    return [
        (projected_f[first : first + count, :] + other[count - first : 2 * count - first, :].astype(f32)).astype(bf16)
        for first in (0, count)
    ]


def my_rows(high):
    return pl.ds(pl.multiple_of(576 * high + 288 * my_core(), 16), 288)


def first_terms_kernel(turned_a, turned_b, projected_f, other, out):
    both = jnp.concatenate(chip_projection(projected_f, other, EARLY))
    for high in range(2):
        left = jnp.concatenate([turned[my_rows(high), :EARLY] for turned in (turned_a, turned_b)], axis=1)
        out[288 * high : 288 * high + 288, :] = jnp.dot(left, both, preferred_element_type=f32)


def first_terms(*parts):
    return pl.pallas_call(
        first_terms_kernel,
        in_specs=[IN_VMEM] * 4,
        out_specs=IN_VMEM,
        out_shape=jax.ShapeDtypeStruct((HALF, WIDTH), f32),
        compiler_params=params(),
        cost_estimate=cost(1000, 1000),
        name="first_terms",
    )(*parts)


def cut_terms_kernel(turned_a, turned_b, projected_f, other, first, mine, two, one, three, total):
    both_a, both_b = chip_projection(projected_f, other, HALF - EARLY)
    for high in range(2):
        rows = slice(288 * high, 288 * high + 288)
        term = first[rows, :]
        for turned, both in ((turned_a, both_a), (turned_b, both_b)):
            term = term + jnp.dot(turned[my_rows(high), EARLY:], both, preferred_element_type=f32)
        for tile in range(9):
            total[tile, rows, :] = term[:, 128 * tile : 128 * tile + 128]
    index = lax.axis_index(AXIS)
    outs = ((0, mine), (2, two), (1, one), (3, three))

    @pl.when(my_core() == 0)
    def _():
        for steps, out in outs:
            first = 72 * (((index >> 3) + steps) & 3)
            for tile in range(9):
                for row in range(9):
                    parts = [
                        total[tile, pl.ds(288 * high + first + row, 8, stride=9), :]
                        for high in range(2)
                    ]
                    out[16 * row : 16 * row + 16, 128 * tile : 128 * tile + 128] = (
                        jnp.concatenate(parts).astype(out.dtype)
                    )

    @pl.when(my_core() == 1)
    def _():
        for steps, out in outs:
            first = 9 * ((index + steps) & 3)
            for tile in range(9):
                for row in range(9):
                    part = total[tile, pl.ds(first + row, 16, stride=36), :]
                    out[16 * row : 16 * row + 16, 128 * tile : 128 * tile + 128] = part.astype(
                        out.dtype
                    )


def cut_terms(*parts):
    return pl.pallas_call(
        cut_terms_kernel,
        in_specs=[IN_VMEM] * 5,
        out_specs=[IN_VMEM] * 4,
        out_shape=[jax.ShapeDtypeStruct((ROWS, WIDTH), f32)]
        + [jax.ShapeDtypeStruct((ROWS, WIDTH), bf16)] * 3,
        scratch_shapes=[pltpu.VMEM((9, HALF, 128), f32)],
        compiler_params=params(),
        name="cut_terms",
    )(*parts)


def ring_sum_kernel(mine, two, one, three, out, eights, ninth):
    ninth[...] = jnp.zeros(ninth.shape, f32)
    for tile in range(9):
        lanes = slice(128 * tile, 128 * tile + 128)
        value = mine[:, lanes]
        for part in (two, one, three):
            value = value + part[:, lanes].astype(f32)
        for row in range(8):
            eights[tile, pl.ds(row, 16, stride=8), :] = value[16 * row : 16 * row + 16]
        ninth[tile // 8, pl.ds(tile % 8, 16, stride=8), :] = value[128:]
        out[:, lanes] = eights[tile].astype(bf16)
    out[:, WIDTH : WIDTH + 128] = ninth[0].astype(bf16)
    out[:, WIDTH + 128 :] = ninth[1].astype(bf16)


def ring_sum(*parts):
    return pl.pallas_call(
        ring_sum_kernel,
        out_shape=jax.ShapeDtypeStruct((128, SLAB), bf16),
        scratch_shapes=[pltpu.VMEM((9, 128, 128), f32), pltpu.VMEM((2, 128, 128), f32)],
        compiler_params=params(),
        name="ring_sum",
    )(*parts)


def last_sum_kernel(pieces, out):
    total = jnp.zeros((16, SLAB), f32)
    for step in range(8):
        total = total + pieces[16 * step : 16 * step + 16, :].astype(f32)
    total = total[:8] + total[8:]
    out[:8, :] = total[:, :WIDTH]
    for tile in range(9):
        sublane, lane = tile % 8, WIDTH + 128 * (tile // 8)
        out[8:9, 128 * tile : 128 * tile + 128] = total[sublane : sublane + 1, lane : lane + 128]


def last_sum(pieces):
    return pl.pallas_call(
        last_sum_kernel,
        out_shape=jax.ShapeDtypeStruct((9, WIDTH), f32),
        compiler_params=params(),
        name="last_sum",
    )(pieces)


def ring(value, axis):
    return [send(value, axis(steps)) for steps in (2, 1, 3)]


def per_device(features, text_emb, proj_w, log_scale, bias):
    image_ring = ring(features, along_x)
    next_1, opposite, next_3 = (send(text_emb, along_y_or_z(steps)) for steps in (1, 2, 3))
    low = normalized(kept(text_emb), next_1)
    high = normalized(opposite, next_3)
    images, scalars = held(features, log_scale, bias, high)
    here, low_later, high_later = joined(images, *image_ring, low, high)
    there = send(here, other_core)
    low_1, high_3 = send(low, along_z_or_y(1)), send(high, along_z_or_y(3))
    high_1, low_3 = send(high_later, along_z_or_y(1)), send(low_later, along_z_or_y(3))
    *there, mark = projected(there, proj_w, 1)
    units, units_f, inverses, turns = zip(projected(here, proj_w, 0), there)
    low_on, high_on = passed(low_1, high_3, mark)
    low_2, high_2 = send(low_on, along_z_or_y(1)), send(high_on, along_z_or_y(3))

    sums = [jax.ShapeDtypeStruct((HALF, WIDTH), f32)] * 2
    totals = wave(
        first_wave_kernel,
        ((0, 0, 288), (1, 0, 224)),
        (scalars, low, high, *units),
        IMAGES,
        sums,
        {},
        "first_wave",
    )
    totals = wave(
        next_wave_kernel,
        ((0, 224, 64), (1, 0, 288), (2, 0, 288), (3, 0, 288), (4, 0, 96)),
        (scalars, high, low_1, high_3, high_1, low_3, *units, *totals),
        IMAGES,
        sums,
        {8: 0, 9: 1},
        "second_wave",
    )
    states = (*units, *totals, *units_f, *inverses)
    texts = jax.ShapeDtypeStruct((768, WIDTH), bf16)
    own_1, sent_1, text = wave(
        last_wave_kernel,
        ((0, 96, 192), (1, 0, 288), (2, 0, 288)),
        (scalars, low_3, low_2, high_2, *states),
        2 * EARLY,
        [
            jax.ShapeDtypeStruct((2 * EARLY, WIDTH), f32),
            jax.ShapeDtypeStruct((2 * EARLY, WIDTH), bf16),
            texts,
        ],
        {},
        "last_wave",
        stacked=False,
    )
    own_2, sent_2 = wave(
        rest_wave_kernel,
        ((0, 0, 768),),
        (scalars, text, *states),
        IMAGES - 2 * EARLY,
        [
            jax.ShapeDtypeStruct((IMAGES - 2 * EARLY, WIDTH), f32),
            jax.ShapeDtypeStruct((IMAGES - 2 * EARLY, WIDTH), bf16),
        ],
        {},
        "rest_wave",
        stacked=False,
    )
    got_1, got_2 = send(sent_1, other_core), send(sent_2, other_core)
    first = first_terms(*turns, own_1, got_1)
    mine, two, one, three = cut_terms(*turns, own_2, got_2, first)
    parts = [send(part, along_z_or_y(steps)) for part, steps in ((two, 2), (one, 1), (three, 3))]
    pieces = ring_sum(mine, *parts)
    pieces = lax.all_to_all(pieces, AXIS, 0, 0, axis_index_groups=LAST_GROUPS, tiled=True)
    return last_sum(pieces)


def solution(mesh):
    flat = Mesh(mesh.devices.reshape(-1), (AXIS,))
    rows = P(AXIS, None)
    return jax.shard_map(
        per_device,
        mesh=flat,
        in_specs=(rows, rows, P(), P(), P()),
        out_specs=rows,
        check_vma=False,
    )
```

```python
import jax
import jax.numpy as jnp
from jax import lax
from jax.experimental import pallas as pl
from jax.experimental.pallas import tpu as pltpu
from jax.sharding import Mesh, PartitionSpec as P

epsilon = 1e-06
bf16 = jnp.bfloat16
f32 = jnp.float32

AXIS = "d"
ROWS = 144
WIDTH = 1152
HALF = 4 * ROWS
IMAGES = 2 * HALF
TURNED = 512
EARLY = 384
SLAB = 1408
VMEM_LIMIT = 20 << 20
WORK = 12_000_000_000
PROJ = 20_000_000_000
W1 = 30_000_000_000
WAVES = {"first_wave": W1, "second_wave": 1000, "last_wave": 1000, "rest_wave": 1000}
HOLD = 1000
NORM = 1000
KEEP = 1000
MARK = jax.ShapeDtypeStruct((8, 128), f32)


def place(index):
    y, xl, z = index & 3, (index >> 2) & 1, (index >> 3) & 3
    core, xh = (index >> 5) & 1, (index >> 6) & 1
    return 2 * xh + xl, y, z, core


def index_of(x, y, z, core):
    return (x >> 1) * 64 + core * 32 + z * 8 + (x & 1) * 4 + y


def send(value, target):
    pairs = [(source, index_of(*target(*place(source)))) for source in range(128)]
    return lax.ppermute(value, AXIS, pairs)


def along_x(steps):
    return lambda x, y, z, core: ((x + steps) % 4, y, z, core)


def along_y_or_z(steps):
    return lambda x, y, z, core: (
        (x, y, (z + steps) % 4, core) if core else (x, (y + steps) % 4, z, core)
    )


def along_z_or_y(steps):
    return lambda x, y, z, core: (
        (x, (y + steps) % 4, z, core) if core else (x, y, (z + steps) % 4, core)
    )


def other_core(x, y, z, core):
    return (x, y, z, 1 - core)


LAST_GROUPS = [
    [index_of(2 * xh + xl, y, z, 0) for xh in range(2) for xl in range(2) for y in range(4)]
    for z in range(4)
] + [
    [index_of(2 * xh + xl, y, z, 1) for xh in range(2) for z in range(4) for xl in range(2)]
    for y in range(4)
]


def my_core():
    return (lax.axis_index(AXIS) >> 5) & 1


IN_VMEM = pl.BlockSpec(memory_space=pltpu.VMEM)
IN_SMEM = pl.BlockSpec(memory_space=pltpu.SMEM)


def params():
    return pltpu.CompilerParams(vmem_limit_bytes=VMEM_LIMIT)


def cost(flops, bytes_accessed):
    return pl.CostEstimate(flops=flops, bytes_accessed=bytes_accessed, transcendentals=0)


def begin(pairs, sems, first=0):
    copies = [
        pltpu.make_async_copy(source, target, sems.at[first + slot])
        for slot, (source, target) in enumerate(pairs)
    ]
    for copy in copies:
        copy.start()
    return copies


def finish(copies):
    for copy in copies:
        copy.wait()


def stack(cuts, refs, target):
    offset = 0
    for which, start, rows in cuts:
        target[offset : offset + rows, :] = refs[which][start : start + rows, :]
        offset += rows


def keep_kernel(text, held):
    held[...] = text[...]


def kept(text):
    return pl.pallas_call(
        keep_kernel,
        in_specs=[IN_VMEM],
        out_specs=IN_VMEM,
        out_shape=jax.ShapeDtypeStruct((ROWS, WIDTH), bf16),
        compiler_params=params(),
        cost_estimate=cost(KEEP, 0),
        name="hold_text",
    )(text)


def hold_kernel(features, log_scale, bias, after, features_held, scalars):
    features_held[...] = features[...]
    scalars[0:1, :] = jnp.full((1, 128), log_scale[0], f32)
    scalars[1:2, :] = jnp.full((1, 128), bias[0], f32)


def held(*arrays):
    return pl.pallas_call(
        hold_kernel,
        in_specs=[IN_VMEM] + [IN_SMEM] * 2 + [IN_VMEM],
        out_specs=[IN_VMEM] * 2,
        out_shape=[jax.ShapeDtypeStruct((ROWS, WIDTH), bf16), MARK],
        compiler_params=params(),
        cost_estimate=cost(HOLD, 0),
        name="hold",
    )(*arrays)


def normalize_kernel(upper, lower, *refs):
    unit = refs[-1]
    for slot, part in enumerate((upper, lower)):
        values = part[...].astype(f32)
        inverse = lax.rsqrt(jnp.sum(values * values, axis=1, keepdims=True) + epsilon)
        unit[ROWS * slot : ROWS * slot + ROWS, :] = (values * inverse).astype(bf16)


def normalized(*parts):
    return pl.pallas_call(
        normalize_kernel,
        in_specs=[IN_VMEM] * len(parts),
        out_specs=IN_VMEM,
        out_shape=jax.ShapeDtypeStruct((HALF // 2, WIDTH), bf16),
        compiler_params=params(),
        cost_estimate=cost(NORM, 0),
        name="normalize_texts",
    )(*parts)


def join_kernel(own, opposite, next_1, next_3, low, high, joined, low_later, high_later):
    for slot, part in enumerate((own, opposite, next_1, next_3)):
        joined[ROWS * slot : ROWS * slot + ROWS, :] = part[...]
    low_later[...] = low[...]
    high_later[...] = high[...]


def joined(*parts):
    return pl.pallas_call(
        join_kernel,
        in_specs=[IN_VMEM] * 6,
        out_specs=[IN_VMEM] * 3,
        out_shape=[jax.ShapeDtypeStruct((HALF, WIDTH), bf16)]
        + [jax.ShapeDtypeStruct((HALF // 2, WIDTH), bf16)] * 2,
        compiler_params=params(),
        cost_estimate=cost(WORK, 0),
        name="join",
    )(*parts)


def pass_kernel(low, high, after, low_on, high_on):
    low_on[...] = low[...]
    high_on[...] = high[...]


def passed(*parts):
    return pl.pallas_call(
        pass_kernel,
        in_specs=[IN_VMEM] * 3,
        out_specs=[IN_VMEM] * 2,
        out_shape=[jax.ShapeDtypeStruct((HALF // 2, WIDTH), bf16)] * 2,
        compiler_params=params(),
        name="pass_on",
    )(*parts)


def project_kernel(images, proj, unit, unit_f, inverse, turned, *marks):
    for mark in marks:
        mark[...] = jnp.zeros(mark.shape, f32)
    emb = jnp.dot(images[...], proj[...], preferred_element_type=f32)
    inv = lax.rsqrt(jnp.sum(emb * emb, axis=1, keepdims=True) + epsilon)
    emb = emb * inv
    unit_f[...] = emb
    inverse[...] = jnp.broadcast_to(inv, inverse.shape)
    unit[...] = emb.astype(bf16)
    turned[...] = images[...].T


def projected(images, proj_w, marks):
    return pl.pallas_call(
        project_kernel,
        in_specs=[IN_VMEM] * 2,
        out_specs=[IN_VMEM] * (4 + marks),
        out_shape=[
            jax.ShapeDtypeStruct((HALF, WIDTH), bf16),
            jax.ShapeDtypeStruct((HALF, WIDTH), f32),
            jax.ShapeDtypeStruct((HALF, 128), f32),
            jax.ShapeDtypeStruct((WIDTH, HALF), bf16),
        ]
        + [MARK] * marks,
        compiler_params=params(),
        cost_estimate=cost(PROJ, 0),
        name="project_images",
    )(images, proj_w)


def wave_body(blocks, text, scalars, sim, weights, diagonal, take):
    half = 0.5 * jnp.exp(scalars[0:1, 0:1])
    half_shift = 0.5 * scalars[1:2, 0:1]
    rows, offset = [], 0
    for unit, start, count in blocks:
        rows.append(slice(offset, offset + count))
        offset += count
    for which, (unit, start, count) in enumerate(blocks):
        sim[rows[which], :] = lax.dot_general(
            unit[start : start + count, :],
            text[...],
            (((1,), (1,)), ((), ())),
            preferred_element_type=f32,
        )
        weights[rows[which], :] = (
            half + half * jnp.tanh(half * sim[rows[which], :] + half_shift)
        ).astype(bf16)
        if diagonal and which == 0:
            tanh = jnp.tanh(half * sim[:ROWS, :256] + half_shift)
            row = lax.broadcasted_iota(jnp.int32, (ROWS, 256), 0)
            column = lax.broadcasted_iota(jnp.int32, (ROWS, 256), 1)
            pair = jnp.where(row == column, half * tanh - half, half + half * tanh)
            weights[:ROWS, :256] = pair.astype(bf16)
    for which in range(len(blocks)):
        take(which, jnp.dot(weights[rows[which], :], text[...], preferred_element_type=f32))


def first_wave_kernel(cuts, scalars, low, high, unit_a, unit_b, total_a, total_b, text, sim, weights):
    stack(cuts, (low, high), text)
    totals = (total_a, total_b)

    def take(which, product):
        totals[which][...] = product

    blocks = ((unit_a, 0, HALF), (unit_b, 0, HALF))
    wave_body(blocks, text, scalars, sim, weights, True, take)


def next_wave_kernel(cuts, scalars, *refs):
    count = len(refs) - 9
    texts, (unit_a, unit_b), before, totals = (
        refs[:count],
        refs[count : count + 2],
        refs[count + 2 : count + 4],
        refs[count + 4 : count + 6],
    )
    text, sim, weights = refs[count + 6 :]
    stack(cuts, texts, text)

    def take(which, product):
        totals[which][...] = before[which][...] + product

    blocks = ((unit_a, 0, HALF), (unit_b, 0, HALF))
    wave_body(blocks, text, scalars, sim, weights, False, take)


def project_gradient(start, count, scalars, text, states, projected_f, projected_b, sim, weights):
    units, totals, units_f, inverses = (states[2 * slot : 2 * slot + 2] for slot in range(4))
    rows = slice(start, start + count)

    def take(which, product):
        gradient = totals[which][rows, :] + product
        image = units_f[which][rows, :]
        along = jnp.sum(image * gradient, axis=1, keepdims=True)
        projection = (gradient - image * along) * inverses[which][rows, 0:1]
        out = slice(which * count, which * count + count)
        projected_f[out, :] = projection
        projected_b[out, :] = projection.astype(bf16)

    blocks = tuple((unit, start, count) for unit in units)
    wave_body(blocks, text, scalars, sim, weights, False, take)


def last_wave_kernel(cuts, scalars, *refs):
    count = len(refs) - 13
    projected_f, projected_b, text, sim, weights = refs[count + 8 :]
    stack(cuts, refs[:count], text)
    project_gradient(
        0, EARLY, scalars, text, refs[count : count + 8], projected_f, projected_b, sim, weights
    )


def rest_wave_kernel(cuts, scalars, text, *refs):
    project_gradient(EARLY, HALF - EARLY, scalars, text, refs[:8], *refs[8:])


def wave(kernel, cuts, operands, images, out_shape, aliases, name, stacked=True):
    rows = sum(cut[2] for cut in cuts)
    return pl.pallas_call(
        lambda *refs: kernel(cuts, *refs),
        in_specs=[IN_VMEM] * len(operands),
        out_specs=[IN_VMEM] * len(out_shape),
        out_shape=out_shape,
        input_output_aliases=aliases,
        scratch_shapes=[pltpu.VMEM((rows, WIDTH), bf16)] * stacked
        + [pltpu.VMEM((images, rows), f32), pltpu.VMEM((images, rows), bf16)],
        compiler_params=params(),
        cost_estimate=cost(WAVES[name], 0),
        name=name,
    )(*operands)


def chip_projection(projected_f, other, count):
    return [
        (projected_f[first : first + count, :] + other[count - first : 2 * count - first, :].astype(f32)).astype(bf16)
        for first in (0, count)
    ]


def my_rows(high):
    return pl.ds(pl.multiple_of(576 * high + 288 * my_core(), 16), 288)


def first_terms_kernel(turned_a, turned_b, projected_f, other, out):
    both = jnp.concatenate(chip_projection(projected_f, other, EARLY))
    for high in range(2):
        left = jnp.concatenate([turned[my_rows(high), :EARLY] for turned in (turned_a, turned_b)], axis=1)
        out[288 * high : 288 * high + 288, :] = jnp.dot(left, both, preferred_element_type=f32)


def first_terms(*parts):
    return pl.pallas_call(
        first_terms_kernel,
        in_specs=[IN_VMEM] * 4,
        out_specs=IN_VMEM,
        out_shape=jax.ShapeDtypeStruct((HALF, WIDTH), f32),
        compiler_params=params(),
        cost_estimate=cost(1000, 1000),
        name="first_terms",
    )(*parts)


def cut_terms_kernel(turned_a, turned_b, projected_f, other, first, mine, two, one, three, total):
    both_a, both_b = chip_projection(projected_f, other, HALF - EARLY)
    for high in range(2):
        rows = slice(288 * high, 288 * high + 288)
        term = first[rows, :]
        for turned, both in ((turned_a, both_a), (turned_b, both_b)):
            term = term + jnp.dot(turned[my_rows(high), EARLY:], both, preferred_element_type=f32)
        for tile in range(9):
            total[tile, rows, :] = term[:, 128 * tile : 128 * tile + 128]
    index = lax.axis_index(AXIS)
    outs = ((0, mine), (2, two), (1, one), (3, three))

    @pl.when(my_core() == 0)
    def _():
        for steps, out in outs:
            first = 72 * (((index >> 3) + steps) & 3)
            for tile in range(9):
                for row in range(9):
                    parts = [
                        total[tile, pl.ds(288 * high + first + row, 8, stride=9), :]
                        for high in range(2)
                    ]
                    out[16 * row : 16 * row + 16, 128 * tile : 128 * tile + 128] = (
                        jnp.concatenate(parts).astype(out.dtype)
                    )

    @pl.when(my_core() == 1)
    def _():
        for steps, out in outs:
            first = 9 * ((index + steps) & 3)
            for tile in range(9):
                for row in range(9):
                    part = total[tile, pl.ds(first + row, 16, stride=36), :]
                    out[16 * row : 16 * row + 16, 128 * tile : 128 * tile + 128] = part.astype(
                        out.dtype
                    )


def cut_terms(*parts):
    return pl.pallas_call(
        cut_terms_kernel,
        in_specs=[IN_VMEM] * 5,
        out_specs=[IN_VMEM] * 4,
        out_shape=[jax.ShapeDtypeStruct((ROWS, WIDTH), f32)]
        + [jax.ShapeDtypeStruct((ROWS, WIDTH), bf16)] * 3,
        scratch_shapes=[pltpu.VMEM((9, HALF, 128), f32)],
        compiler_params=params(),
        name="cut_terms",
    )(*parts)


def ring_sum_kernel(mine, two, one, three, out, eights, ninth):
    ninth[...] = jnp.zeros(ninth.shape, f32)
    for tile in range(9):
        lanes = slice(128 * tile, 128 * tile + 128)
        value = mine[:, lanes]
        for part in (two, one, three):
            value = value + part[:, lanes].astype(f32)
        for row in range(8):
            eights[tile, pl.ds(row, 16, stride=8), :] = value[16 * row : 16 * row + 16]
        ninth[tile // 8, pl.ds(tile % 8, 16, stride=8), :] = value[128:]
        out[:, lanes] = eights[tile].astype(bf16)
    out[:, WIDTH : WIDTH + 128] = ninth[0].astype(bf16)
    out[:, WIDTH + 128 :] = ninth[1].astype(bf16)


def ring_sum(*parts):
    return pl.pallas_call(
        ring_sum_kernel,
        out_shape=jax.ShapeDtypeStruct((128, SLAB), bf16),
        scratch_shapes=[pltpu.VMEM((9, 128, 128), f32), pltpu.VMEM((2, 128, 128), f32)],
        compiler_params=params(),
        name="ring_sum",
    )(*parts)


def last_sum_kernel(pieces, out):
    total = jnp.zeros((16, SLAB), f32)
    for step in range(8):
        total = total + pieces[16 * step : 16 * step + 16, :].astype(f32)
    total = total[:8] + total[8:]
    out[:8, :] = total[:, :WIDTH]
    for tile in range(9):
        sublane, lane = tile % 8, WIDTH + 128 * (tile // 8)
        out[8:9, 128 * tile : 128 * tile + 128] = total[sublane : sublane + 1, lane : lane + 128]


def last_sum(pieces):
    return pl.pallas_call(
        last_sum_kernel,
        out_shape=jax.ShapeDtypeStruct((9, WIDTH), f32),
        compiler_params=params(),
        name="last_sum",
    )(pieces)


def ring(value, axis):
    return [send(value, axis(steps)) for steps in (2, 1, 3)]


def per_device(features, text_emb, proj_w, log_scale, bias):
    image_ring = ring(features, along_x)
    next_1, opposite, next_3 = (send(text_emb, along_y_or_z(steps)) for steps in (1, 2, 3))
    low = normalized(kept(text_emb), next_1, image_ring[0])
    high = normalized(opposite, next_3)
    images, scalars = held(features, log_scale, bias, high)
    here, low_later, high_later = joined(images, *image_ring, low, high)
    there = send(here, other_core)
    low_1, high_3 = send(low, along_z_or_y(1)), send(high, along_z_or_y(3))
    high_1, low_3 = send(high_later, along_z_or_y(1)), send(low_later, along_z_or_y(3))
    *there, mark = projected(there, proj_w, 1)
    units, units_f, inverses, turns = zip(projected(here, proj_w, 0), there)
    low_on, high_on = passed(low_1, high_3, mark)
    low_2, high_2 = send(low_on, along_z_or_y(1)), send(high_on, along_z_or_y(3))

    sums = [jax.ShapeDtypeStruct((HALF, WIDTH), f32)] * 2
    totals = wave(
        first_wave_kernel,
        ((0, 0, 288), (1, 0, 224)),
        (scalars, low, high, *units),
        IMAGES,
        sums,
        {},
        "first_wave",
    )
    totals = wave(
        next_wave_kernel,
        ((0, 224, 64), (1, 0, 288), (2, 0, 288), (3, 0, 288), (4, 0, 96)),
        (scalars, high, low_1, high_3, high_1, low_3, *units, *totals),
        IMAGES,
        sums,
        {8: 0, 9: 1},
        "second_wave",
    )
    states = (*units, *totals, *units_f, *inverses)
    texts = jax.ShapeDtypeStruct((768, WIDTH), bf16)
    own_1, sent_1, text = wave(
        last_wave_kernel,
        ((0, 96, 192), (1, 0, 288), (2, 0, 288)),
        (scalars, low_3, low_2, high_2, *states),
        2 * EARLY,
        [
            jax.ShapeDtypeStruct((2 * EARLY, WIDTH), f32),
            jax.ShapeDtypeStruct((2 * EARLY, WIDTH), bf16),
            texts,
        ],
        {},
        "last_wave",
        stacked=False,
    )
    own_2, sent_2 = wave(
        rest_wave_kernel,
        ((0, 0, 768),),
        (scalars, text, *states),
        IMAGES - 2 * EARLY,
        [
            jax.ShapeDtypeStruct((IMAGES - 2 * EARLY, WIDTH), f32),
            jax.ShapeDtypeStruct((IMAGES - 2 * EARLY, WIDTH), bf16),
        ],
        {},
        "rest_wave",
        stacked=False,
    )
    got_1, got_2 = send(sent_1, other_core), send(sent_2, other_core)
    first = first_terms(*turns, own_1, got_1)
    mine, two, one, three = cut_terms(*turns, own_2, got_2, first)
    parts = [send(part, along_z_or_y(steps)) for part, steps in ((two, 2), (one, 1), (three, 3))]
    pieces = ring_sum(mine, *parts)
    pieces = lax.all_to_all(pieces, AXIS, 0, 0, axis_index_groups=LAST_GROUPS, tiled=True)
    return last_sum(pieces)


def solution(mesh):
    flat = Mesh(mesh.devices.reshape(-1), (AXIS,))
    rows = P(AXIS, None)
    return jax.shard_map(
        per_device,
        mesh=flat,
        in_specs=(rows, rows, P(), P(), P()),
        out_specs=rows,
        check_vma=False,
    )
```

```python
import jax
import jax.numpy as jnp
from jax import lax
from jax.experimental import pallas as pl
from jax.experimental.pallas import tpu as pltpu
from jax.sharding import Mesh, PartitionSpec as P

epsilon = 1e-06
bf16 = jnp.bfloat16
f32 = jnp.float32

AXIS = "d"
ROWS = 144
WIDTH = 1152
HALF = 4 * ROWS
IMAGES = 2 * HALF
EARLY = 384
SLAB = 1408
VMEM_LIMIT = 20 << 20
WORK = 12_000_000_000
PROJ = 20_000_000_000
W1 = 30_000_000_000
WAVES = {"first_wave": W1, "second_wave": 1000, "last_wave": 1000, "rest_wave": 1000}
HOLD = 12_000_000_000
NORM = 1000
KEEP = 1000
MARK = jax.ShapeDtypeStruct((8, 128), f32)


def place(index):
    y, xl, z = index & 3, (index >> 2) & 1, (index >> 3) & 3
    core, xh = (index >> 5) & 1, (index >> 6) & 1
    return 2 * xh + xl, y, z, core


def index_of(x, y, z, core):
    return (x >> 1) * 64 + core * 32 + z * 8 + (x & 1) * 4 + y


def send(value, target):
    pairs = [(source, index_of(*target(*place(source)))) for source in range(128)]
    return lax.ppermute(value, AXIS, pairs)


def along_x(steps):
    return lambda x, y, z, core: ((x + steps) % 4, y, z, core)


def along_y_or_z(steps):
    return lambda x, y, z, core: (
        (x, y, (z + steps) % 4, core) if core else (x, (y + steps) % 4, z, core)
    )


def along_z_or_y(steps):
    return lambda x, y, z, core: (
        (x, (y + steps) % 4, z, core) if core else (x, y, (z + steps) % 4, core)
    )


def other_core(x, y, z, core):
    return (x, y, z, 1 - core)


LAST_GROUPS = [
    [index_of(2 * xh + xl, y, z, 0) for xh in range(2) for xl in range(2) for y in range(4)]
    for z in range(4)
] + [
    [index_of(2 * xh + xl, y, z, 1) for xh in range(2) for z in range(4) for xl in range(2)]
    for y in range(4)
]


def my_core():
    return (lax.axis_index(AXIS) >> 5) & 1


IN_VMEM = pl.BlockSpec(memory_space=pltpu.VMEM)
IN_SMEM = pl.BlockSpec(memory_space=pltpu.SMEM)


def params():
    return pltpu.CompilerParams(vmem_limit_bytes=VMEM_LIMIT)


def cost(flops, bytes_accessed):
    return pl.CostEstimate(flops=flops, bytes_accessed=bytes_accessed, transcendentals=0)


def stack(cuts, refs, target):
    offset = 0
    for which, start, rows in cuts:
        target[offset : offset + rows, :] = refs[which][start : start + rows, :]
        offset += rows


def keep_kernel(text, held):
    held[...] = text[...]


def kept(text):
    return pl.pallas_call(
        keep_kernel,
        in_specs=[IN_VMEM],
        out_specs=IN_VMEM,
        out_shape=jax.ShapeDtypeStruct((ROWS, WIDTH), bf16),
        compiler_params=params(),
        cost_estimate=cost(KEEP, 0),
        name="hold_text",
    )(text)


def hold_kernel(features, log_scale, bias, after, features_held, scalars):
    features_held[...] = features[...]
    scalars[0:1, :] = jnp.full((1, 128), log_scale[0], f32)
    scalars[1:2, :] = jnp.full((1, 128), bias[0], f32)


def held(*arrays):
    return pl.pallas_call(
        hold_kernel,
        in_specs=[IN_VMEM] + [IN_SMEM] * 2 + [IN_VMEM],
        out_specs=[IN_VMEM] * 2,
        out_shape=[jax.ShapeDtypeStruct((ROWS, WIDTH), bf16), MARK],
        compiler_params=params(),
        cost_estimate=cost(HOLD, 0),
        name="hold",
    )(*arrays)


def normalize_kernel(upper, lower, *refs):
    unit = refs[-1]
    for slot, part in enumerate((upper, lower)):
        values = part[...].astype(f32)
        inverse = lax.rsqrt(jnp.sum(values * values, axis=1, keepdims=True) + epsilon)
        unit[ROWS * slot : ROWS * slot + ROWS, :] = (values * inverse).astype(bf16)


def normalized(*parts):
    return pl.pallas_call(
        normalize_kernel,
        in_specs=[IN_VMEM] * len(parts),
        out_specs=IN_VMEM,
        out_shape=jax.ShapeDtypeStruct((HALF // 2, WIDTH), bf16),
        compiler_params=params(),
        cost_estimate=cost(NORM, 0),
        name="normalize_texts",
    )(*parts)


def join_kernel(own, opposite, next_1, next_3, low, high, joined, low_later, high_later):
    for slot, part in enumerate((own, opposite, next_1, next_3)):
        joined[ROWS * slot : ROWS * slot + ROWS, :] = part[...]
    low_later[...] = low[...]
    high_later[...] = high[...]


def joined(*parts):
    return pl.pallas_call(
        join_kernel,
        in_specs=[IN_VMEM] * 6,
        out_specs=[IN_VMEM] * 3,
        out_shape=[jax.ShapeDtypeStruct((HALF, WIDTH), bf16)]
        + [jax.ShapeDtypeStruct((HALF // 2, WIDTH), bf16)] * 2,
        compiler_params=params(),
        cost_estimate=cost(WORK, 0),
        name="join",
    )(*parts)


def pass_kernel(low, high, after, low_on, high_on):
    low_on[...] = low[...]
    high_on[...] = high[...]


def passed(*parts):
    return pl.pallas_call(
        pass_kernel,
        in_specs=[IN_VMEM] * 3,
        out_specs=[IN_VMEM] * 2,
        out_shape=[jax.ShapeDtypeStruct((HALF // 2, WIDTH), bf16)] * 2,
        compiler_params=params(),
        name="pass_on",
    )(*parts)


def project_kernel(images, proj, unit, unit_f, inverse, turned, *marks):
    for mark in marks:
        mark[...] = jnp.zeros(mark.shape, f32)
    emb = jnp.dot(images[...], proj[...], preferred_element_type=f32)
    inv = lax.rsqrt(jnp.sum(emb * emb, axis=1, keepdims=True) + epsilon)
    emb = emb * inv
    unit_f[...] = emb
    inverse[...] = jnp.broadcast_to(inv, inverse.shape)
    unit[...] = emb.astype(bf16)
    turned[...] = images[...].T


def projected(images, proj_w, marks):
    return pl.pallas_call(
        project_kernel,
        in_specs=[IN_VMEM] * 2,
        out_specs=[IN_VMEM] * (4 + marks),
        out_shape=[
            jax.ShapeDtypeStruct((HALF, WIDTH), bf16),
            jax.ShapeDtypeStruct((HALF, WIDTH), f32),
            jax.ShapeDtypeStruct((HALF, 128), f32),
            jax.ShapeDtypeStruct((WIDTH, HALF), bf16),
        ]
        + [MARK] * marks,
        compiler_params=params(),
        cost_estimate=cost(PROJ, 0),
        name="project_images",
    )(images, proj_w)


def wave_body(blocks, text, scalars, sim, weights, diagonal, take):
    half = 0.5 * jnp.exp(scalars[0:1, 0:1])
    half_shift = 0.5 * scalars[1:2, 0:1]
    rows, offset = [], 0
    for unit, start, count in blocks:
        rows.append(slice(offset, offset + count))
        offset += count
    for which, (unit, start, count) in enumerate(blocks):
        sim[rows[which], :] = lax.dot_general(
            unit[start : start + count, :],
            text[...],
            (((1,), (1,)), ((), ())),
            preferred_element_type=f32,
        )
        weights[rows[which], :] = (
            half + half * jnp.tanh(half * sim[rows[which], :] + half_shift)
        ).astype(bf16)
        if diagonal and which == 0:
            tanh = jnp.tanh(half * sim[:ROWS, :256] + half_shift)
            row = lax.broadcasted_iota(jnp.int32, (ROWS, 256), 0)
            column = lax.broadcasted_iota(jnp.int32, (ROWS, 256), 1)
            pair = jnp.where(row == column, half * tanh - half, half + half * tanh)
            weights[:ROWS, :256] = pair.astype(bf16)
    for which in range(len(blocks)):
        take(which, jnp.dot(weights[rows[which], :], text[...], preferred_element_type=f32))


def first_wave_kernel(cuts, scalars, low, high, unit_a, unit_b, total_a, total_b, text, sim, weights):
    stack(cuts, (low, high), text)
    totals = (total_a, total_b)

    def take(which, product):
        totals[which][...] = product

    blocks = ((unit_a, 0, HALF), (unit_b, 0, HALF))
    wave_body(blocks, text, scalars, sim, weights, True, take)


def next_wave_kernel(cuts, scalars, *refs):
    count = len(refs) - 9
    texts, (unit_a, unit_b), before, totals = (
        refs[:count],
        refs[count : count + 2],
        refs[count + 2 : count + 4],
        refs[count + 4 : count + 6],
    )
    text, sim, weights = refs[count + 6 :]
    stack(cuts, texts, text)

    def take(which, product):
        totals[which][...] = before[which][...] + product

    blocks = ((unit_a, 0, HALF), (unit_b, 0, HALF))
    wave_body(blocks, text, scalars, sim, weights, False, take)


def project_gradient(start, count, scalars, text, states, projected_f, projected_b, sim, weights):
    units, totals, units_f, inverses = (states[2 * slot : 2 * slot + 2] for slot in range(4))
    rows = slice(start, start + count)

    def take(which, product):
        gradient = totals[which][rows, :] + product
        image = units_f[which][rows, :]
        along = jnp.sum(image * gradient, axis=1, keepdims=True)
        projection = (gradient - image * along) * inverses[which][rows, 0:1]
        out = slice(which * count, which * count + count)
        projected_f[out, :] = projection
        projected_b[out, :] = projection.astype(bf16)

    blocks = tuple((unit, start, count) for unit in units)
    wave_body(blocks, text, scalars, sim, weights, False, take)


def last_wave_kernel(cuts, scalars, *refs):
    count = len(refs) - 13
    projected_f, projected_b, text, sim, weights = refs[count + 8 :]
    stack(cuts, refs[:count], text)
    project_gradient(
        0, EARLY, scalars, text, refs[count : count + 8], projected_f, projected_b, sim, weights
    )


def rest_wave_kernel(cuts, scalars, text, *refs):
    project_gradient(EARLY, HALF - EARLY, scalars, text, refs[:8], *refs[8:])


def wave(kernel, cuts, operands, images, out_shape, aliases, name, stacked=True):
    rows = sum(cut[2] for cut in cuts)
    return pl.pallas_call(
        lambda *refs: kernel(cuts, *refs),
        in_specs=[IN_VMEM] * len(operands),
        out_specs=[IN_VMEM] * len(out_shape),
        out_shape=out_shape,
        input_output_aliases=aliases,
        scratch_shapes=[pltpu.VMEM((rows, WIDTH), bf16)] * stacked
        + [pltpu.VMEM((images, rows), f32), pltpu.VMEM((images, rows), bf16)],
        compiler_params=params(),
        cost_estimate=cost(WAVES[name], 0),
        name=name,
    )(*operands)


def chip_projection(projected_f, other, count):
    return [
        (projected_f[first : first + count, :] + other[count - first : 2 * count - first, :].astype(f32)).astype(bf16)
        for first in (0, count)
    ]


def my_rows(high):
    return pl.ds(pl.multiple_of(576 * high + 288 * my_core(), 16), 288)


def first_terms_kernel(turned_a, turned_b, projected_f, other, out):
    both = jnp.concatenate(chip_projection(projected_f, other, EARLY))
    for high in range(2):
        left = jnp.concatenate([turned[my_rows(high), :EARLY] for turned in (turned_a, turned_b)], axis=1)
        out[288 * high : 288 * high + 288, :] = jnp.dot(left, both, preferred_element_type=f32)


def first_terms(*parts):
    return pl.pallas_call(
        first_terms_kernel,
        in_specs=[IN_VMEM] * 4,
        out_specs=IN_VMEM,
        out_shape=jax.ShapeDtypeStruct((HALF, WIDTH), f32),
        compiler_params=params(),
        cost_estimate=cost(1000, 1000),
        name="first_terms",
    )(*parts)


def cut_terms_kernel(turned_a, turned_b, projected_f, other, first, mine, two, one, three, total):
    both_a, both_b = chip_projection(projected_f, other, HALF - EARLY)
    for high in range(2):
        rows = slice(288 * high, 288 * high + 288)
        term = first[rows, :]
        for turned, both in ((turned_a, both_a), (turned_b, both_b)):
            term = term + jnp.dot(turned[my_rows(high), EARLY:], both, preferred_element_type=f32)
        for tile in range(9):
            total[tile, rows, :] = term[:, 128 * tile : 128 * tile + 128]
    index = lax.axis_index(AXIS)
    outs = ((0, mine), (2, two), (1, one), (3, three))

    @pl.when(my_core() == 0)
    def _():
        for steps, out in outs:
            first = 72 * (((index >> 3) + steps) & 3)
            for tile in range(9):
                for row in range(9):
                    parts = [
                        total[tile, pl.ds(288 * high + first + row, 8, stride=9), :]
                        for high in range(2)
                    ]
                    out[16 * row : 16 * row + 16, 128 * tile : 128 * tile + 128] = (
                        jnp.concatenate(parts).astype(out.dtype)
                    )

    @pl.when(my_core() == 1)
    def _():
        for steps, out in outs:
            first = 9 * ((index + steps) & 3)
            for tile in range(9):
                for row in range(9):
                    part = total[tile, pl.ds(first + row, 16, stride=36), :]
                    out[16 * row : 16 * row + 16, 128 * tile : 128 * tile + 128] = part.astype(
                        out.dtype
                    )


def cut_terms(*parts):
    return pl.pallas_call(
        cut_terms_kernel,
        in_specs=[IN_VMEM] * 5,
        out_specs=[IN_VMEM] * 4,
        out_shape=[jax.ShapeDtypeStruct((ROWS, WIDTH), f32)]
        + [jax.ShapeDtypeStruct((ROWS, WIDTH), bf16)] * 3,
        scratch_shapes=[pltpu.VMEM((9, HALF, 128), f32)],
        compiler_params=params(),
        name="cut_terms",
    )(*parts)


def ring_sum_kernel(mine, two, one, three, out, eights, ninth):
    ninth[...] = jnp.zeros(ninth.shape, f32)
    for tile in range(9):
        lanes = slice(128 * tile, 128 * tile + 128)
        value = mine[:, lanes]
        for part in (two, one, three):
            value = value + part[:, lanes].astype(f32)
        for row in range(8):
            eights[tile, pl.ds(row, 16, stride=8), :] = value[16 * row : 16 * row + 16]
        ninth[tile // 8, pl.ds(tile % 8, 16, stride=8), :] = value[128:]
        out[:, lanes] = eights[tile].astype(bf16)
    out[:, WIDTH : WIDTH + 128] = ninth[0].astype(bf16)
    out[:, WIDTH + 128 :] = ninth[1].astype(bf16)


def ring_sum(*parts):
    return pl.pallas_call(
        ring_sum_kernel,
        out_shape=jax.ShapeDtypeStruct((128, SLAB), bf16),
        scratch_shapes=[pltpu.VMEM((9, 128, 128), f32), pltpu.VMEM((2, 128, 128), f32)],
        compiler_params=params(),
        name="ring_sum",
    )(*parts)


def last_sum_kernel(pieces, out):
    total = jnp.zeros((16, SLAB), f32)
    for step in range(8):
        total = total + pieces[16 * step : 16 * step + 16, :].astype(f32)
    total = total[:8] + total[8:]
    out[:8, :] = total[:, :WIDTH]
    for tile in range(9):
        sublane, lane = tile % 8, WIDTH + 128 * (tile // 8)
        out[8:9, 128 * tile : 128 * tile + 128] = total[sublane : sublane + 1, lane : lane + 128]


def last_sum(pieces):
    return pl.pallas_call(
        last_sum_kernel,
        out_shape=jax.ShapeDtypeStruct((9, WIDTH), f32),
        compiler_params=params(),
        name="last_sum",
    )(pieces)


def ring(value, axis):
    return [send(value, axis(steps)) for steps in (2, 1, 3)]


def per_device(features, text_emb, proj_w, log_scale, bias):
    image_ring = ring(features, along_x)
    next_1, opposite, next_3 = (send(text_emb, along_y_or_z(steps)) for steps in (1, 2, 3))
    low = normalized(kept(text_emb), next_1, image_ring[0])
    high = normalized(opposite, next_3)
    images, scalars = held(features, log_scale, bias, high)
    here, low_later, high_later = joined(images, *image_ring, low, high)
    there = send(here, other_core)
    low_1, high_3 = send(low, along_z_or_y(1)), send(high, along_z_or_y(3))
    high_1, low_3 = send(high_later, along_z_or_y(1)), send(low_later, along_z_or_y(3))
    *there, mark = projected(there, proj_w, 1)
    units, units_f, inverses, turns = zip(projected(here, proj_w, 0), there)
    low_on, high_on = passed(low_1, high_3, mark)
    low_2, high_2 = send(low_on, along_z_or_y(1)), send(high_on, along_z_or_y(3))

    sums = [jax.ShapeDtypeStruct((HALF, WIDTH), f32)] * 2
    totals = wave(
        first_wave_kernel,
        ((0, 0, 288), (1, 0, 224)),
        (scalars, low, high, *units),
        IMAGES,
        sums,
        {},
        "first_wave",
    )
    totals = wave(
        next_wave_kernel,
        ((0, 224, 64), (1, 0, 288), (2, 0, 288), (3, 0, 288), (4, 0, 96)),
        (scalars, high, low_1, high_3, high_1, low_3, *units, *totals),
        IMAGES,
        sums,
        {8: 0, 9: 1},
        "second_wave",
    )
    states = (*units, *totals, *units_f, *inverses)
    texts = jax.ShapeDtypeStruct((768, WIDTH), bf16)
    own_1, sent_1, text = wave(
        last_wave_kernel,
        ((0, 96, 192), (1, 0, 288), (2, 0, 288)),
        (scalars, low_3, low_2, high_2, *states),
        2 * EARLY,
        [
            jax.ShapeDtypeStruct((2 * EARLY, WIDTH), f32),
            jax.ShapeDtypeStruct((2 * EARLY, WIDTH), bf16),
            texts,
        ],
        {},
        "last_wave",
        stacked=False,
    )
    own_2, sent_2 = wave(
        rest_wave_kernel,
        ((0, 0, 768),),
        (scalars, text, *states),
        IMAGES - 2 * EARLY,
        [
            jax.ShapeDtypeStruct((IMAGES - 2 * EARLY, WIDTH), f32),
            jax.ShapeDtypeStruct((IMAGES - 2 * EARLY, WIDTH), bf16),
        ],
        {},
        "rest_wave",
        stacked=False,
    )
    got_1, got_2 = send(sent_1, other_core), send(sent_2, other_core)
    first = first_terms(*turns, own_1, got_1)
    mine, two, one, three = cut_terms(*turns, own_2, got_2, first)
    parts = [send(part, along_z_or_y(steps)) for part, steps in ((two, 2), (one, 1), (three, 3))]
    pieces = ring_sum(mine, *parts)
    pieces = lax.all_to_all(pieces, AXIS, 0, 0, axis_index_groups=LAST_GROUPS, tiled=True)
    return last_sum(pieces)


def solution(mesh):
    flat = Mesh(mesh.devices.reshape(-1), (AXIS,))
    rows = P(AXIS, None)
    return jax.shard_map(
        per_device,
        mesh=flat,
        in_specs=(rows, rows, P(), P(), P()),
        out_specs=rows,
        check_vma=False,
    )
```
